32 devices in a mesh: track: 4 (over y, x), lateral: 4 (over z), depth: 2 (over core).
Axes of the slice: x: 2, y: 2, z: 4, core: 2. Of those that a mesh axis runs over, the one named last changes fastest.
Arguments:
- rhs: float32 [32, 8, 2, 64, 256], P('track', 'lateral', None, None, 'depth'), may hold values from -6 to 6
- start: float32 [32, 8, 2, 64, 256], P('track', 'lateral', None, None, 'depth'), may hold values from -6 to 6
- fine_blocks: bfloat16 [32, 8, 2, 27, 4096], P('track', 'lateral'), may hold values from -0.15625 to 0.15625
- fine_cols: int32 [32, 8, 2, 27], P('track', 'lateral'), may hold values from 0 to 26, each once within a row
- fine_mass: bfloat16 [32, 8, 2, 64], P('track', 'lateral'), may hold values from 4 to 8
- fine_smoother: bfloat16 [32, 8, 2, 4096], P('track', 'lateral'), may hold values from -0.05 to 0.25
- transfer: bfloat16 [32, 8, 2, 4096], P('track', 'lateral'), may hold values from -0.75 to 0.75
- aggregate: int32 [32, 8, 2], P('track', 'lateral'), may hold values from 0 to 31, as said below
- coarse_blocks: bfloat16 [32, 4, 2, 27, 4096], P(('track', 'lateral'), None, 'depth'), may hold values from -0.15625 to 0.15625
- coarse_cols: int32 [32, 4, 2, 27], P(('track', 'lateral'), None, 'depth'), may hold values from 0 to 26, each once within a row
- coarse_mass: bfloat16 [32, 4, 2, 64], P(('track', 'lateral'), None, 'depth'), may hold values from 1.5 to 3
- coarse_smoother: bfloat16 [32, 4, 2, 4096], P(('track', 'lateral'), None, 'depth'), may hold values from -0.2 to 1
Outputs:
- solution: float32 [32, 8, 2, 64, 256], P('track', 'lateral', None, None, 'depth')
The draws below stay inside these ranges and needn't reach their ends.
Inputs may be any that keep to these rules, and one draw needn't show every extreme that they name: `fine_cols`: each row lists every neighbour code once. `coarse_cols`: each row lists every neighbour code once. `aggregate`: for every y and z, the entries at x = 8 * q to 8 * q + 7 are a permutation of those same x.
All inputs are finite; a program needn't handle non-finite values.
Results may differ from the reference program's by a relative error of at most 0.01.
The reference program's roundings to bfloat16 on the way (of `correction`) count: a program that leaves them out, or rounds other values in their place, can miss the bound.
Values may be sent and summed in bfloat16 or wider, within the bound.
No kernel may reach another device: no remote copies, remote signals or barrier semaphores. Data moves between devices by JAX's collectives and lax.ppermute only.
A program may use at most 128 MiB of HBM per device.

```python
import math
import jax
import jax.numpy as jnp
from jax import lax

B = 64
FX = 8
NZ = 2
SWEEPS = 2
NX = 32
NY = 8
CY = 4
LOADS = 256


def smoother_values(key, shape, width, centre_lo, centre_hi, spread):
    first_key, second_key = jax.random.split(key)
    centre = jax.random.uniform(first_key, shape, jnp.float32, centre_lo, centre_hi)
    noise = spread * jax.random.normal(second_key, shape, jnp.float32)
    noise = jnp.clip(noise, -4.0 * spread, 4.0 * spread)
    position = jnp.arange(width * width, dtype=jnp.int32)
    on_diagonal = position // width == position % width
    return jnp.where(on_diagonal, centre, noise)


def draw_fine_smoother(key, part):
    return smoother_values(key, (NX, NY, NZ, B * B), B, 0.12, 0.2, 0.005).astype(jnp.bfloat16)


def draw_coarse_smoother(key, part):
    return smoother_values(key, (NX, NY // 2, NZ, B * B), B, 0.3, 0.5, 0.015).astype(jnp.bfloat16)


def draw_aggregate(key, part):
    blocks_x = NX // FX
    scores = jax.random.randint(key, (blocks_x, FX, NY, NZ), 0, 1 << 20, dtype=jnp.int32)
    scores = scores * FX + jnp.arange(FX, dtype=jnp.int32)[None, :, None, None]
    ranking = jnp.argsort(scores, axis=1, stable=True).astype(jnp.int32)
    starts = (jnp.arange(blocks_x, dtype=jnp.int32) * FX)[:, None, None, None]
    return (ranking + starts).reshape(NX, NY, NZ).astype(jnp.int32)


def steps_of(own_key, dims, shards, least, largest):
    level, own = 1.0, jax.random.fold_in(own_key, 6)
    for dim, blocks in shards:
        steps = jnp.exp(jax.random.uniform(jax.random.fold_in(own, dim), (blocks,), jnp.float32, least / len(shards), largest / len(shards)))
        level = level * jnp.repeat(steps, dims[dim] // blocks).reshape([-1 if axis == dim else 1 for axis in range(len(dims))])
    return level


def scatter_about(stream_key, shape, deviation, most, shards=(), kind=jnp.bfloat16):
    drawn = jax.random.normal(stream_key, shape, jnp.float32) * deviation
    if len(shards) > 0:
        drawn = steps_of(stream_key, shape, shards, -0.22, 0.18) * drawn
    return jnp.clip(drawn, min=-most, max=most).astype(kind)


def setup_inputs(seed: int = 0) -> dict:
    splits = jax.random.split(jax.random.key(seed), 13)
    return {
        "rhs": scatter_about(splits[0], (NX, NY, NZ, B, LOADS), 1.0, 6.0, ((0, 4), (1, 4), (4, 2)), jnp.float32),
        "start": scatter_about(splits[1], (NX, NY, NZ, B, LOADS), 1.0, 6.0, ((0, 4), (1, 4), (4, 2)), jnp.float32),
        "fine_blocks": scatter_about(splits[2], (NX, NY, NZ, 27, B * B), (27 * B) ** -0.5, 0.15625, ((0, 4), (1, 4))),
        "fine_cols": jax.vmap(lambda own: jax.random.permutation(own, 27))(jax.random.split(splits[3], NX * NY * NZ)).reshape((NX, NY, NZ, 27)).astype(jnp.int32),
        "fine_mass": jnp.clip(jnp.exp(math.log(8.0) - 0.6931472 * jax.random.uniform(splits[4], (NX, NY, NZ, B), jnp.float32) ** steps_of(splits[4], (NX, NY, NZ, B), ((0, 4), (1, 4)), -0.2, 0.2)), 4.0, 8.0).astype(jnp.bfloat16),
        "fine_smoother": draw_fine_smoother(jax.random.fold_in(splits[12], 71), 0),
        "transfer": scatter_about(splits[6], (NX, NY, NZ, B * B), B ** -0.5, 0.75, ((0, 4), (1, 4))),
        "aggregate": draw_aggregate(jax.random.fold_in(splits[12], 71), 0),
        "coarse_blocks": scatter_about(splits[8], (NX, CY, NZ, 27, B * B), (27 * B) ** -0.5, 0.15625, ((0, 16), (2, 2))),
        "coarse_cols": jax.vmap(lambda own: jax.random.permutation(own, 27))(jax.random.split(splits[9], NX * CY * NZ)).reshape((NX, CY, NZ, 27)).astype(jnp.int32),
        "coarse_mass": jnp.clip(jnp.exp(math.log(3.0) - 0.6931472 * jax.random.uniform(splits[10], (NX, CY, NZ, B), jnp.float32) ** steps_of(splits[10], (NX, CY, NZ, B), ((0, 16), (2, 2)), -0.2, 0.2)), 1.5, 3.0).astype(jnp.bfloat16),
        "coarse_smoother": draw_coarse_smoother(jax.random.fold_in(splits[12], 71), 0),
    }


damping = 0.8


def offset_slots(lists):
    codes = jnp.arange(27, dtype=jnp.int32)
    match = lists[..., :, None] == codes
    return jnp.sum(jnp.where(match, codes[:, None], 0), axis=-2).astype(jnp.int32)


def sort_blocks(blocks, lists, width):
    slots = offset_slots(lists)
    taken = jnp.take_along_axis(blocks, slots[..., None], axis=3)
    return taken.reshape(blocks.shape[:3] + (27, width, width))


def round_keep(values):
    return lax.optimization_barrier(values.astype(jnp.bfloat16))


def apply_operator(sorted_ops, mass, rounded):
    size_x, size_y, size_z = rounded.shape[:3]
    padded = jnp.pad(rounded, ((1, 1), (1, 1), (1, 1), (0, 0), (0, 0)))
    total = mass.astype(jnp.float32)[..., None] * rounded.astype(jnp.float32)
    for offset in range(27):
        along_x = offset // 9
        along_y = (offset // 3) % 3
        along_z = offset % 3
        piece = padded[along_x:along_x + size_x, along_y:along_y + size_y, along_z:along_z + size_z]
        total = total + jnp.einsum("xyzij,xyzjk->xyzik", sorted_ops[:, :, :, offset].astype(jnp.float32),
                                   piece.astype(jnp.float32), precision=lax.Precision.HIGHEST)
    return total


def smooth_step(smoother, residual, width):
    mats = smoother.reshape(smoother.shape[:3] + (width, width)).astype(jnp.float32)
    rounded = residual.astype(jnp.bfloat16).astype(jnp.float32)
    return damping * jnp.einsum("xyzij,xyzjk->xyzik", mats, rounded, precision=lax.Precision.HIGHEST)


def reference(rhs, start, fine_blocks, fine_cols, fine_mass, fine_smoother, transfer, aggregate,
              coarse_blocks, coarse_cols, coarse_mass, coarse_smoother):
    sorted_fine = sort_blocks(fine_blocks, fine_cols, B)
    iterate = start
    for sweep in range(SWEEPS):
        rounded = round_keep(iterate)
        fine_res = rhs - apply_operator(sorted_fine, fine_mass, rounded)
        iterate = iterate + smooth_step(fine_smoother, fine_res, B)
    rounded = round_keep(iterate)
    residual = rhs - apply_operator(sorted_fine, fine_mass, rounded)
    mats = transfer.reshape(transfer.shape[:3] + (B, B)).astype(jnp.float32)
    projected = jnp.einsum("xyzji,xyzjk->xyzik", mats, residual.astype(jnp.bfloat16).astype(jnp.float32),
                           precision=lax.Precision.HIGHEST)
    blocks_x = NX // FX
    starts = (jnp.arange(blocks_x, dtype=jnp.int32) * FX)[:, None, None, None]
    local = aggregate.reshape(blocks_x, FX, NY, NZ) - starts
    local = local.reshape(blocks_x, FX, NY // 2, 2, NZ)
    targets = jnp.arange(FX, dtype=jnp.int32)[None, :, None, None, None, None]
    selector = (local[:, None] == targets).astype(jnp.float32)
    grouped = projected.reshape(blocks_x, FX, NY // 2, 2, NZ, B, LOADS)
    coarse_res = jnp.einsum("nuxyvz,nxyvzik->nuyzik", selector, grouped, precision=lax.Precision.HIGHEST)
    coarse_res = coarse_res.reshape(NX, NY // 2, NZ, B, LOADS)
    sorted_coarse = sort_blocks(coarse_blocks, coarse_cols, B)
    first = smooth_step(coarse_smoother, coarse_res, B)
    first_round = round_keep(first)
    remain = coarse_res - apply_operator(sorted_coarse, coarse_mass, first_round)
    correction = (first + smooth_step(coarse_smoother, remain, B)).astype(jnp.bfloat16)
    spread = jnp.einsum("nuxyvz,nuyzik->nxyvzik", selector,
                        correction.astype(jnp.float32).reshape(blocks_x, FX, NY // 2, NZ, B, LOADS),
                        precision=lax.Precision.HIGHEST)
    spread = spread.reshape(NX, NY, NZ, B, LOADS)
    added = jnp.einsum("xyzij,xyzjk->xyzik", mats, spread, precision=lax.Precision.HIGHEST)
    return iterate + added
```

```python
import functools

import jax
import jax.numpy as jnp
from jax import lax
from jax.experimental import pallas as pl
from jax.experimental.pallas import tpu as pltpu
from jax.sharding import PartitionSpec as P

SWEEPS = 2
DAMPING = 0.8
HALF = 32
LANES = 128
WIDE = 256
STEPS = 9
MASS = STEPS * HALF
LAST = MASS + HALF
ROWS = LAST + HALF
BF16 = jnp.bfloat16
F32 = jnp.float32


def sort_kernel(where_ref, cols_ref, mass_ref, smoother_ref, transfer_ref, blocks_ref, out_ref, scratch, *, layers, fixed):
    lane = lax.broadcasted_iota(jnp.int32, (HALF, LANES), 1)
    row = lax.broadcasted_iota(jnp.int32, (HALF, LANES), 0)
    on_diagonal = lane % 64 == 2 * row + lane // 64
    slot = lax.broadcasted_iota(jnp.int32, (24, 27), 0)
    tail = lax.broadcasted_iota(jnp.int32, (24, LANES), 0)
    for index in range(layers):
        layer = index if fixed else where_ref[0]
        code = (slot // 2) * 3 + slot % 2 - layer + 1
        cols = cols_ref[0, index : index + 1, :]
        pick = jnp.where((cols == code) & (slot < 18), 1.0, 0.0).astype(BF16)
        for t in range(0, HALF, 2):
            span = slice(t * LANES, (t + 2) * LANES)
            chosen = jnp.dot(pick, blocks_ref[index, :, span], preferred_element_type=F32)
            for half in range(2):
                part = slice((t + half) * LANES, (t + half + 1) * LANES)
                values = chosen[:, half * LANES : (half + 1) * LANES]
                values = jnp.where(tail == 18, smoother_ref[0, index : index + 1, part].astype(F32), values)
                values = jnp.where(tail == 19, transfer_ref[0, index : index + 1, part].astype(F32), values)
                scratch[pl.ds(t + half, 24, stride=HALF), :] = values
        for step in range(STEPS + 1):
            rows = step * HALF if step < STEPS else LAST
            for side in range(2):
                taken = scratch[(2 * step + side) * HALF : (2 * step + side + 1) * HALF, :]
                out_ref[index, rows : rows + HALF, side * LANES : (side + 1) * LANES] = taken.astype(BF16)
        mass = jnp.where(on_diagonal, mass_ref[0, index : index + 1, :].astype(F32), 0.0)
        for side in range(2):
            placed = jnp.where(layer == side, mass, 0.0)
            out_ref[index, MASS : MASS + HALF, side * LANES : (side + 1) * LANES] = placed.astype(BF16)


def sort_blocks(where, blocks, cols, mass, smoother, transfer, layers, fixed):
    steps = blocks.shape[0] // layers
    doubled = jnp.concatenate([mass, mass], axis=-1)
    per_row = lambda size: pl.BlockSpec((1, layers, size), lambda i: (i, 0, 0))
    return pl.pallas_call(
        functools.partial(sort_kernel, layers=layers, fixed=fixed),
        grid=(steps,),
        in_specs=[
            pl.BlockSpec(memory_space=pltpu.SMEM),
            per_row(27),
            per_row(LANES),
            per_row(4096),
            per_row(4096),
            pl.BlockSpec((layers, 27, 4096), lambda i: (i, 0, 0)),
        ],
        out_specs=pl.BlockSpec((layers, ROWS, WIDE), lambda i: (i, 0, 0)),
        out_shape=jax.ShapeDtypeStruct((steps * layers, ROWS, WIDE), BF16),
        scratch_shapes=[pltpu.VMEM((24 * HALF, LANES), F32)],
        name="sort_blocks",
    )(where, cols, doubled, smoother, transfer, blocks)


def two_sided(block):
    none = jnp.zeros_like(block)
    return jnp.concatenate(
        [jnp.concatenate([block, none], axis=1), jnp.concatenate([none, block], axis=1)], axis=0
    )


def add_from(total_ref, ops_ref, place, layers_of, targets):
    right = jnp.concatenate([two_sided(layers_of[0]), two_sided(layers_of[1])], axis=0)
    left, kept = [], []
    for x, y, step in targets:
        for z in range(2):
            row = place(x, y, z)
            left.append(ops_ref[row, step * HALF : (step + 1) * HALF, :])
            kept.append((x, y, z))
    given = jnp.dot(jnp.concatenate(left, axis=0), right, preferred_element_type=F32)
    sums = {}
    for index, key in enumerate(kept):
        part = given[index * HALF : (index + 1) * HALF]
        name = (id(key[0]), key[1], key[2])
        sums[name] = (key, part if name not in sums else sums[name][1] + part)
    for (x, y, z), part in sums.values():
        total_ref[x, y, z] += part


def natural(pairs, scratch):
    scratch[pl.ds(0, HALF, stride=2), :] = pairs[:, :LANES]
    scratch[pl.ds(1, HALF, stride=2), :] = pairs[:, LANES:]
    return scratch[...]


def make_place(where_ref, size_y, moved):
    if not moved:
        return lambda x, y, z: (x * size_y + y) * 2 + z
    count, each = moved

    def place(x, y, z):
        group = lax.bitwise_xor(jnp.asarray(x // each, jnp.int32), where_ref[1])
        layer = lax.bitwise_xor(jnp.int32(z), where_ref[0])
        return ((layer * count + group) * each + x % each) * size_y + y

    return place


def inner_kernel(where_ref, cells_ref, ops_ref, total_ref, *, moved):
    size_x, size_y = cells_ref.shape[:2]
    place = make_place(where_ref, size_y, moved)
    total_ref[...] = jnp.zeros_like(total_ref)

    def column(x, shifts):
        xs = {shift: x - shift for shift in shifts}
        for near in range(size_y):
            targets = []
            for shift in shifts:
                for y in range(size_y):
                    targets.append((xs[shift], y, (shift + 1) * 3 + near - y + 1))
            targets += [(xs[0], near, STEPS)]
            add_from(total_ref, ops_ref, place, cells_ref[x, near], targets)

    column(0, (-1, 0))
    lax.fori_loop(1, size_x - 1, lambda x, c: (column(x, (-1, 0, 1)), c)[1], 0)
    column(size_x - 1, (0, 1))


def beside_kernel(where_ref, low_ref, high_ref, ops_ref, given_ref, total_ref, *, moved):
    size_x, size_y = total_ref.shape[:2]
    place = make_place(where_ref, size_y, moved)
    total_ref[...] = given_ref[...]

    def column(x, shifts):
        xs = {shift: x - shift for shift in shifts}
        for ref, y, step in ((low_ref, 0, 0), (high_ref, size_y - 1, 2)):
            targets = [(xs[shift], y, (shift + 1) * 3 + step) for shift in shifts]
            add_from(total_ref, ops_ref, place, ref[x], targets)

    column(0, (-1, 0))
    lax.fori_loop(1, size_x - 1, lambda x, c: (column(x, (-1, 0, 1)), c)[1], 0)
    column(size_x - 1, (0, 1))


def add_ends(where_ref, before_ref, after_ref, ops_ref, total, place):
    size_x, size_y = total.shape[:2]
    for near in range(-1, size_y + 1):
        ys = [y for y in range(size_y) if abs(near - y) <= 1]
        keep_before = (where_ref[2] > 0).astype(BF16)
        keep_after = (where_ref[2] < where_ref[3] - 1).astype(BF16)
        before = [(0, y, near - y + 1) for y in ys]
        after = [(size_x - 1, y, 6 + near - y + 1) for y in ys]
        add_from(total, ops_ref, place, before_ref[near + 1] * keep_before, before)
        add_from(total, ops_ref, place, after_ref[near + 1] * keep_after, after)


def per_block(size_x, size_y, body):
    def step(x, carry):
        for y in range(size_y):
            for z in range(2):
                body(x, y, z)
        return carry

    lax.fori_loop(0, size_x, step, 0)


def smooth_kernel(where_ref, before_ref, after_ref, ops_ref, given_ref, rhs_ref, old_ref, new_ref, round_ref, total, scratch):
    size_x, size_y = total.shape[:2]
    place = make_place(where_ref, size_y, None)
    total[...] = given_ref[...]
    add_ends(where_ref, before_ref, after_ref, ops_ref, total, place)

    def body(x, y, z):
        residual = rhs_ref[x, y, z] - natural(total[x, y, z], scratch.at[0, y, z])
        left = ops_ref[place(x, y, z), LAST : LAST + HALF, :LANES]
        change = jnp.dot(left, two_sided(residual.astype(BF16)), preferred_element_type=F32)
        value = old_ref[x, y, z] + DAMPING * natural(change, scratch.at[1, y, z])
        new_ref[x, y, z] = value
        round_ref[x, y, z] = value.astype(BF16)

    per_block(size_x, size_y, body)


def restrict_kernel(
    where_ref, group_ref, before_ref, after_ref, ops_ref, given_ref, rhs_ref, coarse_ops_ref,
    coarse_ref, first_ref, round_ref, total, scratch, *, moved,
):
    size_x, size_y = total.shape[:2]
    coarse_y = coarse_ref.shape[1]
    place = make_place(where_ref, size_y, None)
    total[...] = given_ref[...]
    coarse_ref[...] = jnp.zeros_like(coarse_ref)
    add_ends(where_ref, before_ref, after_ref, ops_ref, total, place)

    def body(x, y, z):
        residual = rhs_ref[x, y, z] - natural(total[x, y, z], scratch.at[0, y, z])
        scratch[1, y, z] = residual
        even = scratch[1, y, z, pl.ds(0, HALF, stride=2), :]
        odd = scratch[1, y, z, pl.ds(1, HALF, stride=2), :]
        pairs = jnp.concatenate([even, odd], axis=1).astype(BF16)
        left = ops_ref[place(x, y, z), LAST : LAST + HALF, LANES:]
        both = lax.dot_general(left, pairs, (((0,), (0,)), ((), ())), preferred_element_type=F32)
        target = group_ref[(x * size_y + y) * 2 + z] - where_ref[2] * size_x
        coarse_ref[target, y // 2, z] += both[:64, :LANES] + both[64:, LANES:]

    per_block(size_x, size_y, body)
    coarse_place = make_place(where_ref, coarse_y, moved)

    def first(x, y, z):
        left = coarse_ops_ref[coarse_place(x, y, z), LAST : LAST + HALF, :LANES]
        change = jnp.dot(left, two_sided(coarse_ref[x, y, z].astype(BF16)), preferred_element_type=F32)
        value = DAMPING * natural(change, scratch.at[0, y, z])
        first_ref[x, y, z] = value
        round_ref[x, y, z] = value.astype(BF16)

    per_block(size_x, coarse_y, first)


def correct_kernel(
    where_ref, group_ref, before_ref, after_ref, coarse_ops_ref, given_ref, coarse_ref, first_ref, ops_ref, iterate_ref,
    out_ref, total, correction, scratch, *, moved,
):
    size_x, coarse_y = total.shape[:2]
    size_y = out_ref.shape[1]
    coarse_place = make_place(where_ref, coarse_y, moved)
    total[...] = given_ref[...]
    add_ends(where_ref, before_ref, after_ref, coarse_ops_ref, total, coarse_place)

    def second(x, y, z):
        remain = coarse_ref[x, y, z] - natural(total[x, y, z], scratch.at[0, y, z])
        left = coarse_ops_ref[coarse_place(x, y, z), LAST : LAST + HALF, :LANES]
        change = jnp.dot(left, two_sided(remain.astype(BF16)), preferred_element_type=F32)
        correction[x, y, z] = (first_ref[x, y, z] + DAMPING * natural(change, scratch.at[1, y, z])).astype(BF16)

    per_block(size_x, coarse_y, second)
    place = make_place(where_ref, size_y, None)

    def added(x, y, z):
        source = group_ref[(x * size_y + y) * 2 + z] - where_ref[2] * size_x
        left = ops_ref[place(x, y, z), LAST : LAST + HALF, LANES:]
        change = jnp.dot(left, two_sided(correction[source, y // 2, z]), preferred_element_type=F32)
        out_ref[x, y, z] = iterate_ref[x, y, z] + natural(change, scratch.at[0, y, z])

    per_block(size_x, size_y, added)


SMEM = pl.BlockSpec(memory_space=pltpu.SMEM)
VMEM = pl.BlockSpec(memory_space=pltpu.VMEM)


def call(kernel, name, scalars, operands, out_shape, scratch=()):
    return pl.pallas_call(
        kernel,
        in_specs=[SMEM] * len(scalars) + [VMEM] * len(operands),
        out_specs=jax.tree.map(lambda _: VMEM, out_shape),
        out_shape=out_shape,
        scratch_shapes=list(scratch),
        compiler_params=pltpu.CompilerParams(vmem_limit_bytes=24 * 1024 * 1024),
        name=name,
    )(*scalars, *operands)


def chain(axis, lateral, depth):
    up, down = [], []
    for i in range(lateral - 1):
        for d in range(depth):
            rise = (i * depth + d, (i + 1) * depth + d)
            fall = ((i + 1) * depth + d, i * depth + d)
            up.append(rise if d % 2 == 0 else fall)
            down.append(fall if d % 2 == 0 else rise)
    return up, down


def swap_sides(cells):
    lateral, depth = lax.axis_size("lateral"), lax.axis_size("depth")
    even = lax.axis_index("depth") % 2 == 0
    up, down = chain(("lateral", "depth"), lateral, depth)
    low, high = cells[:, 0], cells[:, -1]
    one = lax.ppermute(jnp.where(even, high, low), ("lateral", "depth"), up)
    two = lax.ppermute(jnp.where(even, low, high), ("lateral", "depth"), down)
    return jnp.where(even, one, two), jnp.where(even, two, one)


def swap_ends(cells, low, high):
    count = lax.axis_size("track")
    first = jnp.concatenate([low[:1], cells[0], high[:1]], axis=0)
    last = jnp.concatenate([low[-1:], cells[-1], high[-1:]], axis=0)
    before = lax.ppermute(last, "track", [(i, (i + 1) % count) for i in range(count)])
    after = lax.ppermute(first, "track", [((i + 1) % count, i) for i in range(count)])
    return before, after


def gather_coarse(sorted_ops, lateral):
    count = lax.axis_size("lateral")
    size_x, size_y = sorted_ops.shape[:2]
    each = size_y // count
    pieces = []
    for step in range(count):
        other = lax.bitwise_xor(lateral, step)
        piece = lax.dynamic_slice_in_dim(sorted_ops, other * each, each, axis=1)
        if step:
            piece = lax.ppermute(piece, "lateral", [(i, i ^ step) for i in range(count)])
        pieces.append(piece)
    own = jnp.stack(pieces)
    other = lax.ppermute(own, "depth", [(0, 1), (1, 0)])
    return jnp.stack([own, other]).reshape((2 * count * size_x * each,) + sorted_ops.shape[2:])


def per_device(
    rhs,
    start,
    fine_blocks,
    fine_cols,
    fine_mass,
    fine_smoother,
    transfer,
    aggregate,
    coarse_blocks,
    coarse_cols,
    coarse_mass,
    coarse_smoother,
):
    size_x, size_y, size_z, width, loads = rhs.shape
    track, lateral, depth = (lax.axis_index(a) for a in ("track", "lateral", "depth"))
    where = jnp.stack([depth, lateral, track, jnp.int32(lax.axis_size("track"))]).astype(jnp.int32)
    groups = aggregate.reshape(-1)
    part_x, all_y = coarse_blocks.shape[:2]
    coarse_y = size_y // 2
    moved = (lax.axis_size("lateral"), part_x)

    coarse_rows = part_x * all_y
    flat = lambda a: a.reshape((coarse_rows, 1) + a.shape[3:])
    coarse_local = sort_blocks(
        where, coarse_blocks.reshape(coarse_rows, 27, -1), flat(coarse_cols), flat(coarse_mass),
        flat(coarse_smoother), flat(coarse_smoother), 1, False,
    )
    coarse_ops = gather_coarse(coarse_local.reshape(part_x, all_y, ROWS, WIDE), lateral)

    columns = size_x * size_y
    pair = lambda a: a.reshape((columns, 2) + a.shape[3:])
    fine_ops = sort_blocks(
        where, fine_blocks.reshape(columns * 2, 27, -1), pair(fine_cols), pair(fine_mass),
        pair(fine_smoother), pair(transfer), 2, True,
    )

    field = (size_x, size_y, size_z, width, loads)
    coarse_field = (size_x, coarse_y, size_z, width, loads)
    sums = lambda shape: shape[:3] + (HALF, WIDE)
    full = jax.ShapeDtypeStruct
    scratch = [pltpu.VMEM((2, size_y, 2, width, loads), F32)]

    def apply(cells, ops, shift):
        low, high = swap_sides(cells)
        shape = full(sums(cells.shape), F32)
        inner = call(functools.partial(inner_kernel, moved=shift), "inner", [where], [cells, ops], shape)
        before, after = swap_ends(cells, low, high)
        beside = call(functools.partial(beside_kernel, moved=shift), "beside", [where], [low, high, ops, inner], shape)
        return before, after, beside

    iterate, rounded = start, start.astype(BF16)
    fine_total = [pltpu.VMEM(sums(field), F32)] + scratch
    for sweep in range(SWEEPS):
        before, after, beside = apply(rounded, fine_ops, None)
        iterate, rounded = call(
            smooth_kernel, "smooth", [where], [before, after, fine_ops, beside, rhs, iterate],
            [full(field, F32), full(field, BF16)], fine_total,
        )
    before, after, beside = apply(rounded, fine_ops, None)
    coarse_res, first, rounded = call(
        functools.partial(restrict_kernel, moved=moved), "restrict", [where, groups],
        [before, after, fine_ops, beside, rhs, coarse_ops],
        [full(coarse_field, F32), full(coarse_field, F32), full(coarse_field, BF16)], fine_total,
    )
    before, after, beside = apply(rounded, coarse_ops, moved)
    return call(
        functools.partial(correct_kernel, moved=moved), "correct", [where, groups],
        [before, after, coarse_ops, beside, coarse_res, first, fine_ops, iterate],
        full(field, F32),
        [pltpu.VMEM(sums(coarse_field), F32), pltpu.VMEM(coarse_field, BF16)] + scratch,
    )


def solution(mesh):
    in_specs = (
        P("track", "lateral", None, None, "depth"),
        P("track", "lateral", None, None, "depth"),
        P("track", "lateral", None, None, None),
        P("track", "lateral", None, None),
        P("track", "lateral", None, None),
        P("track", "lateral", None, None),
        P("track", "lateral", None, None),
        P("track", "lateral", None),
        P(("track", "lateral"), None, "depth", None, None),
        P(("track", "lateral"), None, "depth", None),
        P(("track", "lateral"), None, "depth", None),
        P(("track", "lateral"), None, "depth", None),
    )
    out_specs = P("track", "lateral", None, None, "depth")
    return jax.shard_map(
        per_device, mesh=mesh, in_specs=in_specs, out_specs=out_specs, check_vma=False
    )
```

```python
import functools

import jax
import jax.numpy as jnp
from jax import lax
from jax.experimental import pallas as pl
from jax.experimental.pallas import tpu as pltpu
from jax.sharding import PartitionSpec as P

SWEEPS = 2
DAMPING = 0.8
HALF = 32
LANES = 128
WIDE = 256
STEPS = 9
BF16 = jnp.bfloat16
F32 = jnp.float32
LIMIT = 8 * 1024 * 1024


def listed_at(cols_ref, slots, index, groups):
    for group in range(groups):
        codes = [cols_ref[index * groups + group, slot] for slot in range(27)]
        for slot, code in enumerate(codes):
            slots[group, code] = slot


def diagonal(mass, rows, groups):
    row = lax.broadcasted_iota(jnp.int32, (rows, LANES), 0)
    lane = lax.broadcasted_iota(jnp.int32, (rows, LANES), 1)
    spread = jnp.zeros((rows, LANES), F32)
    for group in range(groups):
        spread = jnp.where(row % groups == group, mass[group : group + 1], spread)
    return jnp.where(lane % 64 == 2 * (row // groups) + lane // 64, spread, 0.0)


def fine_sort_kernel(cols_ref, mass_ref, blocks_ref, out_ref, slots):
    second = lax.broadcasted_iota(jnp.int32, (2 * HALF, LANES), 0) % 2 == 1
    count = out_ref.shape[0]

    def column(index, carry):
        listed_at(cols_ref, slots, pl.program_id(0) * count + index, 2)
        for step in range(STEPS):
            for side in range(2):
                upper = blocks_ref[index, slots[0, 3 * step + side + 1]]
                lower = blocks_ref[index, slots[1, 3 * step + side]]
                span = slice(side * LANES, (side + 1) * LANES)
                out_ref[index, step * 2 * HALF : (step + 1) * 2 * HALF, span] = jnp.where(second, lower, upper)
        mass = mass_ref[index].astype(F32)
        mass = diagonal(jnp.concatenate([mass, mass], axis=1), 2 * HALF, 2)
        for side in range(2):
            span = slice(side * LANES, (side + 1) * LANES)
            out_ref[index, STEPS * 2 * HALF :, span] = jnp.where(second == (side == 1), mass, 0.0).astype(BF16)
        return carry

    lax.fori_loop(0, count, column, 0)


def coarse_sort_kernel(where_ref, cols_ref, mass_ref, smoother_ref, blocks_ref, *refs):
    pieces, (slots, scratch) = refs[:-2], refs[-2:]
    groups = blocks_ref.shape[2] // HALF
    each = groups // len(pieces)
    rows = groups * HALF
    kind = lax.broadcasted_iota(jnp.int32, (rows, LANES), 0) % groups

    def hand_out(values, first, span):
        scratch[...] = values
        for step, piece in enumerate(pieces):
            for part in range(each):
                y = lax.bitwise_xor(where_ref[1], step) * each + part
                taken = scratch[pl.ds(y, HALF, stride=groups), :]
                piece[part, first : first + HALF, span] = taken.astype(BF16)

    listed_at(cols_ref, slots, pl.program_id(0), groups)
    for step in range(STEPS):
        for side in range(2):
            code = 3 * step + side + 1 - where_ref[0]
            values = blocks_ref[0, slots[0, code]]
            for group in range(1, groups):
                values = jnp.where(kind == group, blocks_ref[0, slots[group, code]], values)
            hand_out(values.astype(F32), step * HALF, slice(side * LANES, (side + 1) * LANES))
    hand_out(smoother_ref[0].astype(F32), STEPS * HALF, slice(0, LANES))
    mass = mass_ref[0].astype(F32)
    mass = diagonal(jnp.concatenate([mass, mass], axis=1), rows, groups)
    hand_out(mass, STEPS * HALF, slice(LANES, WIDE))


def in_hbm(array):
    return pltpu.with_memory_space_constraint(array, pltpu.HBM)


def sort_fine(blocks, cols, mass):
    size_x, size_y, layers = blocks.shape[:3]
    columns = size_x * size_y
    paired = blocks.reshape(size_x, size_y, layers, 27, HALF, LANES).transpose(0, 1, 3, 4, 2, 5)
    batch = size_y
    rows = (STEPS + 1) * 2 * HALF
    return pl.pallas_call(
        fine_sort_kernel,
        grid=(columns // batch // 2,),
        in_specs=[
            SMEM,
            pl.BlockSpec((2 * batch, layers, 64), lambda i: (i, 0, 0)),
            pl.BlockSpec((2 * batch, 27, layers * HALF, LANES), lambda i: (i, 0, 0, 0)),
        ],
        out_specs=pl.BlockSpec((2 * batch, rows, WIDE), lambda i: (i, 0, 0)),
        out_shape=jax.ShapeDtypeStruct((columns, rows, WIDE), BF16),
        scratch_shapes=[pltpu.SMEM((2, 27), jnp.int32)],
        compiler_params=pltpu.CompilerParams(vmem_limit_bytes=LIMIT),
        name="sort_fine",
    )(
        cols.reshape(columns * layers, 27),
        in_hbm(mass.reshape(columns, layers, 64)),
        in_hbm(paired.reshape(columns, 27, layers * HALF, LANES)),
    )


def sort_coarse(where, blocks, cols, mass, smoother, count):
    size_x, size_y = blocks.shape[:2]
    paired = blocks.reshape(size_x, size_y, 27, HALF, LANES).transpose(0, 2, 3, 1, 4)
    smoothers = smoother.reshape(size_x, size_y, HALF, LANES).transpose(0, 2, 1, 3)
    each = size_y // count
    rows = (STEPS + 1) * HALF
    piece = jax.ShapeDtypeStruct((size_x * each, rows, WIDE), BF16)
    return pl.pallas_call(
        coarse_sort_kernel,
        grid=(size_x,),
        in_specs=[
            SMEM,
            SMEM,
            pl.BlockSpec((1, size_y, 64), lambda i: (i, 0, 0)),
            pl.BlockSpec((1, size_y * HALF, LANES), lambda i: (i, 0, 0)),
            pl.BlockSpec((1, 27, size_y * HALF, LANES), lambda i: (i, 0, 0, 0)),
        ],
        out_specs=[pl.BlockSpec((each, rows, WIDE), lambda i: (i, 0, 0))] * count,
        out_shape=[piece] * count,
        scratch_shapes=[pltpu.SMEM((size_y, 27), jnp.int32), pltpu.VMEM((size_y * HALF, LANES), F32)],
        compiler_params=pltpu.CompilerParams(vmem_limit_bytes=LIMIT),
        name="sort_coarse",
    )(
        where,
        cols.reshape(size_x * size_y, 27),
        in_hbm(mass.reshape(size_x, size_y, 64)),
        in_hbm(smoothers.reshape(size_x, size_y * HALF, LANES)),
        in_hbm(paired.reshape(size_x, 27, size_y * HALF, LANES)),
    )


def two_sided(block):
    none = jnp.zeros_like(block)
    return jnp.concatenate(
        [jnp.concatenate([block, none], axis=1), jnp.concatenate([none, block], axis=1)], axis=0
    )


def mask_layers(block, kind):
    none = jnp.zeros_like(block)
    return jnp.concatenate([jnp.where(kind == 0, block, none), jnp.where(kind == 1, block, none)], axis=1)


class Fine:
    def __init__(self, ops_ref, size_y):
        self.ops_ref, self.size_y = ops_ref, size_y

    def kind(self):
        return lax.broadcasted_iota(jnp.int32, (2 * HALF, LANES), 0) % 2

    def step(self, x, y, step):
        return self.ops_ref[x * self.size_y + y, step * 2 * HALF : (step + 1) * 2 * HALF, :]

    def mass(self, x, y):
        return self.step(x, y, STEPS)

    def half(self, total, place, z, parity):
        return total[(*place, parity, pl.ds(z, HALF, stride=2), slice(None))]


class Coarse(Fine):
    def kind(self):
        return lax.broadcasted_iota(jnp.int32, (2 * HALF, LANES), 0) // HALF

    def smoother(self, x, y):
        return self.step(x, y, STEPS)[:, :LANES]

    def mass(self, x, y):
        return mask_layers(self.step(x, y, STEPS)[:, LANES:], self.kind())

    def half(self, total, place, z, parity):
        return total[(*place, parity, pl.ds(z * HALF, HALF), slice(None))]


def join_coarse(where_ref, pieces, ops_ref, size_y):
    count = len(pieces) // 2
    each = pieces[0].shape[0] // size_y
    for index, piece in enumerate(pieces):
        layer = lax.bitwise_xor(where_ref[0], index // count)
        group = lax.bitwise_xor(where_ref[1], index % count)
        for part in range(piece.shape[0]):
            for step in range(STEPS + 1):
                rows = pl.ds(pl.multiple_of(step * 2 * HALF + layer * HALF, HALF), HALF)
                ops_ref[group * each * size_y + part, rows, :] = piece[part, step * HALF : (step + 1) * HALF, :]


def both_layers(cells):
    return jnp.concatenate([two_sided(cells[0]), two_sided(cells[1])], axis=0)


def add_from(total_ref, rows, cells, targets, own=None):
    left = [rows.step(*target) for target in targets]
    if own is not None:
        left.append(rows.mass(*own))
    given = jnp.dot(jnp.concatenate(left, axis=0), both_layers(cells), preferred_element_type=F32)
    parts = [given[index * 2 * HALF : (index + 1) * 2 * HALF] for index in range(len(left))]
    for (x, y, _), part in zip(targets, parts):
        if own is not None and own[0] is x and own[1] == y:
            part = part + parts[-1]
        for parity in range(2):
            total_ref[x, y, parity] += part[:, parity * LANES : (parity + 1) * LANES]


def natural(rows, total, place, scratch):
    blocks = []
    for z in range(2):
        for parity in range(2):
            scratch[z, pl.ds(parity, HALF, stride=2), :] = rows.half(total, place, z, parity)
        blocks.append(scratch[z])
    return blocks


def smoothed(rows, left, cells, total, place, scratch):
    given = jnp.dot(left, both_layers([cell.astype(BF16) for cell in cells]), preferred_element_type=F32)
    for parity in range(2):
        total[(*place, parity)] = given[:, parity * LANES : (parity + 1) * LANES]
    return natural(rows, total, place, scratch)


def over_columns(size_x, column):
    column(0, (-1, 0))
    lax.fori_loop(1, size_x - 1, lambda x, c: (column(x, (-1, 0, 1)), c)[1], 0)
    column(size_x - 1, (0, 1))


def inner_kernel(cells_ref, ops_ref, total_ref, *, grid):
    size_x, size_y = cells_ref.shape[:2]
    rows = grid(ops_ref, size_y)
    total_ref[...] = jnp.zeros_like(total_ref)

    def column(x, shifts):
        for near in range(size_y):
            targets = []
            for shift in shifts:
                own = x - shift if shift else x
                targets += [(own, y, (shift + 1) * 3 + near - y + 1) for y in range(size_y)]
            add_from(total_ref, rows, cells_ref[x, near], targets, (x, near))

    over_columns(size_x, column)


def beside_kernel(where_ref, one_ref, two_ref, ops_ref, given_ref, total_ref, *, grid):
    size_x, size_y = total_ref.shape[:2]
    rows = grid(ops_ref, size_y)
    total_ref[...] = given_ref[...]

    def side(ref, y, step):
        def column(x, shifts):
            add_from(total_ref, rows, ref[x], [(x - shift, y, (shift + 1) * 3 + step) for shift in shifts])

        over_columns(size_x, column)

    for odd, low_ref, high_ref in ((0, one_ref, two_ref), (1, two_ref, one_ref)):
        pl.when((where_ref[0] == odd) & (where_ref[1] > 0))(functools.partial(side, low_ref, 0, 0))
        pl.when((where_ref[0] == odd) & (where_ref[1] < where_ref[4] - 1))(functools.partial(side, high_ref, size_y - 1, 2))


def give_faces(where_ref, cells, one_ref, two_ref, x):
    even = where_ref[0] % 2 == 0
    for z in range(2):
        low, high = (cells[0][z], cells[-1][z]) if isinstance(cells, list) else (cells[0, z], cells[cells.shape[0] - 1, z])
        one_ref[x, z] = jnp.where(even, high, low)
        two_ref[x, z] = jnp.where(even, low, high)


def round_kernel(where_ref, start_ref, round_ref, one_ref, two_ref):
    for x in range(start_ref.shape[0]):
        cells = [[start_ref[x, y, z].astype(BF16) for z in range(2)] for y in range(start_ref.shape[1])]
        for y, column in enumerate(cells):
            for z in range(2):
                round_ref[x, y, z] = column[z]
        give_faces(where_ref, cells, one_ref, two_ref, x)


def round_start(where, start):
    size_x, size_y, layers, width, loads = start.shape
    batch = size_x // 4
    side = pl.BlockSpec((batch, layers, width, loads), lambda i: (i, 0, 0, 0))
    whole = pl.BlockSpec((batch, size_y, layers, width, loads), lambda i: (i, 0, 0, 0, 0))
    face = jax.ShapeDtypeStruct((size_x, layers, width, loads), BF16)
    return pl.pallas_call(
        round_kernel,
        grid=(4,),
        in_specs=[SMEM, whole],
        out_specs=[whole, side, side],
        out_shape=[jax.ShapeDtypeStruct(start.shape, BF16), face, face],
        compiler_params=pltpu.CompilerParams(vmem_limit_bytes=LIMIT),
        name="round_start",
    )(where, in_hbm(start))


def add_ends(where_ref, before_ref, after_ref, rows, total):
    size_x, size_y = total.shape[:2]
    for near in range(-1, size_y + 1):
        ys = [y for y in range(size_y) if abs(near - y) <= 1]
        place = near + 1
        if near in (-1, size_y):
            odd = where_ref[0] % 2
            place = odd * (size_y + 1) if near < 0 else (1 - odd) * (size_y + 1)
        inside = True
        if near < 0:
            inside = where_ref[1] > 0
        if near == size_y:
            inside = where_ref[1] < where_ref[4] - 1
        before, after = before_ref[place], after_ref[place]
        before = jnp.where((where_ref[2] > 0) & inside, before, jnp.zeros_like(before))
        after = jnp.where((where_ref[2] < where_ref[3] - 1) & inside, after, jnp.zeros_like(after))
        add_from(total, rows, before, [(0, y, near - y + 1) for y in ys])
        add_from(total, rows, after, [(size_x - 1, y, 6 + near - y + 1) for y in ys])


def per_column(size_x, size_y, body, after=None):
    def step(x, carry):
        for y in range(size_y):
            body(x, y)
        if after is not None:
            after(x)
        return carry

    lax.fori_loop(0, size_x, step, 0)


def smooth_kernel(
    where_ref, before_ref, after_ref, ops_ref, smoother_ref, given_ref, rhs_ref, old_ref, new_ref, round_ref, one_ref, two_ref,
    total, scratch,
):
    size_x, size_y = total.shape[:2]
    rows = Fine(ops_ref, size_y)
    total[...] = given_ref[...]
    add_ends(where_ref, before_ref, after_ref, rows, total)

    def body(x, y):
        applied = natural(rows, total, (x, y), scratch.at[0, y])
        residual = [rhs_ref[x, y, z] - applied[z] for z in range(2)]
        left = mask_layers(smoother_ref[x * size_y + y], rows.kind())
        change = smoothed(rows, left, residual, total, (x, y), scratch.at[1, y])
        for z in range(2):
            value = old_ref[x, y, z] + DAMPING * change[z]
            new_ref[x, y, z] = value
            round_ref[x, y, z] = value.astype(BF16)

    per_column(size_x, size_y, body, lambda x: give_faces(where_ref, round_ref.at[x], one_ref, two_ref, x))


def restrict_kernel(
    where_ref, group_ref, before_ref, after_ref, ops_ref, transfer_ref, given_ref, rhs_ref, *refs
):
    pieces = refs[:-8]
    coarse_ref, first_ref, round_ref, one_ref, two_ref, coarse_ops_ref, total, scratch = refs[-8:]
    size_x, size_y = total.shape[:2]
    coarse_y = coarse_ref.shape[1]
    rows = Fine(ops_ref, size_y)
    total[...] = given_ref[...]
    coarse_ref[...] = jnp.zeros_like(coarse_ref)
    add_ends(where_ref, before_ref, after_ref, rows, total)

    def body(x, y):
        applied = natural(rows, total, (x, y), scratch.at[0, y])
        for z in range(2):
            scratch[1, y, z] = rhs_ref[x, y, z] - applied[z]
            for parity in range(2):
                total[x, y, parity, pl.ds(z, HALF, stride=2), :] = scratch[1, y, z, pl.ds(parity, HALF, stride=2), :]
        left = mask_layers(transfer_ref[x * size_y + y], rows.kind())
        right = jnp.concatenate([total[x, y, 0], total[x, y, 1]], axis=1).astype(BF16)
        both = lax.dot_general(left, right, (((0,), (0,)), ((), ())), preferred_element_type=F32)
        for z in range(2):
            target = group_ref[(x * size_y + y) * 2 + z] - where_ref[2] * size_x
            own = both[z * LANES : (z + 1) * LANES]
            coarse_ref[target, y // 2, z] += own[:64, :LANES] + own[64:, LANES:]

    per_column(size_x, size_y, body)
    join_coarse(where_ref, pieces, coarse_ops_ref, coarse_y)
    coarse_rows = Coarse(coarse_ops_ref, coarse_y)

    def first(x, y):
        left = mask_layers(coarse_rows.smoother(x, y), coarse_rows.kind())
        cells = [coarse_ref[x, y, z] for z in range(2)]
        change = smoothed(coarse_rows, left, cells, total, (x, y), scratch.at[0, y])
        for z in range(2):
            value = DAMPING * change[z]
            first_ref[x, y, z] = value
            round_ref[x, y, z] = value.astype(BF16)

    per_column(size_x, coarse_y, first, lambda x: give_faces(where_ref, round_ref.at[x], one_ref, two_ref, x))


def correct_kernel(
    where_ref, group_ref, before_ref, after_ref, coarse_ops_ref, given_ref, coarse_ref, first_ref, transfer_ref,
    iterate_ref, out_ref, total, correction, scratch,
):
    size_x, coarse_y = total.shape[:2]
    size_y = out_ref.shape[1]
    coarse_rows = Coarse(coarse_ops_ref, coarse_y)
    total[...] = given_ref[...]
    add_ends(where_ref, before_ref, after_ref, coarse_rows, total)

    def second(x, y):
        applied = natural(coarse_rows, total, (x, y), scratch.at[0, y])
        remain = [coarse_ref[x, y, z] - applied[z] for z in range(2)]
        left = mask_layers(coarse_rows.smoother(x, y), coarse_rows.kind())
        change = smoothed(coarse_rows, left, remain, total, (x, y), scratch.at[1, y])
        for z in range(2):
            correction[x, y, z] = (first_ref[x, y, z] + DAMPING * change[z]).astype(BF16)

    per_column(size_x, coarse_y, second)
    rows = Fine(None, size_y)

    def added(x, y):
        sources = [group_ref[(x * size_y + y) * 2 + z] - where_ref[2] * size_x for z in range(2)]
        cells = [correction[sources[z], y // 2, z] for z in range(2)]
        left = mask_layers(transfer_ref[x * size_y + y], rows.kind())
        change = smoothed(rows, left, cells, total, (x, 0), scratch.at[0, y])
        for z in range(2):
            out_ref[x, y, z] = iterate_ref[x, y, z] + change[z]

    per_column(size_x, size_y, added)


SMEM = pl.BlockSpec(memory_space=pltpu.SMEM)
VMEM = pl.BlockSpec(memory_space=pltpu.VMEM)


def call(kernel, name, scalars, operands, out_shape, scratch=()):
    return pl.pallas_call(
        kernel,
        in_specs=[SMEM] * len(scalars) + [VMEM] * len(operands),
        out_specs=jax.tree.map(lambda _: VMEM, out_shape),
        out_shape=out_shape,
        scratch_shapes=list(scratch),
        compiler_params=pltpu.CompilerParams(vmem_limit_bytes=LIMIT),
        name=name,
    )(*scalars, *operands)


def swap_sides(one, two):
    lateral, depth = lax.axis_size("lateral"), lax.axis_size("depth")
    ring = [i * depth for i in range(lateral)] + [i * depth + 1 for i in reversed(range(lateral))]
    onward = list(zip(ring, ring[1:] + ring[:1]))
    back = [(b, a) for a, b in onward]
    return lax.ppermute(one, ("lateral", "depth"), onward), lax.ppermute(two, ("lateral", "depth"), back)


def swap_ends(cells, one, two):
    count = lax.axis_size("track")
    first = jnp.concatenate([one[:1], cells[0], two[:1]], axis=0)
    last = jnp.concatenate([one[-1:], cells[-1], two[-1:]], axis=0)
    before = lax.ppermute(last, "track", [(i, (i + 1) % count) for i in range(count)])
    after = lax.ppermute(first, "track", [((i + 1) % count, i) for i in range(count)])
    return before, after


def send_coarse(piece, step):
    count = lax.axis_size("lateral")
    return lax.ppermute(piece, "lateral", [(i, i ^ step) for i in range(count)])


def per_device(
    rhs,
    start,
    fine_blocks,
    fine_cols,
    fine_mass,
    fine_smoother,
    transfer,
    aggregate,
    coarse_blocks,
    coarse_cols,
    coarse_mass,
    coarse_smoother,
):
    size_x, size_y, size_z, width, loads = rhs.shape
    track, lateral, depth = (lax.axis_index(a) for a in ("track", "lateral", "depth"))
    count = lax.axis_size("lateral")
    where = jnp.stack([depth, lateral, track, jnp.int32(lax.axis_size("track")), jnp.int32(count)]).astype(jnp.int32)
    groups = aggregate.reshape(-1)
    part_x = coarse_blocks.shape[0]
    coarse_y = size_y // 2

    paired = lambda a: a.reshape(size_x, size_y, size_z, HALF, LANES).transpose(0, 1, 3, 2, 4).reshape(-1, 2 * HALF, LANES)
    smoothers, transfers = paired(fine_smoother), paired(transfer)
    field = (size_x, size_y, size_z, width, loads)
    coarse_field = (size_x, coarse_y, size_z, width, loads)
    sums = lambda shape: shape[:2] + (2, 2 * HALF, LANES)
    full = jax.ShapeDtypeStruct
    scratch = [pltpu.VMEM((2, size_y, 2, width, loads), F32)]

    def outer(cells, ops, grid, one, two, *others):
        shape = full(sums(cells.shape), F32)
        inner = call(functools.partial(inner_kernel, grid=grid), "inner", [], [cells, ops], shape)
        inner, one, two, *others = lax.optimization_barrier((inner, one, two, *others))
        before, after = swap_ends(cells, one, two)
        beside = call(functools.partial(beside_kernel, grid=grid), "beside", [where], [one, two, ops, inner], shape)
        return before, after, beside, *others

    face = full((size_x, size_z, width, loads), BF16)
    rounded, one, two = round_start(where, start)
    iterate = start
    later, one, two = lax.optimization_barrier((where, one, two))
    one, two = swap_sides(one, two)
    pieces = sort_coarse(later, coarse_blocks, coarse_cols, coarse_mass, coarse_smoother, count)
    fine_cols, *pieces = lax.optimization_barrier((fine_cols, *pieces))
    middle = count // 2 + 1
    pieces[1:middle] = [send_coarse(pieces[step], step) for step in range(1, middle)]
    fine_ops = sort_fine(fine_blocks, fine_cols, fine_mass)
    fine_total = [pltpu.VMEM(sums(field), F32)] + scratch
    for sweep in range(SWEEPS):
        last = sweep == SWEEPS - 1
        before, after, beside, *held = outer(rounded, fine_ops, Fine, one, two, *(pieces[middle:] if last else ()))
        if last:
            pieces[middle:] = [send_coarse(piece, middle + index) for index, piece in enumerate(held)]
        iterate, rounded, one, two = call(
            smooth_kernel, "smooth", [where], [before, after, fine_ops, smoothers, beside, rhs, iterate],
            [full(field, F32), full(field, BF16), face, face], fine_total,
        )
        if sweep == 0:
            one, *pieces[1:middle] = lax.optimization_barrier((one, *pieces[1:middle]))
        one, two = swap_sides(one, two)
    before, after, beside, *pieces[middle:] = outer(rounded, fine_ops, Fine, one, two, *pieces[middle:])
    pieces = pieces + [lax.ppermute(piece, "depth", [(0, 1), (1, 0)]) for piece in pieces]
    coarse_rows = full((size_x * coarse_y, (STEPS + 1) * 2 * HALF, WIDE), BF16)
    coarse_res, first, rounded, one, two, coarse_ops = call(
        restrict_kernel, "restrict", [where, groups], [before, after, fine_ops, transfers, beside, rhs, *pieces],
        [full(coarse_field, F32), full(coarse_field, F32), full(coarse_field, BF16), face, face, coarse_rows],
        fine_total,
    )
    one, two = swap_sides(one, two)
    before, after, beside = outer(rounded, coarse_ops, Coarse, one, two)
    return call(
        correct_kernel, "correct", [where, groups],
        [before, after, coarse_ops, beside, coarse_res, first, transfers, iterate],
        full(field, F32),
        [pltpu.VMEM(sums(coarse_field), F32), pltpu.VMEM(coarse_field, BF16)] + scratch,
    )


def solution(mesh):
    in_specs = (
        P("track", "lateral", None, None, "depth"),
        P("track", "lateral", None, None, "depth"),
        P("track", "lateral", None, None, None),
        P("track", "lateral", None, None),
        P("track", "lateral", None, None),
        P("track", "lateral", None, None),
        P("track", "lateral", None, None),
        P("track", "lateral", None),
        P(("track", "lateral"), None, "depth", None, None),
        P(("track", "lateral"), None, "depth", None),
        P(("track", "lateral"), None, "depth", None),
        P(("track", "lateral"), None, "depth", None),
    )
    out_specs = P("track", "lateral", None, None, "depth")
    return jax.shard_map(
        per_device, mesh=mesh, in_specs=in_specs, out_specs=out_specs, check_vma=False
    )
```

```python
import functools

import jax
import jax.numpy as jnp
from jax import lax
from jax.experimental import pallas as pl
from jax.experimental.pallas import tpu as pltpu
from jax.sharding import PartitionSpec as P

SWEEPS = 2
DAMPING = 0.8
HALF = 32
LANES = 128
WIDE = 256
STEPS = 9
BF16 = jnp.bfloat16
F32 = jnp.float32
LIMIT = 8 * 1024 * 1024


def listed_at(cols_ref, slots, index, groups):
    for group in range(groups):
        codes = [cols_ref[index * groups + group, slot] for slot in range(27)]
        for slot, code in enumerate(codes):
            slots[group, code] = slot


def diagonal(mass, rows, groups):
    row = lax.broadcasted_iota(jnp.int32, (rows, LANES), 0)
    lane = lax.broadcasted_iota(jnp.int32, (rows, LANES), 1)
    spread = jnp.zeros((rows, LANES), F32)
    for group in range(groups):
        spread = jnp.where(row % groups == group, mass[group : group + 1], spread)
    return jnp.where(lane % 64 == 2 * (row // groups) + lane // 64, spread, 0.0)


def fine_sort_kernel(cols_ref, mass_ref, blocks_ref, out_ref, slots):
    second = lax.broadcasted_iota(jnp.int32, (2 * HALF, LANES), 0) % 2 == 1
    count = out_ref.shape[0]

    def column(index, carry):
        listed_at(cols_ref, slots, pl.program_id(0) * count + index, 2)
        for step in range(STEPS):
            for side in range(2):
                upper = blocks_ref[index, slots[0, 3 * step + side + 1]]
                lower = blocks_ref[index, slots[1, 3 * step + side]]
                span = slice(side * LANES, (side + 1) * LANES)
                out_ref[index, step * 2 * HALF : (step + 1) * 2 * HALF, span] = jnp.where(second, lower, upper)
        mass = mass_ref[index].astype(F32)
        mass = diagonal(jnp.concatenate([mass, mass], axis=1), 2 * HALF, 2)
        for side in range(2):
            span = slice(side * LANES, (side + 1) * LANES)
            out_ref[index, STEPS * 2 * HALF :, span] = jnp.where(second == (side == 1), mass, 0.0).astype(BF16)
        return carry

    lax.fori_loop(0, count, column, 0)


def coarse_sort_kernel(cols_ref, mass_ref, smoother_ref, blocks_ref, *refs):
    pieces, (slots, scratch) = refs[:-2], refs[-2:]
    groups = blocks_ref.shape[2] // HALF
    each = groups // len(pieces)
    rows = groups * HALF
    kind = lax.broadcasted_iota(jnp.int32, (rows, LANES), 0) % groups

    def hand_out(values, first, span):
        scratch[...] = values
        for step, piece in enumerate(pieces):
            for part in range(each):
                y = lax.bitwise_xor(lax.axis_index("lateral"), step) * each + part
                taken = scratch[pl.ds(y, HALF, stride=groups), :]
                piece[part, first : first + HALF, span] = taken.astype(BF16)

    listed_at(cols_ref, slots, pl.program_id(0), groups)
    for step in range(STEPS):
        for side in range(2):
            code = 3 * step + side + 1 - lax.axis_index("depth")
            values = blocks_ref[0, slots[0, code]]
            for group in range(1, groups):
                values = jnp.where(kind == group, blocks_ref[0, slots[group, code]], values)
            hand_out(values.astype(F32), step * HALF, slice(side * LANES, (side + 1) * LANES))
    hand_out(smoother_ref[0].astype(F32), STEPS * HALF, slice(0, LANES))
    mass = mass_ref[0].astype(F32)
    mass = diagonal(jnp.concatenate([mass, mass], axis=1), rows, groups)
    hand_out(mass, STEPS * HALF, slice(LANES, WIDE))


def in_hbm(array):
    return pltpu.with_memory_space_constraint(array, pltpu.HBM)


def sort_fine(blocks, cols, mass):
    size_x, size_y, layers = blocks.shape[:3]
    columns = size_x * size_y
    paired = blocks.reshape(size_x, size_y, layers, 27, HALF, LANES).transpose(0, 1, 3, 4, 2, 5)
    batch = size_y
    rows = (STEPS + 1) * 2 * HALF
    return pl.pallas_call(
        fine_sort_kernel,
        grid=(columns // batch // 2,),
        in_specs=[
            SMEM,
            pl.BlockSpec((2 * batch, layers, 64), lambda i: (i, 0, 0)),
            pl.BlockSpec((2 * batch, 27, layers * HALF, LANES), lambda i: (i, 0, 0, 0)),
        ],
        out_specs=pl.BlockSpec((2 * batch, rows, WIDE), lambda i: (i, 0, 0)),
        out_shape=jax.ShapeDtypeStruct((columns, rows, WIDE), BF16),
        scratch_shapes=[pltpu.SMEM((2, 27), jnp.int32)],
        compiler_params=pltpu.CompilerParams(vmem_limit_bytes=LIMIT),
        name="sort_fine",
    )(
        in_hbm(cols.reshape(columns * layers, 27)),
        in_hbm(mass.reshape(columns, layers, 64)),
        in_hbm(paired.reshape(columns, 27, layers * HALF, LANES)),
    )


def sort_coarse(blocks, cols, mass, smoother, count):
    size_x, size_y = blocks.shape[:2]
    paired = blocks.reshape(size_x, size_y, 27, HALF, LANES).transpose(0, 2, 3, 1, 4)
    smoothers = smoother.reshape(size_x, size_y, HALF, LANES).transpose(0, 2, 1, 3)
    each = size_y // count
    rows = (STEPS + 1) * HALF
    piece = jax.ShapeDtypeStruct((size_x * each, rows, WIDE), BF16)
    return pl.pallas_call(
        coarse_sort_kernel,
        grid=(size_x,),
        in_specs=[
            SMEM,
            pl.BlockSpec((1, size_y, 64), lambda i: (i, 0, 0)),
            pl.BlockSpec((1, size_y * HALF, LANES), lambda i: (i, 0, 0)),
            pl.BlockSpec((1, 27, size_y * HALF, LANES), lambda i: (i, 0, 0, 0)),
        ],
        out_specs=[pl.BlockSpec((each, rows, WIDE), lambda i: (i, 0, 0))] * count,
        out_shape=[piece] * count,
        scratch_shapes=[pltpu.SMEM((size_y, 27), jnp.int32), pltpu.VMEM((size_y * HALF, LANES), F32)],
        compiler_params=pltpu.CompilerParams(vmem_limit_bytes=LIMIT),
        name="sort_coarse",
    )(
        in_hbm(cols.reshape(size_x * size_y, 27)),
        in_hbm(mass.reshape(size_x, size_y, 64)),
        in_hbm(smoothers.reshape(size_x, size_y * HALF, LANES)),
        in_hbm(paired.reshape(size_x, 27, size_y * HALF, LANES)),
    )


def two_sided(block):
    none = jnp.zeros_like(block)
    return jnp.concatenate(
        [jnp.concatenate([block, none], axis=1), jnp.concatenate([none, block], axis=1)], axis=0
    )


def mask_layers(block, kind):
    none = jnp.zeros_like(block)
    return jnp.concatenate([jnp.where(kind == 0, block, none), jnp.where(kind == 1, block, none)], axis=1)


class Fine:
    def __init__(self, ops_ref, size_y):
        self.ops_ref, self.size_y = ops_ref, size_y

    def kind(self):
        return lax.broadcasted_iota(jnp.int32, (2 * HALF, LANES), 0) % 2

    def step(self, x, y, step):
        return self.ops_ref[x * self.size_y + y, step * 2 * HALF : (step + 1) * 2 * HALF, :]

    def mass(self, x, y):
        return self.step(x, y, STEPS)

    def half(self, total, place, z, parity):
        return total[(*place, parity, pl.ds(z, HALF, stride=2), slice(None))]


class Coarse:
    def __init__(self, ops_ref, size_y):
        self.ops_ref, self.size_y = ops_ref, size_y

    def kind(self):
        return lax.broadcasted_iota(jnp.int32, (2 * HALF, LANES), 0) // HALF

    def step(self, x, y, step):
        count, each = self.ops_ref.shape[1], self.ops_ref.shape[2] // self.size_y
        x = jnp.asarray(x, jnp.int32)
        group = lax.bitwise_xor(x // each, lax.axis_index("lateral"))
        span = slice(step * HALF, (step + 1) * HALF)
        rows = [
            self.ops_ref[lax.bitwise_xor(lax.axis_index("depth"), z), group, x % each * self.size_y + y, span, :] for z in range(2)
        ]
        return jnp.concatenate(rows, axis=0)

    def smoother(self, x, y):
        return self.step(x, y, STEPS)[:, :LANES]

    def mass(self, x, y):
        return mask_layers(self.step(x, y, STEPS)[:, LANES:], self.kind())

    def half(self, total, place, z, parity):
        return total[(*place, parity, pl.ds(z * HALF, HALF), slice(None))]


def rows_of(grid, ops_ref, size_y):
    return Coarse(ops_ref, size_y) if grid is Coarse else Fine(ops_ref, size_y)


def both_layers(cells):
    return jnp.concatenate([two_sided(cells[0]), two_sided(cells[1])], axis=0)


def add_from(total_ref, rows, cells, targets, own=None):
    left = [rows.step(*target) for target in targets]
    if own is not None:
        left.append(rows.mass(*own))
    given = jnp.dot(jnp.concatenate(left, axis=0), both_layers(cells), preferred_element_type=F32)
    parts = [given[index * 2 * HALF : (index + 1) * 2 * HALF] for index in range(len(left))]
    for (x, y, _), part in zip(targets, parts):
        if own is not None and own[0] is x and own[1] == y:
            part = part + parts[-1]
        for parity in range(2):
            total_ref[x, y, parity] += part[:, parity * LANES : (parity + 1) * LANES]


def natural(rows, total, place, scratch):
    blocks = []
    for z in range(2):
        for parity in range(2):
            scratch[z, pl.ds(parity, HALF, stride=2), :] = rows.half(total, place, z, parity)
        blocks.append(scratch[z])
    return blocks


def smoothed(rows, left, cells, total, place, scratch):
    given = jnp.dot(left, both_layers([cell.astype(BF16) for cell in cells]), preferred_element_type=F32)
    for parity in range(2):
        total[(*place, parity)] = given[:, parity * LANES : (parity + 1) * LANES]
    return natural(rows, total, place, scratch)


def over_columns(size_x, column):
    column(0, (-1, 0))
    lax.fori_loop(1, size_x - 1, lambda x, c: (column(x, (-1, 0, 1)), c)[1], 0)
    column(size_x - 1, (0, 1))


def inner_kernel(cells_ref, ops_ref, total_ref, *, grid):
    size_x, size_y = cells_ref.shape[:2]
    rows = rows_of(grid, ops_ref, size_y)
    total_ref[...] = jnp.zeros_like(total_ref)

    def column(x, shifts):
        for near in range(size_y):
            targets = []
            for shift in shifts:
                own = x - shift if shift else x
                targets += [(own, y, (shift + 1) * 3 + near - y + 1) for y in range(size_y)]
            add_from(total_ref, rows, cells_ref[x, near], targets, (x, near))

    over_columns(size_x, column)


def beside_kernel(one_ref, two_ref, ops_ref, given_ref, total_ref, *, grid):
    size_x, size_y = total_ref.shape[:2]
    rows = rows_of(grid, ops_ref, size_y)
    total_ref[...] = given_ref[...]

    def side(ref, y, step):
        def column(x, shifts):
            add_from(total_ref, rows, ref[x], [(x - shift, y, (shift + 1) * 3 + step) for shift in shifts])

        over_columns(size_x, column)

    for odd, low_ref, high_ref in ((0, one_ref, two_ref), (1, two_ref, one_ref)):
        pl.when((lax.axis_index("depth") == odd) & (lax.axis_index("lateral") > 0))(functools.partial(side, low_ref, 0, 0))
        pl.when((lax.axis_index("depth") == odd) & (lax.axis_index("lateral") < lax.axis_size("lateral") - 1))(functools.partial(side, high_ref, size_y - 1, 2))


def give_faces(cells, one_ref, two_ref, x):
    even = lax.axis_index("depth") % 2 == 0
    for z in range(2):
        low, high = (cells[0][z], cells[-1][z]) if isinstance(cells, list) else (cells[0, z], cells[cells.shape[0] - 1, z])
        one_ref[x, z] = jnp.where(even, high, low)
        two_ref[x, z] = jnp.where(even, low, high)


def round_kernel(start_ref, round_ref, one_ref, two_ref):
    for x in range(start_ref.shape[0]):
        cells = [[start_ref[x, y, z].astype(BF16) for z in range(2)] for y in range(start_ref.shape[1])]
        for y, column in enumerate(cells):
            for z in range(2):
                round_ref[x, y, z] = column[z]
        give_faces(cells, one_ref, two_ref, x)


def round_start(start):
    size_x, size_y, layers, width, loads = start.shape
    batch = size_x // 4
    side = pl.BlockSpec((batch, layers, width, loads), lambda i: (i, 0, 0, 0))
    whole = pl.BlockSpec((batch, size_y, layers, width, loads), lambda i: (i, 0, 0, 0, 0))
    face = jax.ShapeDtypeStruct((size_x, layers, width, loads), BF16)
    return pl.pallas_call(
        round_kernel,
        grid=(4,),
        in_specs=[whole],
        out_specs=[whole, side, side],
        out_shape=[jax.ShapeDtypeStruct(start.shape, BF16), face, face],
        compiler_params=pltpu.CompilerParams(vmem_limit_bytes=LIMIT),
        name="round_start",
    )(in_hbm(start))


def add_ends(before_ref, after_ref, rows, total):
    size_x, size_y = total.shape[:2]
    for near in range(-1, size_y + 1):
        ys = [y for y in range(size_y) if abs(near - y) <= 1]
        place = near + 1
        if near in (-1, size_y):
            odd = lax.axis_index("depth") % 2
            place = odd * (size_y + 1) if near < 0 else (1 - odd) * (size_y + 1)
        inside = True
        if near < 0:
            inside = lax.axis_index("lateral") > 0
        if near == size_y:
            inside = lax.axis_index("lateral") < lax.axis_size("lateral") - 1
        before, after = before_ref[place], after_ref[place]
        before = jnp.where((lax.axis_index("track") > 0) & inside, before, jnp.zeros_like(before))
        after = jnp.where((lax.axis_index("track") < lax.axis_size("track") - 1) & inside, after, jnp.zeros_like(after))
        add_from(total, rows, before, [(0, y, near - y + 1) for y in ys])
        add_from(total, rows, after, [(size_x - 1, y, 6 + near - y + 1) for y in ys])


def per_column(size_x, size_y, body, after=None):
    def step(x, carry):
        for y in range(size_y):
            body(x, y)
        if after is not None:
            after(x)
        return carry

    lax.fori_loop(0, size_x, step, 0)


def smooth_kernel(
    before_ref, after_ref, ops_ref, smoother_ref, given_ref, rhs_ref, old_ref, new_ref, round_ref, one_ref, two_ref,
    total, scratch,
):
    size_x, size_y = total.shape[:2]
    rows = Fine(ops_ref, size_y)
    total[...] = given_ref[...]
    add_ends(before_ref, after_ref, rows, total)

    def body(x, y):
        applied = natural(rows, total, (x, y), scratch.at[0, y])
        residual = [rhs_ref[x, y, z] - applied[z] for z in range(2)]
        left = mask_layers(smoother_ref[x * size_y + y], rows.kind())
        change = smoothed(rows, left, residual, total, (x, y), scratch.at[1, y])
        for z in range(2):
            value = old_ref[x, y, z] + DAMPING * change[z]
            new_ref[x, y, z] = value
            round_ref[x, y, z] = value.astype(BF16)

    per_column(size_x, size_y, body, lambda x: give_faces(round_ref.at[x], one_ref, two_ref, x))


def restrict_kernel(
    group_ref, before_ref, after_ref, ops_ref, transfer_ref, given_ref, rhs_ref, *refs, layers_at, groups_at
):
    pieces = refs[:-9]
    coarse_ref, first_ref, round_ref, one_ref, two_ref, coarse_ops_ref, total, scratch, arrived = refs[-9:]
    copies, filled = [], {}
    for index, (layer, group, piece) in enumerate(zip(layers_at, groups_at, pieces)):
        begin = filled.get((layer, group), 0)
        filled[layer, group] = begin + piece.shape[0]
        target = coarse_ops_ref.at[layer, group, pl.ds(begin, piece.shape[0])]
        copies.append(pltpu.make_async_copy(piece, target, arrived.at[index]))
        copies[-1].start()
    size_x, size_y = total.shape[:2]
    coarse_y = coarse_ref.shape[1]
    rows = Fine(ops_ref, size_y)
    total[...] = given_ref[...]
    coarse_ref[...] = jnp.zeros_like(coarse_ref)
    add_ends(before_ref, after_ref, rows, total)

    def body(x, y):
        applied = natural(rows, total, (x, y), scratch.at[0, y])
        for z in range(2):
            scratch[1, y, z] = rhs_ref[x, y, z] - applied[z]
            for parity in range(2):
                total[x, y, parity, pl.ds(z, HALF, stride=2), :] = scratch[1, y, z, pl.ds(parity, HALF, stride=2), :]
        left = mask_layers(transfer_ref[x * size_y + y], rows.kind())
        right = jnp.concatenate([total[x, y, 0], total[x, y, 1]], axis=1).astype(BF16)
        both = lax.dot_general(left, right, (((0,), (0,)), ((), ())), preferred_element_type=F32)
        for z in range(2):
            target = group_ref[y, z, x] - lax.axis_index("track") * size_x
            own = both[z * LANES : (z + 1) * LANES]
            coarse_ref[target, y // 2, z] += own[:64, :LANES] + own[64:, LANES:]

    per_column(size_x, size_y, body)
    for copy in copies:
        copy.wait()
    coarse_rows = Coarse(coarse_ops_ref, coarse_y)

    def first(x, y):
        left = mask_layers(coarse_rows.smoother(x, y), coarse_rows.kind())
        cells = [coarse_ref[x, y, z] for z in range(2)]
        change = smoothed(coarse_rows, left, cells, total, (x, y), scratch.at[0, y])
        for z in range(2):
            value = DAMPING * change[z]
            first_ref[x, y, z] = value
            round_ref[x, y, z] = value.astype(BF16)

    per_column(size_x, coarse_y, first, lambda x: give_faces(round_ref.at[x], one_ref, two_ref, x))


def correct_kernel(
    group_ref, before_ref, after_ref, coarse_ops_ref, given_ref, coarse_ref, first_ref, transfer_ref,
    iterate_ref, out_ref, total, correction, scratch,
):
    size_x, coarse_y = total.shape[:2]
    size_y = out_ref.shape[1]
    coarse_rows = Coarse(coarse_ops_ref, coarse_y)
    total[...] = given_ref[...]
    add_ends(before_ref, after_ref, coarse_rows, total)

    def second(x, y):
        applied = natural(coarse_rows, total, (x, y), scratch.at[0, y])
        remain = [coarse_ref[x, y, z] - applied[z] for z in range(2)]
        left = mask_layers(coarse_rows.smoother(x, y), coarse_rows.kind())
        change = smoothed(coarse_rows, left, remain, total, (x, y), scratch.at[1, y])
        for z in range(2):
            correction[x, y, z] = (first_ref[x, y, z] + DAMPING * change[z]).astype(BF16)

    per_column(size_x, coarse_y, second)
    rows = Fine(None, size_y)

    def added(x, y):
        sources = [group_ref[y, z, x] - lax.axis_index("track") * size_x for z in range(2)]
        cells = [correction[sources[z], y // 2, z] for z in range(2)]
        left = mask_layers(transfer_ref[x * size_y + y], rows.kind())
        change = smoothed(rows, left, cells, total, (x, 0), scratch.at[0, y])
        for z in range(2):
            out_ref[x, y, z] = iterate_ref[x, y, z] + change[z]

    per_column(size_x, size_y, added)


SMEM = pl.BlockSpec(memory_space=pltpu.SMEM)
VMEM = pl.BlockSpec(memory_space=pltpu.VMEM)


def call(kernel, name, scalars, operands, out_shape, scratch=(), outside=()):
    operands = list(operands) + [in_hbm(array) for array in outside]
    inside = len(operands) - len(outside)
    return pl.pallas_call(
        kernel,
        in_specs=[SMEM] * len(scalars) + [VMEM] * inside + [pl.BlockSpec(memory_space=pltpu.HBM)] * len(outside),
        out_specs=jax.tree.map(lambda _: VMEM, out_shape),
        out_shape=out_shape,
        scratch_shapes=list(scratch),
        compiler_params=pltpu.CompilerParams(vmem_limit_bytes=LIMIT),
        name=name,
    )(*scalars, *operands)


def swap_sides(one, two):
    lateral, depth = lax.axis_size("lateral"), lax.axis_size("depth")
    ring = [i * depth for i in range(lateral)] + [i * depth + 1 for i in reversed(range(lateral))]
    onward = list(zip(ring, ring[1:] + ring[:1]))
    back = [(b, a) for a, b in onward]
    return lax.ppermute(one, ("lateral", "depth"), onward), lax.ppermute(two, ("lateral", "depth"), back)


def swap_ends(cells, one, two):
    count = lax.axis_size("track")
    first = jnp.concatenate([one[:1], cells[0], two[:1]], axis=0)
    last = jnp.concatenate([one[-1:], cells[-1], two[-1:]], axis=0)
    before = lax.ppermute(last, "track", [(i, (i + 1) % count) for i in range(count)])
    after = lax.ppermute(first, "track", [((i + 1) % count, i) for i in range(count)])
    return before, after


def send_coarse(piece, step):
    count = lax.axis_size("lateral")
    return lax.ppermute(piece, "lateral", [(i, i ^ step) for i in range(count)])


def swap_layer(piece):
    return lax.ppermute(piece, "depth", [(0, 1), (1, 0)])


def per_device(
    rhs,
    start,
    fine_blocks,
    fine_cols,
    fine_mass,
    fine_smoother,
    transfer,
    aggregate,
    coarse_blocks,
    coarse_cols,
    coarse_mass,
    coarse_smoother,
):
    size_x, size_y, size_z, width, loads = rhs.shape
    count = lax.axis_size("lateral")
    groups = in_hbm(aggregate.transpose(1, 2, 0))
    part_x = coarse_blocks.shape[0]
    coarse_y = size_y // 2

    paired = lambda a: a.reshape(size_x, size_y, size_z, HALF, LANES).transpose(0, 1, 3, 2, 4).reshape(-1, 2 * HALF, LANES)
    smoothers, transfers = paired(fine_smoother), paired(transfer)
    field = (size_x, size_y, size_z, width, loads)
    coarse_field = (size_x, coarse_y, size_z, width, loads)
    sums = lambda shape: shape[:2] + (2, 2 * HALF, LANES)
    full = jax.ShapeDtypeStruct
    scratch = [pltpu.VMEM((2, size_y, 2, width, loads), F32)]

    def outer(cells, ops, grid, one, two, *others):
        shape = full(sums(cells.shape), F32)
        inner = call(functools.partial(inner_kernel, grid=grid), "inner", [], [cells, ops], shape)
        inner, one, two, *others = lax.optimization_barrier((inner, one, two, *others))
        before, after = swap_ends(cells, one, two)
        beside = call(functools.partial(beside_kernel, grid=grid), "beside", [], [one, two, ops, inner], shape)
        return before, after, beside, *others

    face = full((size_x, size_z, width, loads), BF16)
    rounded, one, two = round_start(start)
    iterate = start
    coarse_cols, one, two = lax.optimization_barrier((coarse_cols, one, two))
    one, two = swap_sides(one, two)
    pieces = sort_coarse(coarse_blocks, coarse_cols, coarse_mass, coarse_smoother, count)
    fine_cols, *pieces = lax.optimization_barrier((fine_cols, *pieces))
    groups_at = list(range(count))
    middle = count // 2 + 1
    early, late = pieces[:middle], pieces[middle:]
    late_at = groups_at[middle:]
    split = pieces[0].shape[0] // 2
    if split:
        early += [piece[:split] for piece in late]
        late = [piece[split:] for piece in late]
        groups_at = groups_at + late_at
    early = [send_coarse(piece, groups_at[index]) if index else piece for index, piece in enumerate(early)]
    fine_ops = sort_fine(fine_blocks, fine_cols, fine_mass)
    fine_total = [pltpu.VMEM(sums(field), F32)] + scratch
    for sweep in range(SWEEPS):
        last = sweep == SWEEPS - 1
        if last:
            before, after, beside, *held = outer(rounded, fine_ops, Fine, one, two, *late, *early_other)
            late, early_other = held[: len(late)], held[len(late) :]
            late = [send_coarse(piece, group) for piece, group in zip(late, late_at)]
        else:
            before, after, beside = outer(rounded, fine_ops, Fine, one, two)
        iterate, rounded, one, two = call(
            smooth_kernel, "smooth", [], [before, after, fine_ops, smoothers, beside, rhs, iterate],
            [full(field, F32), full(field, BF16), face, face], fine_total,
        )
        if last:
            one, *late = lax.optimization_barrier((one, *late))
        else:
            one, *early = lax.optimization_barrier((one, *early))
            early_other = [swap_layer(piece) for piece in early]
        one, two = swap_sides(one, two)
    before, after, beside, *late = outer(rounded, fine_ops, Fine, one, two, *late)
    pieces = early + late + early_other + [swap_layer(piece) for piece in late]
    layers_at = [0] * len(groups_at) + [1] * len(groups_at)
    coarse_rows = full((2, count, part_x * coarse_y, (STEPS + 1) * HALF, WIDE), BF16)
    coarse_res, first, rounded, one, two, coarse_ops = call(
        functools.partial(restrict_kernel, layers_at=layers_at, groups_at=groups_at * 2),
        "restrict", [groups], [before, after, fine_ops, transfers, beside, rhs],
        [full(coarse_field, F32), full(coarse_field, F32), full(coarse_field, BF16), face, face, coarse_rows],
        fine_total + [pltpu.SemaphoreType.DMA((len(pieces),))], pieces,
    )
    one, two = swap_sides(one, two)
    before, after, beside = outer(rounded, coarse_ops, Coarse, one, two)
    return call(
        correct_kernel, "correct", [groups],
        [before, after, coarse_ops, beside, coarse_res, first, transfers, iterate],
        full(field, F32),
        [pltpu.VMEM(sums(coarse_field), F32), pltpu.VMEM(coarse_field, BF16)] + scratch,
    )


def solution(mesh):
    in_specs = (
        P("track", "lateral", None, None, "depth"),
        P("track", "lateral", None, None, "depth"),
        P("track", "lateral", None, None, None),
        P("track", "lateral", None, None),
        P("track", "lateral", None, None),
        P("track", "lateral", None, None),
        P("track", "lateral", None, None),
        P("track", "lateral", None),
        P(("track", "lateral"), None, "depth", None, None),
        P(("track", "lateral"), None, "depth", None),
        P(("track", "lateral"), None, "depth", None),
        P(("track", "lateral"), None, "depth", None),
    )
    out_specs = P("track", "lateral", None, None, "depth")
    return jax.shard_map(
        per_device, mesh=mesh, in_specs=in_specs, out_specs=out_specs, check_vma=False
    )
```

```python
import functools

import jax
import jax.numpy as jnp
from jax import lax
from jax.experimental import pallas as pl
from jax.experimental.pallas import tpu as pltpu
from jax.sharding import PartitionSpec as P

SWEEPS = 2
DAMPING = 0.8
HALF = 32
LANES = 128
WIDE = 256
STEPS = 9
BF16 = jnp.bfloat16
F32 = jnp.float32
LIMIT = 8 * 1024 * 1024


def listed_at(cols_ref, slots, index, groups):
    for group in range(groups):
        codes = [cols_ref[index * groups + group, slot] for slot in range(27)]
        for slot, code in enumerate(codes):
            slots[group, code] = slot


def diagonal(mass, rows, groups):
    row = lax.broadcasted_iota(jnp.int32, (rows, LANES), 0)
    lane = lax.broadcasted_iota(jnp.int32, (rows, LANES), 1)
    spread = jnp.zeros((rows, LANES), F32)
    for group in range(groups):
        spread = jnp.where(row % groups == group, mass[group : group + 1], spread)
    return jnp.where(lane % 64 == 2 * (row // groups) + lane // 64, spread, 0.0)


def fine_sort_kernel(cols_ref, mass_ref, blocks_ref, out_ref, slots, held, arrived):
    second = lax.broadcasted_iota(jnp.int32, (2 * HALF, LANES), 0) % 2 == 1
    columns, parts = out_ref.shape[0], arrived.shape[0]
    each = columns // parts
    copies = [
        pltpu.make_async_copy(blocks_ref.at[pl.ds(part * each, each)], held.at[pl.ds(part * each, each)], arrived.at[part])
        for part in range(parts)
    ]
    for copy in copies:
        copy.start()
    for index in range(columns):
        listed_at(cols_ref, slots.at[index], index, 2)
    for index in range(columns):
        if index % each == 0:
            copies[index // each].wait()
        for step in range(STEPS):
            for side in range(2):
                upper = held[index, slots[index, 0, 3 * step + side + 1]]
                lower = held[index, slots[index, 1, 3 * step + side]]
                span = slice(side * LANES, (side + 1) * LANES)
                out_ref[index, step * 2 * HALF : (step + 1) * 2 * HALF, span] = jnp.where(second, lower, upper)
        mass = mass_ref[index].astype(F32)
        mass = diagonal(jnp.concatenate([mass, mass], axis=1), 2 * HALF, 2)
        for side in range(2):
            span = slice(side * LANES, (side + 1) * LANES)
            out_ref[index, STEPS * 2 * HALF :, span] = jnp.where(second == (side == 1), mass, 0.0).astype(BF16)


def coarse_sort_kernel(cols_ref, mass_ref, smoother_ref, blocks_ref, out_ref, slots, scratch):
    groups = blocks_ref.shape[2] // HALF
    rows = groups * HALF
    kind = lax.broadcasted_iota(jnp.int32, (rows, LANES), 0) % groups

    def hand_out(values, first, span):
        scratch[...] = values
        for y in range(groups):
            out_ref[y, first : first + HALF, span] = scratch[pl.ds(y, HALF, stride=groups), :].astype(BF16)

    listed_at(cols_ref, slots, pl.program_id(0), groups)
    for step in range(STEPS):
        for side in range(2):
            code = 3 * step + side + 1 - lax.axis_index("depth")
            values = blocks_ref[0, slots[0, code]]
            for group in range(1, groups):
                values = jnp.where(kind == group, blocks_ref[0, slots[group, code]], values)
            hand_out(values.astype(F32), step * HALF, slice(side * LANES, (side + 1) * LANES))
    hand_out(smoother_ref[0].astype(F32), STEPS * HALF, slice(0, LANES))
    mass = mass_ref[0].astype(F32)
    mass = diagonal(jnp.concatenate([mass, mass], axis=1), rows, groups)
    hand_out(mass, STEPS * HALF, slice(LANES, WIDE))


def in_hbm(array):
    return pltpu.with_memory_space_constraint(array, pltpu.HBM)


def sort_fine(blocks, cols, mass):
    size_x, size_y, layers = blocks.shape[:3]
    columns = size_x * size_y
    paired = blocks.reshape(size_x, size_y, layers, 27, HALF, LANES).transpose(0, 1, 3, 4, 2, 5)
    rows = (STEPS + 1) * 2 * HALF
    shape = (columns, 27, layers * HALF, LANES)
    return pl.pallas_call(
        fine_sort_kernel,
        in_specs=[SMEM, VMEM, pl.BlockSpec(memory_space=pltpu.HBM)],
        out_specs=VMEM,
        out_shape=jax.ShapeDtypeStruct((columns, rows, WIDE), BF16),
        scratch_shapes=[
            pltpu.SMEM((columns, 2, 27), jnp.int32), pltpu.VMEM(shape, BF16), pltpu.SemaphoreType.DMA((columns // 2,)),
        ],
        compiler_params=pltpu.CompilerParams(vmem_limit_bytes=2 * LIMIT),
        name="sort_fine",
    )(in_hbm(cols.reshape(columns * layers, 27)), in_hbm(mass.reshape(columns, layers, 64)), in_hbm(paired.reshape(shape)))


def sort_coarse(blocks, cols, mass, smoother):
    size_x, size_y = blocks.shape[:2]
    paired = blocks.reshape(size_x, size_y, 27, HALF, LANES).transpose(0, 2, 3, 1, 4)
    smoothers = smoother.reshape(size_x, size_y, HALF, LANES).transpose(0, 2, 1, 3)
    rows = (STEPS + 1) * HALF
    return pl.pallas_call(
        coarse_sort_kernel,
        grid=(size_x,),
        in_specs=[
            SMEM,
            pl.BlockSpec((1, size_y, 64), lambda i: (i, 0, 0)),
            pl.BlockSpec((1, size_y * HALF, LANES), lambda i: (i, 0, 0)),
            pl.BlockSpec((1, 27, size_y * HALF, LANES), lambda i: (i, 0, 0, 0)),
        ],
        out_specs=pl.BlockSpec((size_y, rows, WIDE), lambda i: (i, 0, 0)),
        out_shape=jax.ShapeDtypeStruct((size_x * size_y, rows, WIDE), BF16),
        scratch_shapes=[pltpu.SMEM((size_y, 27), jnp.int32), pltpu.VMEM((size_y * HALF, LANES), F32)],
        compiler_params=pltpu.CompilerParams(vmem_limit_bytes=LIMIT),
        name="sort_coarse",
    )(
        in_hbm(cols.reshape(size_x * size_y, 27)),
        in_hbm(mass.reshape(size_x, size_y, 64)),
        in_hbm(smoothers.reshape(size_x, size_y * HALF, LANES)),
        in_hbm(paired.reshape(size_x, 27, size_y * HALF, LANES)),
    )


def two_sided(block):
    none = jnp.zeros_like(block)
    return jnp.concatenate(
        [jnp.concatenate([block, none], axis=1), jnp.concatenate([none, block], axis=1)], axis=0
    )


def mask_layers(block, kind):
    none = jnp.zeros_like(block)
    return jnp.concatenate([jnp.where(kind == 0, block, none), jnp.where(kind == 1, block, none)], axis=1)


class Fine:
    def __init__(self, ops_ref, size_y):
        self.ops_ref, self.size_y = ops_ref, size_y

    def kind(self):
        return lax.broadcasted_iota(jnp.int32, (2 * HALF, LANES), 0) % 2

    def step(self, x, y, step):
        return self.ops_ref[x * self.size_y + y, step * 2 * HALF : (step + 1) * 2 * HALF, :]

    def mass(self, x, y):
        return self.step(x, y, STEPS)

    def half(self, total, place, z, parity):
        return total[(*place, parity, pl.ds(z, HALF, stride=2), slice(None))]


class Coarse:
    def __init__(self, own_ref, other_ref, size_y):
        self.own_ref, self.other_ref, self.size_y = own_ref, other_ref, size_y

    def kind(self):
        row = lax.broadcasted_iota(jnp.int32, (2 * HALF, LANES), 0)
        return lax.bitwise_xor(row // HALF, lax.axis_index("depth"))

    def step(self, x, y, step):
        place, span = x * self.size_y + y, slice(step * HALF, (step + 1) * HALF)
        return jnp.concatenate([self.own_ref[place, span, :], self.other_ref[place, span, :]], axis=0)

    def smoother(self, x, y):
        return self.step(x, y, STEPS)[:, :LANES]

    def mass(self, x, y):
        return mask_layers(self.step(x, y, STEPS)[:, LANES:], self.kind())

    def half(self, total, place, z, parity):
        first = pl.multiple_of(lax.bitwise_xor(jnp.int32(z), lax.axis_index("depth")) * HALF, HALF)
        return total[(*place, parity, pl.ds(first, HALF), slice(None))]


def both_layers(cells):
    return jnp.concatenate([two_sided(cells[0]), two_sided(cells[1])], axis=0)


def tip(ref, end):
    return ref.at[end * (ref.shape[0] - 1)]


def add_from(total_ref, rows, cells, targets, slot=lambda x: x):
    left = [rows.step(*target) for target in targets]
    given = jnp.dot(jnp.concatenate(left, axis=0), both_layers(cells), preferred_element_type=F32)
    parts = [given[index * 2 * HALF : (index + 1) * 2 * HALF] for index in range(len(left))]
    for (x, y, _), part in zip(targets, parts):
        for parity in range(2):
            total_ref[slot(x), y, parity] += part[:, parity * LANES : (parity + 1) * LANES]


def natural(rows, total, places, scratches):
    for place, scratch in zip(places, scratches):
        for z in range(2):
            for parity in range(2):
                scratch[z, pl.ds(parity, HALF, stride=2), :] = rows.half(total, place, z, parity)
    return [[scratch[z] for z in range(2)] for scratch in scratches]


def smoothed(rows, lefts, columns, total, places, scratches):
    given = [
        jnp.dot(left, both_layers([cell.astype(BF16) for cell in cells]), preferred_element_type=F32)
        for left, cells in zip(lefts, columns)
    ]
    for part, place in zip(given, places):
        for parity in range(2):
            total[(*place, parity)] = part[:, parity * LANES : (parity + 1) * LANES]
    return natural(rows, total, places, scratches)


def over_columns(size_x, column):
    if size_x == 1:
        column(0, (0,))
        return
    column(0, (-1, 0))
    for x in range(1, size_x - 1):
        column(x, (-1, 0, 1))
    column(size_x - 1, (0, 1))


def inner_kernel(cells_ref, ends_ref, *refs, grid):
    *ops, total_ref = refs
    size_x, size_y = cells_ref.shape[:2]
    rows = grid(*ops, size_y)
    total_ref[...] = jnp.zeros_like(total_ref)

    def column(x, shifts):
        row = tip(ends_ref, min(x, 1)) if x in (0, size_x - 1) else cells_ref.at[x]
        sums = {}
        for near in range(size_y):
            targets = [(shift, y) for shift in shifts for y in range(size_y) if abs(near - y) <= 1]
            left = [rows.step(x - shift, y, (shift + 1) * 3 + near - y + 1) for shift, y in targets]
            left.append(rows.mass(x, near))
            given = jnp.dot(jnp.concatenate(left, axis=0), both_layers(row[near]), preferred_element_type=F32)
            for index, target in enumerate(targets + [(0, near)]):
                part = given[index * 2 * HALF : (index + 1) * 2 * HALF]
                sums[target] = sums[target] + part if target in sums else part
        for (shift, y), part in sums.items():
            for parity in range(2):
                total_ref[x - shift, y, parity] += part[:, parity * LANES : (parity + 1) * LANES]

    over_columns(size_x, column)


def inside_track(cells, low):
    at = lax.axis_index("lateral")
    inside = at > 0 if low else at < lax.axis_size("lateral") - 1
    return jnp.where(inside, cells, jnp.zeros_like(cells))


def add_sides(one_ref, two_ref, rows, total):
    size_x, size_y = total.shape[:2]

    def both(low_ref, high_ref):
        def column(x, shifts):
            for cells, y, step in (
                (inside_track(low_ref[x], True), 0, 0),
                (inside_track(high_ref[x], False), size_y - 1, 2),
            ):
                add_from(total, rows, cells, [(x - shift, y, (shift + 1) * 3 + step) for shift in shifts])

        over_columns(size_x, column)

    odd = lax.axis_index("depth") % 2
    pl.when(odd == 0)(lambda: both(one_ref, two_ref))
    pl.when(odd == 1)(lambda: both(two_ref, one_ref))


def give_faces(low, high, one_ref, two_ref, x):
    even = lax.axis_index("depth") % 2 == 0
    for z in range(2):
        one_ref[x, z] = jnp.where(even, high[z], low[z])
        two_ref[x, z] = jnp.where(even, low[z], high[z])


def give_all_faces(cells_ref, ends_ref, one_ref, two_ref):
    size_x, size_y = cells_ref.shape[:2]

    for x in range(1, size_x - 1):
        give_faces(cells_ref.at[x, 0], cells_ref.at[x, size_y - 1], one_ref, two_ref, x)
    for end in range(2):
        ends = tip(ends_ref, end)
        give_faces(ends.at[0], ends.at[size_y - 1], one_ref, two_ref, end * (size_x - 1))


def round_kernel(start_ref, round_ref, one_ref, two_ref):
    for x in range(start_ref.shape[0]):
        cells = [[start_ref[x, y, z].astype(BF16) for z in range(2)] for y in range(start_ref.shape[1])]
        for y, column in enumerate(cells):
            for z in range(2):
                round_ref[x, y, z] = column[z]
        give_faces(cells[0], cells[-1], one_ref, two_ref, x)


def round_start(start):
    size_x, size_y, layers, width, loads = start.shape
    batch = size_x // 4
    side = pl.BlockSpec((batch, layers, width, loads), lambda i: (i, 0, 0, 0))
    whole = pl.BlockSpec((batch, size_y, layers, width, loads), lambda i: (i, 0, 0, 0, 0))
    face = jax.ShapeDtypeStruct((size_x, layers, width, loads), BF16)
    return pl.pallas_call(
        round_kernel,
        grid=(4,),
        in_specs=[whole],
        out_specs=[whole, side, side],
        out_shape=[jax.ShapeDtypeStruct(start.shape, BF16), face, face],
        compiler_params=pltpu.CompilerParams(vmem_limit_bytes=LIMIT),
        name="round_start",
    )(in_hbm(start))


def add_ends(given_refs, rows, total, size_x):
    size_y = total.shape[1]
    odd = lax.axis_index("depth") % 2
    at, count = lax.axis_index("track"), lax.axis_size("track")
    for near in range(-1, size_y + 1):
        ys = [y for y in range(size_y) if abs(near - y) <= 1]
        corner = near in (-1, size_y)
        place = (odd if near < 0 else 1 - odd) if corner else near
        for end, inside in ((0, at > 0), (1, at < count - 1)):
            cells = given_refs[2 * corner + end][place]
            cells = jnp.where(inside, cells, jnp.zeros_like(cells))
            if corner:
                cells = inside_track(cells, near < 0)
            targets = [(end * (size_x - 1), y, 6 * end + near - y + 1) for y in ys]
            add_from(total, rows, cells, targets, slot=lambda x, end=end: end)


def add_coarse_ends(before_ref, after_ref, rows, total):
    size_x, size_y = total.shape[:2]
    at = lax.axis_index(("track", "lateral"))
    count = lax.axis_size(("track", "lateral"))
    for near in range(size_y):
        ys = [y for y in range(size_y) if abs(near - y) <= 1]
        for end, ref, inside in ((0, before_ref, at > 0), (1, after_ref, at < count - 1)):
            cells = ref[near]
            cells = jnp.where(inside, cells, jnp.zeros_like(cells))
            add_from(total, rows, cells, [(end * (size_x - 1), y, 6 * end + near - y + 1) for y in ys])


def over_inside(size_x, body):
    for x in range(1, size_x - 1):
        body(x)


def smooth_columns(rows, total, places, smoothers, rhs, old, scratch):
    first = [scratch.at[index, 0] for index in range(len(places))]
    second = [scratch.at[index, 1] for index in range(len(places))]
    applied = natural(rows, total, places, first)
    residuals = [[ref[z] - part[z] for z in range(2)] for ref, part in zip(rhs, applied)]
    lefts = [mask_layers(smoother, rows.kind()) for smoother in smoothers]
    changes = smoothed(rows, lefts, residuals, total, places, second)
    return [[ref[z] + DAMPING * part[z] for z in range(2)] for ref, part in zip(old, changes)]


def keep_ends(total, end_total_ref):
    for end in range(2):
        end_total_ref[end] = tip(total, end)[...]


def smooth_inside_kernel(
    one_ref, two_ref, ops_ref, smoother_ref, given_ref, rhs_ref, old_ref, end_total_ref, new_ref, round_ref, total, scratch
):
    size_x, size_y = total.shape[:2]
    rows = Fine(ops_ref, size_y)
    total[...] = given_ref[...]
    add_sides(one_ref, two_ref, rows, total)
    keep_ends(total, end_total_ref)

    def body(x):
        ys = range(size_y)
        values = smooth_columns(
            rows, total, [(x, y) for y in ys], [smoother_ref[x * size_y + y] for y in ys],
            [rhs_ref.at[x, y] for y in ys], [old_ref.at[x, y] for y in ys], scratch,
        )
        for y in ys:
            for z in range(2):
                new_ref[x, y, z] = values[y][z]
                round_ref[x, y, z] = values[y][z].astype(BF16)

    over_inside(size_x, body)


def smooth_ends_kernel(
    before_ref, after_ref, corner_before_ref, corner_after_ref, ops_ref, smoother_ref, given_ref, rhs_ref, old_ref, cells_ref,
    new_ref, round_ref, one_ref, two_ref, total, scratch,
):
    size_x, size_y = cells_ref.shape[:2]
    rows = Fine(ops_ref, size_y)
    total[...] = given_ref[...]
    add_ends([before_ref, after_ref, corner_before_ref, corner_after_ref], rows, total, size_x)

    places = [(end, y) for end in range(2) for y in range(size_y)]
    row = lambda end: end * (size_x - 1)
    values = smooth_columns(
        rows, total, places, [smoother_ref[row(end) * size_y + y] for end, y in places],
        [rhs_ref.at[row(end), y] for end, y in places], [tip(old_ref, end).at[y] for end, y in places], scratch,
    )
    for (end, y), value in zip(places, values):
        for z in range(2):
            new_ref[end, y, z] = value[z]
            round_ref[end, y, z] = value[z].astype(BF16)
    give_all_faces(cells_ref, round_ref, one_ref, two_ref)


def restrict_columns(rows, total, places, transfers, rhs, group_ref, xs, coarse_ref, scratch):
    size_x = coarse_ref.shape[0]
    first = [scratch.at[index, 0] for index in range(len(places))]
    applied = natural(rows, total, places, first)
    for index, place in enumerate(places):
        for z in range(2):
            scratch[index, 1, z] = rhs[index][z] - applied[index][z]
    for index, place in enumerate(places):
        for z in range(2):
            for parity in range(2):
                taken = scratch[index, 1, z, pl.ds(parity, HALF, stride=2), :]
                total[(*place, parity, pl.ds(z, HALF, stride=2), slice(None))] = taken
    given = []
    for place, transfer in zip(places, transfers):
        left = mask_layers(transfer, rows.kind())
        right = jnp.concatenate([total[(*place, 0)], total[(*place, 1)]], axis=1).astype(BF16)
        given.append(lax.dot_general(left, right, (((0,), (0,)), ((), ())), preferred_element_type=F32))
    for (_, y), x, both in zip(places, xs, given):
        for z in range(2):
            target = group_ref[y, z, x] - lax.axis_index("track") * size_x
            own = both[z * LANES : (z + 1) * LANES]
            coarse_ref[target, y // 2, z] += own[:64, :LANES] + own[64:, LANES:]


def restrict_inside_kernel(
    group_ref, one_ref, two_ref, ops_ref, transfer_ref, given_ref, rhs_ref, end_total_ref, coarse_ref, total, scratch
):
    size_x, size_y = total.shape[:2]
    rows = Fine(ops_ref, size_y)
    total[...] = given_ref[...]
    coarse_ref[...] = jnp.zeros_like(coarse_ref)
    add_sides(one_ref, two_ref, rows, total)
    keep_ends(total, end_total_ref)

    def body(x):
        ys = range(size_y)
        restrict_columns(
            rows, total, [(x, y) for y in ys], [transfer_ref[x * size_y + y] for y in ys],
            [rhs_ref.at[x, y] for y in ys], group_ref, [x] * size_y, coarse_ref, scratch,
        )

    over_inside(size_x, body)


def restrict_ends_kernel(
    group_ref, before_ref, after_ref, corner_before_ref, corner_after_ref, ops_ref, transfer_ref, given_ref, rhs_ref,
    part_ref, *refs
):
    pieces, (coarse_ref, total, scratch) = refs[:-3], refs[-3:]
    size_x, size_y = rhs_ref.shape[:2]
    rows = Fine(ops_ref, size_y)
    total[...] = given_ref[...]
    coarse_ref[...] = part_ref[...]
    add_ends([before_ref, after_ref, corner_before_ref, corner_after_ref], rows, total, size_x)

    places = [(end, y) for end in range(2) for y in range(size_y)]
    xs = [end * (size_x - 1) for end, _ in places]
    restrict_columns(
        rows, total, places, [transfer_ref[x * size_y + y] for x, (_, y) in zip(xs, places)],
        [rhs_ref.at[x, y] for x, (_, y) in zip(xs, places)], group_ref, xs, coarse_ref, scratch,
    )
    for step, piece in enumerate(pieces):
        first = lax.bitwise_xor(lax.axis_index("lateral"), step) * piece.shape[0]
        for x in range(piece.shape[0]):
            piece[x] = coarse_ref[first + x].astype(BF16)


def placed(pieces):
    found = []
    for step, piece in enumerate(pieces):
        first = lax.bitwise_xor(lax.axis_index("lateral"), step) * piece.shape[1]
        found += [(x, first + y, piece.at[x, y]) for x in range(piece.shape[0]) for y in range(piece.shape[1])]
    return found


def first_kernel(own_ref, other_ref, *refs):
    pieces, (coarse_ref, first_ref, round_ref, total, scratch) = refs[:-5], refs[-5:]
    rows = Coarse(own_ref, other_ref, coarse_ref.shape[1])
    columns = placed(pieces)
    cells = [[piece[z] for z in range(2)] for _, _, piece in columns]
    lefts = [mask_layers(rows.smoother(x, y), rows.kind()) for x, y, _ in columns]
    places = [(index,) for index in range(len(columns))]
    changes = smoothed(rows, lefts, cells, total, places, [scratch.at[index] for index in range(len(columns))])
    for (x, y, _), cell, change in zip(columns, cells, changes):
        for z in range(2):
            value = DAMPING * change[z]
            coarse_ref[x, y, z] = cell[z]
            first_ref[x, y, z] = value
            round_ref[x, y, z] = value.astype(BF16)


def second_kernel(before_ref, after_ref, own_ref, other_ref, given_ref, coarse_ref, first_ref, *refs):
    pieces, (total, scratch) = refs[:-2], refs[-2:]
    rows = Coarse(own_ref, other_ref, total.shape[1])
    total[...] = given_ref[...]
    add_coarse_ends(before_ref, after_ref, rows, total)
    columns = placed(pieces)
    values = smooth_columns(
        rows, total, [(x, y) for x, y, _ in columns], [rows.smoother(x, y) for x, y, _ in columns],
        [[coarse_ref[x, y, z].astype(F32) for z in range(2)] for x, y, _ in columns],
        [first_ref.at[x, y] for x, y, _ in columns], scratch,
    )
    for (_, _, piece), value in zip(columns, values):
        for z in range(2):
            piece[z] = value[z].astype(BF16)


def prolong_kernel(group_ref, transfer_ref, iterate_ref, ends_ref, *refs):
    pieces, (out_ref, correction, total, scratch, made, sent) = refs[:-6], refs[-6:]
    size_x, size_y = out_ref.shape[:2]
    for step, piece in enumerate(pieces):
        first = lax.bitwise_xor(lax.axis_index("lateral"), step) * piece.shape[0]
        for x in range(piece.shape[0]):
            correction[first + x] = piece[x]
    rows = Fine(None, size_y)

    def send(x):
        return pltpu.make_async_copy(made.at[x], out_ref.at[x], sent.at[x])

    def added(x, iterate):
        ys = range(size_y)
        source = lambda y, z: group_ref[y, z, x] - lax.axis_index("track") * size_x
        cells = [[correction[source(y, z), y // 2, z] for z in range(2)] for y in ys]
        lefts = [mask_layers(transfer_ref[x * size_y + y], rows.kind()) for y in ys]
        changes = smoothed(rows, lefts, cells, total, [(y,) for y in ys], [scratch.at[y, 0] for y in ys])
        for y in ys:
            for z in range(2):
                made[x, y, z] = iterate[y, z] + changes[y][z]
        send(x).start()

    for end in range(2):
        added(end * (size_x - 1), tip(ends_ref, end))
    over_inside(size_x, lambda x: added(x, iterate_ref.at[x]))
    for x in range(size_x):
        send(x).wait()


SMEM = pl.BlockSpec(memory_space=pltpu.SMEM)
VMEM = pl.BlockSpec(memory_space=pltpu.VMEM)


def call(kernel, name, scalars, operands, out_shape, scratch=(), out_space=pltpu.VMEM):
    return pl.pallas_call(
        kernel,
        in_specs=[SMEM] * len(scalars) + [VMEM] * len(operands),
        out_specs=jax.tree.map(lambda _: pl.BlockSpec(memory_space=out_space), out_shape),
        out_shape=out_shape,
        scratch_shapes=list(scratch),
        compiler_params=pltpu.CompilerParams(vmem_limit_bytes=LIMIT),
        name=name,
    )(*scalars, *operands)


def swap_sides(one, two):
    lateral, depth = lax.axis_size("lateral"), lax.axis_size("depth")
    ring = [i * depth for i in range(lateral)] + [i * depth + 1 for i in reversed(range(lateral))]
    onward = list(zip(ring, ring[1:] + ring[:1]))
    back = [(b, a) for a, b in onward]
    return lax.ppermute(one, ("lateral", "depth"), onward), lax.ppermute(two, ("lateral", "depth"), back)


def swap_ends(last, first):
    count = lax.axis_size("track")
    before = lax.ppermute(last, "track", [(i, (i + 1) % count) for i in range(count)])
    after = lax.ppermute(first, "track", [((i + 1) % count, i) for i in range(count)])
    return before, after


def swap_corners(one, two):
    return swap_ends(jnp.concatenate([one[-1:], two[-1:]], axis=0), jnp.concatenate([one[:1], two[:1]], axis=0))


def swap_pieces(pieces):
    count = len(pieces)
    moved = [lax.ppermute(pieces[step], "lateral", [(i, i ^ step) for i in range(count)]) for step in range(count - 1, 0, -1)]
    return [pieces[0]] + moved[::-1]


def swap_coarse_ends(cells):
    axes = ("track", "lateral")
    count = lax.axis_size(axes)
    before = lax.ppermute(cells[-1], axes, [(i, (i + 1) % count) for i in range(count)])
    after = lax.ppermute(cells[0], axes, [((i + 1) % count, i) for i in range(count)])
    return before, after


def per_device(
    rhs,
    start,
    fine_blocks,
    fine_cols,
    fine_mass,
    fine_smoother,
    transfer,
    aggregate,
    coarse_blocks,
    coarse_cols,
    coarse_mass,
    coarse_smoother,
):
    size_x, size_y, size_z, width, loads = rhs.shape
    count = lax.axis_size("lateral")
    groups = in_hbm(aggregate.transpose(1, 2, 0))
    part_x, all_y = coarse_blocks.shape[:2]
    coarse_y = size_y // 2

    paired = lambda a: a.reshape(size_x, size_y, size_z, HALF, LANES).transpose(0, 1, 3, 2, 4).reshape(-1, 2 * HALF, LANES)
    smoothers, transfers = paired(fine_smoother), paired(transfer)
    field = (size_x, size_y, size_z, width, loads)
    coarse_field = (size_x, coarse_y, size_z, width, loads)
    solve_field = (part_x, all_y, size_z, width, loads)
    sums = lambda shape: shape[:2] + (2, 2 * HALF, LANES)
    full = jax.ShapeDtypeStruct
    two_ends = lambda shape: (2,) + shape[1:]
    scratch = pltpu.VMEM((2 * size_y, 2, 2, width, loads), F32)
    whole, ends = pltpu.VMEM(sums(field), F32), pltpu.VMEM(two_ends(sums(field)), F32)
    face = full((size_x, size_z, width, loads), BF16)

    def inner_of(cells, tips, ops, grid):
        shape = full(sums(cells.shape), F32)
        return call(functools.partial(inner_kernel, grid=grid), "inner", [], [cells, tips, *ops], shape)

    rounded, one, two = round_start(start)
    tips, old, old_tips = rounded, start, start
    fine_cols, one, two = lax.optimization_barrier((fine_cols, one, two))
    one, two = swap_sides(one, two)
    fine_ops = sort_fine(fine_blocks, fine_cols, fine_mass)
    for sweep in range(SWEEPS + 1):
        inner = inner_of(rounded, tips, [fine_ops], Fine)
        inner, tips = lax.optimization_barrier((inner, tips))
        near = swap_ends(tips[-1], tips[0])
        if sweep == 1:
            coarse_cols, inner = lax.optimization_barrier((coarse_cols, inner))
            own_ops = sort_coarse(coarse_blocks, coarse_cols, coarse_mass, coarse_smoother)
            inner, one, two, own_ops = lax.optimization_barrier((inner, one, two, own_ops))
            other_ops = lax.ppermute(own_ops, "depth", [(0, 1), (1, 0)])
        else:
            inner, one, two = lax.optimization_barrier((inner, one, two))
        around = [*near, *swap_corners(one, two)]
        if sweep == SWEEPS:
            break
        end_total, new, rounded = call(
            smooth_inside_kernel, "smooth_inside", [], [one, two, fine_ops, smoothers, inner, rhs, old],
            [full(two_ends(sums(field)), F32), full(field, F32), full(field, BF16)], [whole, scratch],
        )
        new_tips, tips, one, two = call(
            smooth_ends_kernel, "smooth_ends", [], [*around, fine_ops, smoothers, end_total, rhs, old_tips, rounded],
            [full(two_ends(field), F32), full(two_ends(field), BF16), face, face], [ends, scratch],
        )
        old, old_tips = new, new_tips
        one, two = swap_sides(one, two)
    end_total, coarse_part = call(
        restrict_inside_kernel, "restrict_inside", [groups], [one, two, fine_ops, transfers, inner, rhs],
        [full(two_ends(sums(field)), F32), full(coarse_field, F32)], [whole, scratch],
    )
    piece = full((part_x,) + coarse_field[1:], BF16)
    pieces = call(
        restrict_ends_kernel, "restrict_ends", [groups],
        [*around, fine_ops, transfers, end_total, rhs, coarse_part], [piece] * count,
        [pltpu.VMEM(coarse_field, F32), ends, scratch],
    )
    line = pltpu.VMEM((part_x * all_y, 2, 2, width, loads), F32)
    coarse_ops = [own_ops, other_ops]
    coarse_res, first, rounded = call(
        first_kernel, "first", [], coarse_ops + swap_pieces(pieces),
        [full(solve_field, BF16), full(solve_field, F32), full(solve_field, BF16)],
        [
            pltpu.VMEM((part_x * all_y, 2, 2 * HALF, LANES), F32),
            pltpu.VMEM((part_x * all_y, 2, width, loads), F32),
        ],
    )
    before, after = swap_coarse_ends(rounded)
    inner = inner_of(rounded, rounded, coarse_ops, Coarse)
    pieces = call(
        second_kernel, "second", [], [before, after, *coarse_ops, inner, coarse_res, first], [piece] * count,
        [pltpu.VMEM(sums(solve_field), F32), line],
    )
    return call(
        prolong_kernel, "prolong", [groups], [transfers, old, old_tips] + swap_pieces(pieces), full(field, F32),
        [
            pltpu.VMEM(coarse_field, BF16), pltpu.VMEM((size_y, 2, 2 * HALF, LANES), F32), scratch,
            pltpu.VMEM(field, F32), pltpu.SemaphoreType.DMA((size_x,)),
        ],
        out_space=pltpu.HBM,
    )


def solution(mesh):
    in_specs = (
        P("track", "lateral", None, None, "depth"),
        P("track", "lateral", None, None, "depth"),
        P("track", "lateral", None, None, None),
        P("track", "lateral", None, None),
        P("track", "lateral", None, None),
        P("track", "lateral", None, None),
        P("track", "lateral", None, None),
        P("track", "lateral", None),
        P(("track", "lateral"), None, "depth", None, None),
        P(("track", "lateral"), None, "depth", None),
        P(("track", "lateral"), None, "depth", None),
        P(("track", "lateral"), None, "depth", None),
    )
    out_specs = P("track", "lateral", None, None, "depth")
    return jax.shard_map(
        per_device, mesh=mesh, in_specs=in_specs, out_specs=out_specs, check_vma=False
    )
```

```python
import functools

import jax
import jax.numpy as jnp
from jax import lax
from jax.experimental import pallas as pl
from jax.experimental.pallas import tpu as pltpu
from jax.sharding import PartitionSpec as P

SWEEPS = 2
DAMPING = 0.8
HALF = 32
LANES = 128
WIDE = 256
STEPS = 9
BF16 = jnp.bfloat16
F32 = jnp.float32
LIMIT = 8 * 1024 * 1024


def listed_at(cols_ref, slots, index, groups):
    for group in range(groups):
        codes = [cols_ref[index * groups + group, slot] for slot in range(27)]
        for slot, code in enumerate(codes):
            slots[group, code] = slot


def diagonal(mass, rows, groups):
    row = lax.broadcasted_iota(jnp.int32, (rows, LANES), 0)
    lane = lax.broadcasted_iota(jnp.int32, (rows, LANES), 1)
    spread = jnp.zeros((rows, LANES), F32)
    for group in range(groups):
        spread = jnp.where(row % groups == group, mass[group : group + 1], spread)
    return jnp.where(lane % 64 == 2 * (row // groups) + lane // 64, spread, 0.0)


def fine_sort_kernel(cols_ref, mass_ref, blocks_ref, out_ref, slots, held, arrived):
    second = lax.broadcasted_iota(jnp.int32, (2 * HALF, LANES), 0) % 2 == 1
    columns, parts = out_ref.shape[0], arrived.shape[0]
    each = columns // parts
    copies = [
        pltpu.make_async_copy(blocks_ref.at[pl.ds(part * each, each)], held.at[pl.ds(part * each, each)], arrived.at[part])
        for part in range(parts)
    ]
    for copy in copies:
        copy.start()
    for index in range(columns):
        listed_at(cols_ref, slots.at[index], index, 2)
    for index in range(columns):
        if index % each == 0:
            copies[index // each].wait()
        for step in range(STEPS):
            for side in range(2):
                upper = held[index, slots[index, 0, 3 * step + side + 1]]
                lower = held[index, slots[index, 1, 3 * step + side]]
                span = slice(side * LANES, (side + 1) * LANES)
                out_ref[index, step * 2 * HALF : (step + 1) * 2 * HALF, span] = jnp.where(second, lower, upper)
        mass = mass_ref[index].astype(F32)
        mass = diagonal(jnp.concatenate([mass, mass], axis=1), 2 * HALF, 2)
        for side in range(2):
            span = slice(side * LANES, (side + 1) * LANES)
            out_ref[index, STEPS * 2 * HALF :, span] = jnp.where(second == (side == 1), mass, 0.0).astype(BF16)


def coarse_sort_kernel(cols_ref, mass_ref, smoother_ref, blocks_ref, out_ref, slots, scratch):
    groups = blocks_ref.shape[2] // HALF
    rows = groups * HALF
    kind = lax.broadcasted_iota(jnp.int32, (rows, LANES), 0) % groups

    def hand_out(values, first, span):
        scratch[...] = values
        for y in range(groups):
            out_ref[y, first : first + HALF, span] = scratch[pl.ds(y, HALF, stride=groups), :].astype(BF16)

    listed_at(cols_ref, slots, pl.program_id(0), groups)
    for step in range(STEPS):
        for side in range(2):
            code = 3 * step + side + 1 - lax.axis_index("depth")
            values = blocks_ref[0, slots[0, code]]
            for group in range(1, groups):
                values = jnp.where(kind == group, blocks_ref[0, slots[group, code]], values)
            hand_out(values.astype(F32), step * HALF, slice(side * LANES, (side + 1) * LANES))
    hand_out(smoother_ref[0].astype(F32), STEPS * HALF, slice(0, LANES))
    mass = mass_ref[0].astype(F32)
    mass = diagonal(jnp.concatenate([mass, mass], axis=1), rows, groups)
    hand_out(mass, STEPS * HALF, slice(LANES, WIDE))


def in_hbm(array):
    return pltpu.with_memory_space_constraint(array, pltpu.HBM)


def sort_fine(blocks, cols, mass):
    size_x, size_y, layers = blocks.shape[:3]
    columns = size_x * size_y
    paired = blocks.reshape(size_x, size_y, layers, 27, HALF, LANES).transpose(0, 1, 3, 4, 2, 5)
    rows = (STEPS + 1) * 2 * HALF
    shape = (columns, 27, layers * HALF, LANES)
    return pl.pallas_call(
        fine_sort_kernel,
        in_specs=[SMEM, VMEM, pl.BlockSpec(memory_space=pltpu.HBM)],
        out_specs=VMEM,
        out_shape=jax.ShapeDtypeStruct((columns, rows, WIDE), BF16),
        scratch_shapes=[
            pltpu.SMEM((columns, 2, 27), jnp.int32), pltpu.VMEM(shape, BF16), pltpu.SemaphoreType.DMA((columns // 2,)),
        ],
        compiler_params=pltpu.CompilerParams(vmem_limit_bytes=2 * LIMIT),
        name="sort_fine",
    )(in_hbm(cols.reshape(columns * layers, 27)), in_hbm(mass.reshape(columns, layers, 64)), in_hbm(paired.reshape(shape)))


def sort_coarse(blocks, cols, mass, smoother):
    size_x, size_y = blocks.shape[:2]
    paired = blocks.reshape(size_x, size_y, 27, HALF, LANES).transpose(0, 2, 3, 1, 4)
    smoothers = smoother.reshape(size_x, size_y, HALF, LANES).transpose(0, 2, 1, 3)
    rows = (STEPS + 1) * HALF
    return pl.pallas_call(
        coarse_sort_kernel,
        grid=(size_x,),
        in_specs=[
            SMEM,
            pl.BlockSpec((1, size_y, 64), lambda i: (i, 0, 0)),
            pl.BlockSpec((1, size_y * HALF, LANES), lambda i: (i, 0, 0)),
            pl.BlockSpec((1, 27, size_y * HALF, LANES), lambda i: (i, 0, 0, 0)),
        ],
        out_specs=pl.BlockSpec((size_y, rows, WIDE), lambda i: (i, 0, 0)),
        out_shape=jax.ShapeDtypeStruct((size_x * size_y, rows, WIDE), BF16),
        scratch_shapes=[pltpu.SMEM((size_y, 27), jnp.int32), pltpu.VMEM((size_y * HALF, LANES), F32)],
        compiler_params=pltpu.CompilerParams(vmem_limit_bytes=LIMIT),
        name="sort_coarse",
    )(
        in_hbm(cols.reshape(size_x * size_y, 27)),
        in_hbm(mass.reshape(size_x, size_y, 64)),
        in_hbm(smoothers.reshape(size_x, size_y * HALF, LANES)),
        in_hbm(paired.reshape(size_x, 27, size_y * HALF, LANES)),
    )


def two_sided(block):
    none = jnp.zeros_like(block)
    return jnp.concatenate(
        [jnp.concatenate([block, none], axis=1), jnp.concatenate([none, block], axis=1)], axis=0
    )


def mask_layers(block, kind):
    none = jnp.zeros_like(block)
    return jnp.concatenate([jnp.where(kind == 0, block, none), jnp.where(kind == 1, block, none)], axis=1)


class Fine:
    def __init__(self, ops_ref, size_y):
        self.ops_ref, self.size_y = ops_ref, size_y

    def kind(self):
        return lax.broadcasted_iota(jnp.int32, (2 * HALF, LANES), 0) % 2

    def step(self, x, y, step):
        return self.ops_ref[x * self.size_y + y, step * 2 * HALF : (step + 1) * 2 * HALF, :]

    def mass(self, x, y):
        return self.step(x, y, STEPS)

    def half(self, total, place, z, parity):
        return total[(*place, parity, pl.ds(z, HALF, stride=2), slice(None))]


class Coarse:
    def __init__(self, own_ref, other_ref, size_y):
        self.own_ref, self.other_ref, self.size_y = own_ref, other_ref, size_y

    def kind(self):
        row = lax.broadcasted_iota(jnp.int32, (2 * HALF, LANES), 0)
        return lax.bitwise_xor(row // HALF, lax.axis_index("depth"))

    def step(self, x, y, step):
        place, span = x * self.size_y + y, slice(step * HALF, (step + 1) * HALF)
        return jnp.concatenate([self.own_ref[place, span, :], self.other_ref[place, span, :]], axis=0)

    def smoother(self, x, y):
        return self.step(x, y, STEPS)[:, :LANES]

    def mass(self, x, y):
        return mask_layers(self.step(x, y, STEPS)[:, LANES:], self.kind())

    def half(self, total, place, z, parity):
        first = pl.multiple_of(lax.bitwise_xor(jnp.int32(z), lax.axis_index("depth")) * HALF, HALF)
        return total[(*place, parity, pl.ds(first, HALF), slice(None))]


def both_layers(cells):
    return jnp.concatenate([two_sided(cells[0]), two_sided(cells[1])], axis=0)


def tip(ref, end):
    return ref.at[end * (ref.shape[0] - 1)]


def add_from(total_ref, rows, cells, targets, slot=lambda x: x):
    left = [rows.step(*target) for target in targets]
    given = jnp.dot(jnp.concatenate(left, axis=0), both_layers(cells), preferred_element_type=F32)
    parts = [given[index * 2 * HALF : (index + 1) * 2 * HALF] for index in range(len(left))]
    for (x, y, _), part in zip(targets, parts):
        for parity in range(2):
            total_ref[slot(x), y, parity] += part[:, parity * LANES : (parity + 1) * LANES]


def natural(rows, total, places, scratches):
    for place, scratch in zip(places, scratches):
        for z in range(2):
            for parity in range(2):
                scratch[z, pl.ds(parity, HALF, stride=2), :] = rows.half(total, place, z, parity)
    return [[scratch[z] for z in range(2)] for scratch in scratches]


def smoothed(rows, lefts, columns, total, places, scratches):
    given = [
        jnp.dot(left, both_layers([cell.astype(BF16) for cell in cells]), preferred_element_type=F32)
        for left, cells in zip(lefts, columns)
    ]
    for part, place in zip(given, places):
        for parity in range(2):
            total[(*place, parity)] = part[:, parity * LANES : (parity + 1) * LANES]
    return natural(rows, total, places, scratches)


def over_columns(size_x, column):
    if size_x == 1:
        column(0, (0,))
        return
    column(0, (-1, 0))
    for x in range(1, size_x - 1):
        column(x, (-1, 0, 1))
    column(size_x - 1, (0, 1))


def inner_kernel(cells_ref, ends_ref, *refs, grid):
    *ops, total_ref = refs
    size_x, size_y = cells_ref.shape[:2]
    rows = grid(*ops, size_y)
    total_ref[...] = jnp.zeros_like(total_ref)

    def column(x, shifts):
        row = tip(ends_ref, min(x, 1)) if x in (0, size_x - 1) else cells_ref.at[x]
        sums = {}
        for near in range(size_y):
            targets = [(shift, y) for shift in shifts for y in range(size_y) if abs(near - y) <= 1]
            left = [rows.step(x - shift, y, (shift + 1) * 3 + near - y + 1) for shift, y in targets]
            left.append(rows.mass(x, near))
            given = jnp.dot(jnp.concatenate(left, axis=0), both_layers(row[near]), preferred_element_type=F32)
            for index, target in enumerate(targets + [(0, near)]):
                part = given[index * 2 * HALF : (index + 1) * 2 * HALF]
                sums[target] = sums[target] + part if target in sums else part
        for (shift, y), part in sums.items():
            for parity in range(2):
                total_ref[x - shift, y, parity] += part[:, parity * LANES : (parity + 1) * LANES]

    over_columns(size_x, column)


def inside_track(cells, low):
    at = lax.axis_index("lateral")
    inside = at > 0 if low else at < lax.axis_size("lateral") - 1
    return jnp.where(inside, cells, jnp.zeros_like(cells))


def add_sides(one_ref, two_ref, rows, total):
    size_x, size_y = total.shape[:2]

    def both(low_ref, high_ref):
        def column(x, shifts):
            for cells, y, step in (
                (inside_track(low_ref[x], True), 0, 0),
                (inside_track(high_ref[x], False), size_y - 1, 2),
            ):
                add_from(total, rows, cells, [(x - shift, y, (shift + 1) * 3 + step) for shift in shifts])

        over_columns(size_x, column)

    odd = lax.axis_index("depth") % 2
    pl.when(odd == 0)(lambda: both(one_ref, two_ref))
    pl.when(odd == 1)(lambda: both(two_ref, one_ref))


def give_faces(low, high, one_ref, two_ref, x):
    even = lax.axis_index("depth") % 2 == 0
    for z in range(2):
        one_ref[x, z] = jnp.where(even, high[z], low[z])
        two_ref[x, z] = jnp.where(even, low[z], high[z])


def give_all_faces(cells_ref, ends_ref, one_ref, two_ref):
    size_x, size_y = cells_ref.shape[:2]

    for x in range(1, size_x - 1):
        give_faces(cells_ref.at[x, 0], cells_ref.at[x, size_y - 1], one_ref, two_ref, x)
    for end in range(2):
        ends = tip(ends_ref, end)
        give_faces(ends.at[0], ends.at[size_y - 1], one_ref, two_ref, end * (size_x - 1))


def round_kernel(start_ref, round_ref, one_ref, two_ref):
    for x in range(start_ref.shape[0]):
        cells = [[start_ref[x, y, z].astype(BF16) for z in range(2)] for y in range(start_ref.shape[1])]
        for y, column in enumerate(cells):
            for z in range(2):
                round_ref[x, y, z] = column[z]
        give_faces(cells[0], cells[-1], one_ref, two_ref, x)


def round_start(start):
    size_x, size_y, layers, width, loads = start.shape
    batch = size_x // 4
    side = pl.BlockSpec((batch, layers, width, loads), lambda i: (i, 0, 0, 0))
    whole = pl.BlockSpec((batch, size_y, layers, width, loads), lambda i: (i, 0, 0, 0, 0))
    face = jax.ShapeDtypeStruct((size_x, layers, width, loads), BF16)
    return pl.pallas_call(
        round_kernel,
        grid=(4,),
        in_specs=[whole],
        out_specs=[whole, side, side],
        out_shape=[jax.ShapeDtypeStruct(start.shape, BF16), face, face],
        compiler_params=pltpu.CompilerParams(vmem_limit_bytes=LIMIT),
        name="round_start",
    )(in_hbm(start))


def add_ends(given_refs, rows, total, size_x):
    size_y = total.shape[1]
    odd = lax.axis_index("depth") % 2
    at, count = lax.axis_index("track"), lax.axis_size("track")
    for near in range(-1, size_y + 1):
        ys = [y for y in range(size_y) if abs(near - y) <= 1]
        corner = near in (-1, size_y)
        place = (odd if near < 0 else 1 - odd) if corner else near
        for end, inside in ((0, at > 0), (1, at < count - 1)):
            cells = given_refs[2 * corner + end][place]
            cells = jnp.where(inside, cells, jnp.zeros_like(cells))
            if corner:
                cells = inside_track(cells, near < 0)
            targets = [(end * (size_x - 1), y, 6 * end + near - y + 1) for y in ys]
            add_from(total, rows, cells, targets, slot=lambda x, end=end: end)


def add_coarse_ends(one_ref, two_ref, rows, total):
    size_x, size_y = total.shape[:2]
    even = lax.axis_index("depth") % 2 == 0
    at = lax.axis_index(("track", "lateral"))
    count = lax.axis_size(("track", "lateral"))
    for near in range(size_y):
        ys = [y for y in range(size_y) if abs(near - y) <= 1]
        one, two = one_ref[near], two_ref[near]
        for end, cells, inside in ((0, jnp.where(even, one, two), at > 0), (1, jnp.where(even, two, one), at < count - 1)):
            cells = jnp.where(inside, cells, jnp.zeros_like(cells))
            add_from(total, rows, cells, [(end * (size_x - 1), y, 6 * end + near - y + 1) for y in ys])


def over_inside(size_x, body):
    for x in range(1, size_x - 1):
        body(x)


def smooth_columns(rows, total, places, smoothers, rhs, old, scratch):
    first = [scratch.at[index, 0] for index in range(len(places))]
    second = [scratch.at[index, 1] for index in range(len(places))]
    applied = natural(rows, total, places, first)
    residuals = [[ref[z] - part[z] for z in range(2)] for ref, part in zip(rhs, applied)]
    lefts = [mask_layers(smoother, rows.kind()) for smoother in smoothers]
    changes = smoothed(rows, lefts, residuals, total, places, second)
    return [[ref[z] + DAMPING * part[z] for z in range(2)] for ref, part in zip(old, changes)]


def keep_ends(total, end_total_ref):
    for end in range(2):
        end_total_ref[end] = tip(total, end)[...]


def smooth_inside_kernel(
    one_ref, two_ref, ops_ref, smoother_ref, given_ref, rhs_ref, old_ref, end_total_ref, new_ref, round_ref, total, scratch
):
    size_x, size_y = total.shape[:2]
    rows = Fine(ops_ref, size_y)
    total[...] = given_ref[...]
    add_sides(one_ref, two_ref, rows, total)
    keep_ends(total, end_total_ref)

    def body(x):
        ys = range(size_y)
        values = smooth_columns(
            rows, total, [(x, y) for y in ys], [smoother_ref[x * size_y + y] for y in ys],
            [rhs_ref.at[x, y] for y in ys], [old_ref.at[x, y] for y in ys], scratch,
        )
        for y in ys:
            for z in range(2):
                new_ref[x, y, z] = values[y][z]
                round_ref[x, y, z] = values[y][z].astype(BF16)

    over_inside(size_x, body)


def smooth_ends_kernel(
    before_ref, after_ref, corner_before_ref, corner_after_ref, ops_ref, smoother_ref, given_ref, rhs_ref, old_ref, cells_ref,
    new_ref, round_ref, one_ref, two_ref, total, scratch,
):
    size_x, size_y = cells_ref.shape[:2]
    rows = Fine(ops_ref, size_y)
    total[...] = given_ref[...]
    add_ends([before_ref, after_ref, corner_before_ref, corner_after_ref], rows, total, size_x)

    places = [(end, y) for end in range(2) for y in range(size_y)]
    row = lambda end: end * (size_x - 1)
    values = smooth_columns(
        rows, total, places, [smoother_ref[row(end) * size_y + y] for end, y in places],
        [rhs_ref.at[row(end), y] for end, y in places], [tip(old_ref, end).at[y] for end, y in places], scratch,
    )
    for (end, y), value in zip(places, values):
        for z in range(2):
            new_ref[end, y, z] = value[z]
            round_ref[end, y, z] = value[z].astype(BF16)
    give_all_faces(cells_ref, round_ref, one_ref, two_ref)


def restrict_columns(rows, total, places, transfers, rhs, group_ref, xs, coarse_ref, scratch):
    size_x = coarse_ref.shape[0]
    first = [scratch.at[index, 0] for index in range(len(places))]
    applied = natural(rows, total, places, first)
    for index, place in enumerate(places):
        for z in range(2):
            scratch[index, 1, z] = rhs[index][z] - applied[index][z]
    for index, place in enumerate(places):
        for z in range(2):
            for parity in range(2):
                taken = scratch[index, 1, z, pl.ds(parity, HALF, stride=2), :]
                total[(*place, parity, pl.ds(z, HALF, stride=2), slice(None))] = taken
    given = []
    for place, transfer in zip(places, transfers):
        left = mask_layers(transfer, rows.kind())
        right = jnp.concatenate([total[(*place, 0)], total[(*place, 1)]], axis=1).astype(BF16)
        given.append(lax.dot_general(left, right, (((0,), (0,)), ((), ())), preferred_element_type=F32))
    for (_, y), x, both in zip(places, xs, given):
        for z in range(2):
            target = group_ref[y, z, x] - lax.axis_index("track") * size_x
            own = both[z * LANES : (z + 1) * LANES]
            coarse_ref[target, y // 2, z] += own[:64, :LANES] + own[64:, LANES:]


def restrict_inside_kernel(
    group_ref, one_ref, two_ref, ops_ref, transfer_ref, given_ref, rhs_ref, end_total_ref, coarse_ref, total, scratch
):
    size_x, size_y = total.shape[:2]
    rows = Fine(ops_ref, size_y)
    total[...] = given_ref[...]
    coarse_ref[...] = jnp.zeros_like(coarse_ref)
    add_sides(one_ref, two_ref, rows, total)
    keep_ends(total, end_total_ref)

    def body(x):
        ys = range(size_y)
        restrict_columns(
            rows, total, [(x, y) for y in ys], [transfer_ref[x * size_y + y] for y in ys],
            [rhs_ref.at[x, y] for y in ys], group_ref, [x] * size_y, coarse_ref, scratch,
        )

    over_inside(size_x, body)


def restrict_ends_kernel(
    group_ref, before_ref, after_ref, corner_before_ref, corner_after_ref, ops_ref, transfer_ref, given_ref, rhs_ref,
    part_ref, *refs
):
    pieces, (coarse_ref, total, scratch) = refs[:-3], refs[-3:]
    size_x, size_y = rhs_ref.shape[:2]
    rows = Fine(ops_ref, size_y)
    total[...] = given_ref[...]
    coarse_ref[...] = part_ref[...]
    add_ends([before_ref, after_ref, corner_before_ref, corner_after_ref], rows, total, size_x)

    places = [(end, y) for end in range(2) for y in range(size_y)]
    xs = [end * (size_x - 1) for end, _ in places]
    restrict_columns(
        rows, total, places, [transfer_ref[x * size_y + y] for x, (_, y) in zip(xs, places)],
        [rhs_ref.at[x, y] for x, (_, y) in zip(xs, places)], group_ref, xs, coarse_ref, scratch,
    )
    for step, piece in enumerate(pieces):
        first = lax.bitwise_xor(lax.axis_index("lateral"), step) * piece.shape[0]
        for x in range(piece.shape[0]):
            piece[x] = coarse_ref[first + x].astype(BF16)


def placed(pieces):
    found = []
    for step, piece in enumerate(pieces):
        first = lax.bitwise_xor(lax.axis_index("lateral"), step) * piece.shape[1]
        found += [(x, first + y, piece.at[x, y]) for x in range(piece.shape[0]) for y in range(piece.shape[1])]
    return found


def first_kernel(own_ref, other_ref, *refs):
    pieces, (coarse_ref, first_ref, round_ref, one_ref, two_ref, total, scratch) = refs[:-7], refs[-7:]
    rows = Coarse(own_ref, other_ref, coarse_ref.shape[1])
    columns = placed(pieces[::-1])
    cells = [[piece[z] for z in range(2)] for _, _, piece in columns]
    lefts = [mask_layers(rows.smoother(x, y), rows.kind()) for x, y, _ in columns]
    places = [(index,) for index in range(len(columns))]
    changes = smoothed(rows, lefts, cells, total, places, [scratch.at[index] for index in range(len(columns))])
    for (x, y, _), cell, change in zip(columns, cells, changes):
        for z in range(2):
            value = DAMPING * change[z]
            coarse_ref[x, y, z] = cell[z]
            first_ref[x, y, z] = value
            round_ref[x, y, z] = value.astype(BF16)
    for y in range(one_ref.shape[0]):
        give_faces(round_ref.at[0, y], round_ref.at[round_ref.shape[0] - 1, y], one_ref, two_ref, y)


def second_kernel(one_ref, two_ref, own_ref, other_ref, given_ref, coarse_ref, first_ref, *refs):
    pieces, (total, scratch) = refs[:-2], refs[-2:]
    rows = Coarse(own_ref, other_ref, total.shape[1])
    total[...] = given_ref[...]
    add_coarse_ends(one_ref, two_ref, rows, total)
    columns = placed(pieces)
    values = smooth_columns(
        rows, total, [(x, y) for x, y, _ in columns], [rows.smoother(x, y) for x, y, _ in columns],
        [[coarse_ref[x, y, z].astype(F32) for z in range(2)] for x, y, _ in columns],
        [first_ref.at[x, y] for x, y, _ in columns], scratch,
    )
    for (_, _, piece), value in zip(columns, values):
        for z in range(2):
            piece[z] = value[z].astype(BF16)


def prolong_kernel(group_ref, transfer_ref, iterate_ref, ends_ref, *refs):
    pieces, (out_ref, correction, total, scratch, made, sent) = refs[:-6], refs[-6:]
    size_x, size_y = out_ref.shape[:2]
    for step, piece in enumerate(pieces[::-1]):
        first = lax.bitwise_xor(lax.axis_index("lateral"), step) * piece.shape[0]
        for x in range(piece.shape[0]):
            correction[first + x] = piece[x]
    rows = Fine(None, size_y)

    def send(x):
        return pltpu.make_async_copy(made.at[x], out_ref.at[x], sent.at[x])

    def added(x, iterate):
        ys = range(size_y)
        source = lambda y, z: group_ref[y, z, x] - lax.axis_index("track") * size_x
        cells = [[correction[source(y, z), y // 2, z] for z in range(2)] for y in ys]
        lefts = [mask_layers(transfer_ref[x * size_y + y], rows.kind()) for y in ys]
        changes = smoothed(rows, lefts, cells, total, [(y,) for y in ys], [scratch.at[y, 0] for y in ys])
        for y in ys:
            for z in range(2):
                made[x, y, z] = iterate[y, z] + changes[y][z]
        send(x).start()

    for end in range(2):
        added(end * (size_x - 1), tip(ends_ref, end))
    over_inside(size_x, lambda x: added(x, iterate_ref.at[x]))
    for x in range(size_x):
        send(x).wait()


SMEM = pl.BlockSpec(memory_space=pltpu.SMEM)
VMEM = pl.BlockSpec(memory_space=pltpu.VMEM)


def call(kernel, name, scalars, operands, out_shape, scratch=(), out_space=pltpu.VMEM):
    return pl.pallas_call(
        kernel,
        in_specs=[SMEM] * len(scalars) + [VMEM] * len(operands),
        out_specs=jax.tree.map(lambda _: pl.BlockSpec(memory_space=out_space), out_shape),
        out_shape=out_shape,
        scratch_shapes=list(scratch),
        compiler_params=pltpu.CompilerParams(vmem_limit_bytes=LIMIT),
        name=name,
    )(*scalars, *operands)


def swap_round(one, two, axes):
    count, depth = lax.axis_size(axes), lax.axis_size("depth")
    ring = [i * depth for i in range(count)] + [i * depth + 1 for i in reversed(range(count))]
    onward = list(zip(ring, ring[1:] + ring[:1]))
    back = [(b, a) for a, b in onward]
    return lax.ppermute(one, (*axes, "depth"), onward), lax.ppermute(two, (*axes, "depth"), back)


def swap_sides(one, two):
    return swap_round(one, two, ("lateral",))


def swap_ends(last, first):
    count = lax.axis_size("track")
    before = lax.ppermute(last, "track", [(i, (i + 1) % count) for i in range(count)])
    after = lax.ppermute(first, "track", [((i + 1) % count, i) for i in range(count)])
    return before, after


def swap_corners(one, two):
    return swap_ends(jnp.concatenate([one[-1:], two[-1:]], axis=0), jnp.concatenate([one[:1], two[:1]], axis=0))


def swap_pieces(pieces):
    count = len(pieces)
    moved = [lax.ppermute(pieces[step], "lateral", [(i, i ^ step) for i in range(count)]) for step in range(1, count)]
    return moved[::-1] + [pieces[0]]


def per_device(
    rhs,
    start,
    fine_blocks,
    fine_cols,
    fine_mass,
    fine_smoother,
    transfer,
    aggregate,
    coarse_blocks,
    coarse_cols,
    coarse_mass,
    coarse_smoother,
):
    size_x, size_y, size_z, width, loads = rhs.shape
    count = lax.axis_size("lateral")
    groups = in_hbm(aggregate.transpose(1, 2, 0))
    part_x, all_y = coarse_blocks.shape[:2]
    coarse_y = size_y // 2

    paired = lambda a: a.reshape(size_x, size_y, size_z, HALF, LANES).transpose(0, 1, 3, 2, 4).reshape(-1, 2 * HALF, LANES)
    smoothers, transfers = paired(fine_smoother), paired(transfer)
    field = (size_x, size_y, size_z, width, loads)
    coarse_field = (size_x, coarse_y, size_z, width, loads)
    solve_field = (part_x, all_y, size_z, width, loads)
    sums = lambda shape: shape[:2] + (2, 2 * HALF, LANES)
    full = jax.ShapeDtypeStruct
    two_ends = lambda shape: (2,) + shape[1:]
    scratch = pltpu.VMEM((2 * size_y, 2, 2, width, loads), F32)
    whole, ends = pltpu.VMEM(sums(field), F32), pltpu.VMEM(two_ends(sums(field)), F32)
    face = full((size_x, size_z, width, loads), BF16)

    def inner_of(cells, tips, ops, grid):
        shape = full(sums(cells.shape), F32)
        return call(functools.partial(inner_kernel, grid=grid), "inner", [], [cells, tips, *ops], shape)

    rounded, one, two = round_start(start)
    tips, old, old_tips = rounded, start, start
    fine_cols, one, two = lax.optimization_barrier((fine_cols, one, two))
    one, two = swap_sides(one, two)
    fine_ops = sort_fine(fine_blocks, fine_cols, fine_mass)
    for sweep in range(SWEEPS + 1):
        inner = inner_of(rounded, tips, [fine_ops], Fine)
        inner, tips = lax.optimization_barrier((inner, tips))
        near = swap_ends(tips[-1], tips[0])
        if sweep == 1:
            coarse_cols, inner = lax.optimization_barrier((coarse_cols, inner))
            own_ops = sort_coarse(coarse_blocks, coarse_cols, coarse_mass, coarse_smoother)
            inner, one, two, own_ops = lax.optimization_barrier((inner, one, two, own_ops))
            other_ops = lax.ppermute(own_ops, "depth", [(0, 1), (1, 0)])
        else:
            inner, one, two = lax.optimization_barrier((inner, one, two))
        around = [*near, *swap_corners(one, two)]
        if sweep == SWEEPS:
            break
        end_total, new, rounded = call(
            smooth_inside_kernel, "smooth_inside", [], [one, two, fine_ops, smoothers, inner, rhs, old],
            [full(two_ends(sums(field)), F32), full(field, F32), full(field, BF16)], [whole, scratch],
        )
        new_tips, tips, one, two = call(
            smooth_ends_kernel, "smooth_ends", [], [*around, fine_ops, smoothers, end_total, rhs, old_tips, rounded],
            [full(two_ends(field), F32), full(two_ends(field), BF16), face, face], [ends, scratch],
        )
        old, old_tips = new, new_tips
        one, two = swap_sides(one, two)
    end_total, coarse_part = call(
        restrict_inside_kernel, "restrict_inside", [groups], [one, two, fine_ops, transfers, inner, rhs],
        [full(two_ends(sums(field)), F32), full(coarse_field, F32)], [whole, scratch],
    )
    piece = full((part_x,) + coarse_field[1:], BF16)
    pieces = call(
        restrict_ends_kernel, "restrict_ends", [groups],
        [*around, fine_ops, transfers, end_total, rhs, coarse_part], [piece] * count,
        [pltpu.VMEM(coarse_field, F32), ends, scratch],
    )
    line = pltpu.VMEM((part_x * all_y, 2, 2, width, loads), F32)
    coarse_ops = [own_ops, other_ops]
    row = full(solve_field[1:], BF16)
    coarse_res, first, rounded, one, two = call(
        first_kernel, "first", [], coarse_ops + swap_pieces(pieces),
        [full(solve_field, BF16), full(solve_field, F32), full(solve_field, BF16), row, row],
        [
            pltpu.VMEM((part_x * all_y, 2, 2 * HALF, LANES), F32),
            pltpu.VMEM((part_x * all_y, 2, width, loads), F32),
        ],
    )
    one, two = swap_round(one, two, ("track", "lateral"))
    inner = inner_of(rounded, rounded, coarse_ops, Coarse)
    pieces = call(
        second_kernel, "second", [], [one, two, *coarse_ops, inner, coarse_res, first], [piece] * count,
        [pltpu.VMEM(sums(solve_field), F32), line],
    )
    return call(
        prolong_kernel, "prolong", [groups], [transfers, old, old_tips] + swap_pieces(pieces), full(field, F32),
        [
            pltpu.VMEM(coarse_field, BF16), pltpu.VMEM((size_y, 2, 2 * HALF, LANES), F32), scratch,
            pltpu.VMEM(field, F32), pltpu.SemaphoreType.DMA((size_x,)),
        ],
        out_space=pltpu.HBM,
    )


def solution(mesh):
    in_specs = (
        P("track", "lateral", None, None, "depth"),
        P("track", "lateral", None, None, "depth"),
        P("track", "lateral", None, None, None),
        P("track", "lateral", None, None),
        P("track", "lateral", None, None),
        P("track", "lateral", None, None),
        P("track", "lateral", None, None),
        P("track", "lateral", None),
        P(("track", "lateral"), None, "depth", None, None),
        P(("track", "lateral"), None, "depth", None),
        P(("track", "lateral"), None, "depth", None),
        P(("track", "lateral"), None, "depth", None),
    )
    out_specs = P("track", "lateral", None, None, "depth")
    return jax.shard_map(
        per_device, mesh=mesh, in_specs=in_specs, out_specs=out_specs, check_vma=False
    )
```

```python
import functools

import jax
import jax.numpy as jnp
from jax import lax
from jax.experimental import pallas as pl
from jax.experimental.pallas import tpu as pltpu
from jax.sharding import PartitionSpec as P

SWEEPS = 2
DAMPING = 0.8
HALF = 32
LANES = 128
WIDE = 256
STEPS = 9
BF16 = jnp.bfloat16
F32 = jnp.float32
LIMIT = 8 * 1024 * 1024


def listed_at(cols_ref, slots, index, groups):
    for group in range(groups):
        codes = [cols_ref[index * groups + group, slot] for slot in range(27)]
        for slot, code in enumerate(codes):
            slots[group, code] = slot


def diagonal(mass, rows, groups):
    row = lax.broadcasted_iota(jnp.int32, (rows, LANES), 0)
    lane = lax.broadcasted_iota(jnp.int32, (rows, LANES), 1)
    spread = jnp.zeros((rows, LANES), F32)
    for group in range(groups):
        spread = jnp.where(row % groups == group, mass[group : group + 1], spread)
    return jnp.where(lane % 64 == 2 * (row // groups) + lane // 64, spread, 0.0)


def fine_sort_kernel(cols_ref, mass_ref, blocks_ref, out_ref, slots, held, arrived):
    second = lax.broadcasted_iota(jnp.int32, (2 * HALF, LANES), 0) % 2 == 1
    columns, parts = out_ref.shape[0], arrived.shape[0]
    each = columns // parts
    copies = [
        pltpu.make_async_copy(blocks_ref.at[pl.ds(part * each, each)], held.at[pl.ds(part * each, each)], arrived.at[part])
        for part in range(parts)
    ]
    for copy in copies:
        copy.start()
    for index in range(columns):
        listed_at(cols_ref, slots.at[index], index, 2)
    for index in range(columns):
        if index % each == 0:
            copies[index // each].wait()
        for step in range(STEPS):
            for side in range(2):
                upper = held[index, slots[index, 0, 3 * step + side + 1]]
                lower = held[index, slots[index, 1, 3 * step + side]]
                span = slice(side * LANES, (side + 1) * LANES)
                out_ref[index, step * 2 * HALF : (step + 1) * 2 * HALF, span] = jnp.where(second, lower, upper)
        mass = mass_ref[index].astype(F32)
        mass = diagonal(jnp.concatenate([mass, mass], axis=1), 2 * HALF, 2)
        for side in range(2):
            span = slice(side * LANES, (side + 1) * LANES)
            out_ref[index, STEPS * 2 * HALF :, span] = jnp.where(second == (side == 1), mass, 0.0).astype(BF16)


def coarse_sort_kernel(cols_ref, mass_ref, smoother_ref, blocks_ref, out_ref, slots, scratch):
    groups = blocks_ref.shape[2] // HALF
    rows = groups * HALF
    kind = lax.broadcasted_iota(jnp.int32, (rows, LANES), 0) % groups

    def hand_out(values, first, span):
        scratch[...] = values
        for y in range(groups):
            out_ref[y, first : first + HALF, span] = scratch[pl.ds(y, HALF, stride=groups), :].astype(BF16)

    listed_at(cols_ref, slots, pl.program_id(0), groups)
    for step in range(STEPS):
        for side in range(2):
            code = 3 * step + side + 1 - lax.axis_index("depth")
            values = blocks_ref[0, slots[0, code]]
            for group in range(1, groups):
                values = jnp.where(kind == group, blocks_ref[0, slots[group, code]], values)
            hand_out(values.astype(F32), step * HALF, slice(side * LANES, (side + 1) * LANES))
    hand_out(smoother_ref[0].astype(F32), STEPS * HALF, slice(0, LANES))
    mass = mass_ref[0].astype(F32)
    mass = diagonal(jnp.concatenate([mass, mass], axis=1), rows, groups)
    hand_out(mass, STEPS * HALF, slice(LANES, WIDE))


def in_hbm(array):
    return pltpu.with_memory_space_constraint(array, pltpu.HBM)


def sort_fine(blocks, cols, mass):
    size_x, size_y, layers = blocks.shape[:3]
    columns = size_x * size_y
    paired = blocks.reshape(size_x, size_y, layers, 27, HALF, LANES).transpose(0, 1, 3, 4, 2, 5)
    rows = (STEPS + 1) * 2 * HALF
    shape = (columns, 27, layers * HALF, LANES)
    return pl.pallas_call(
        fine_sort_kernel,
        in_specs=[SMEM, VMEM, pl.BlockSpec(memory_space=pltpu.HBM)],
        out_specs=VMEM,
        out_shape=jax.ShapeDtypeStruct((columns, rows, WIDE), BF16),
        scratch_shapes=[
            pltpu.SMEM((columns, 2, 27), jnp.int32), pltpu.VMEM(shape, BF16), pltpu.SemaphoreType.DMA((columns // 2,)),
        ],
        compiler_params=pltpu.CompilerParams(vmem_limit_bytes=2 * LIMIT),
        name="sort_fine",
    )(in_hbm(cols.reshape(columns * layers, 27)), in_hbm(mass.reshape(columns, layers, 64)), in_hbm(paired.reshape(shape)))


def sort_coarse(blocks, cols, mass, smoother):
    size_x, size_y = blocks.shape[:2]
    paired = blocks.reshape(size_x, size_y, 27, HALF, LANES).transpose(0, 2, 3, 1, 4)
    smoothers = smoother.reshape(size_x, size_y, HALF, LANES).transpose(0, 2, 1, 3)
    rows = (STEPS + 1) * HALF
    return pl.pallas_call(
        coarse_sort_kernel,
        grid=(size_x,),
        in_specs=[
            SMEM,
            pl.BlockSpec((1, size_y, 64), lambda i: (i, 0, 0)),
            pl.BlockSpec((1, size_y * HALF, LANES), lambda i: (i, 0, 0)),
            pl.BlockSpec((1, 27, size_y * HALF, LANES), lambda i: (i, 0, 0, 0)),
        ],
        out_specs=pl.BlockSpec((size_y, rows, WIDE), lambda i: (i, 0, 0)),
        out_shape=jax.ShapeDtypeStruct((size_x * size_y, rows, WIDE), BF16),
        scratch_shapes=[pltpu.SMEM((size_y, 27), jnp.int32), pltpu.VMEM((size_y * HALF, LANES), F32)],
        compiler_params=pltpu.CompilerParams(vmem_limit_bytes=LIMIT),
        name="sort_coarse",
    )(
        in_hbm(cols.reshape(size_x * size_y, 27)),
        in_hbm(mass.reshape(size_x, size_y, 64)),
        in_hbm(smoothers.reshape(size_x, size_y * HALF, LANES)),
        in_hbm(paired.reshape(size_x, 27, size_y * HALF, LANES)),
    )


def two_sided(block):
    none = jnp.zeros_like(block)
    return jnp.concatenate(
        [jnp.concatenate([block, none], axis=1), jnp.concatenate([none, block], axis=1)], axis=0
    )


def mask_layers(block, kind):
    none = jnp.zeros_like(block)
    return jnp.concatenate([jnp.where(kind == 0, block, none), jnp.where(kind == 1, block, none)], axis=1)


class Fine:
    def __init__(self, ops_ref, size_y):
        self.ops_ref, self.size_y = ops_ref, size_y

    def kind(self):
        return lax.broadcasted_iota(jnp.int32, (2 * HALF, LANES), 0) % 2

    def step(self, x, y, step):
        return self.ops_ref[x * self.size_y + y, step * 2 * HALF : (step + 1) * 2 * HALF, :]

    def mass(self, x, y):
        return self.step(x, y, STEPS)

    def half(self, total, place, z, parity):
        return total[(*place, parity, pl.ds(z, HALF, stride=2), slice(None))]


class Coarse:
    def __init__(self, own_ref, other_ref, size_y):
        self.own_ref, self.other_ref, self.size_y = own_ref, other_ref, size_y

    def kind(self):
        row = lax.broadcasted_iota(jnp.int32, (2 * HALF, LANES), 0)
        return lax.bitwise_xor(row // HALF, lax.axis_index("depth"))

    def step(self, x, y, step):
        place, span = x * self.size_y + y, slice(step * HALF, (step + 1) * HALF)
        return jnp.concatenate([self.own_ref[place, span, :], self.other_ref[place, span, :]], axis=0)

    def smoother(self, x, y):
        return self.step(x, y, STEPS)[:, :LANES]

    def mass(self, x, y):
        return mask_layers(self.step(x, y, STEPS)[:, LANES:], self.kind())

    def half(self, total, place, z, parity):
        first = pl.multiple_of(lax.bitwise_xor(jnp.int32(z), lax.axis_index("depth")) * HALF, HALF)
        return total[(*place, parity, pl.ds(first, HALF), slice(None))]


def both_layers(cells):
    return jnp.concatenate([two_sided(cells[0]), two_sided(cells[1])], axis=0)


def tip(ref, end):
    return ref.at[end * (ref.shape[0] - 1)]


def add_from(total_ref, rows, cells, targets, slot=lambda x: x):
    left = [rows.step(*target) for target in targets]
    given = jnp.dot(jnp.concatenate(left, axis=0), both_layers(cells), preferred_element_type=F32)
    parts = [given[index * 2 * HALF : (index + 1) * 2 * HALF] for index in range(len(left))]
    for (x, y, _), part in zip(targets, parts):
        for parity in range(2):
            total_ref[slot(x), y, parity] += part[:, parity * LANES : (parity + 1) * LANES]


def natural(rows, total, places, scratches):
    for place, scratch in zip(places, scratches):
        for z in range(2):
            for parity in range(2):
                scratch[z, pl.ds(parity, HALF, stride=2), :] = rows.half(total, place, z, parity)
    return [[scratch[z] for z in range(2)] for scratch in scratches]


def smoothed(rows, lefts, columns, total, places, scratches):
    given = [
        jnp.dot(left, both_layers([cell.astype(BF16) for cell in cells]), preferred_element_type=F32)
        for left, cells in zip(lefts, columns)
    ]
    for part, place in zip(given, places):
        for parity in range(2):
            total[(*place, parity)] = part[:, parity * LANES : (parity + 1) * LANES]
    return natural(rows, total, places, scratches)


def over_columns(size_x, column):
    if size_x == 1:
        column(0, (0,))
        return
    column(0, (-1, 0))
    for x in range(1, size_x - 1):
        column(x, (-1, 0, 1))
    column(size_x - 1, (0, 1))


def inner_kernel(cells_ref, ends_ref, *refs, grid):
    *ops, total_ref = refs
    size_x, size_y = cells_ref.shape[:2]
    rows = grid(*ops, size_y)
    total_ref[...] = jnp.zeros_like(total_ref)

    def column(x, shifts):
        row = tip(ends_ref, min(x, 1)) if x in (0, size_x - 1) else cells_ref.at[x]
        sums = {}
        for near in range(size_y):
            targets = [(shift, y) for shift in shifts for y in range(size_y) if abs(near - y) <= 1]
            left = [rows.step(x - shift, y, (shift + 1) * 3 + near - y + 1) for shift, y in targets]
            left.append(rows.mass(x, near))
            given = jnp.dot(jnp.concatenate(left, axis=0), both_layers(row[near]), preferred_element_type=F32)
            for index, target in enumerate(targets + [(0, near)]):
                part = given[index * 2 * HALF : (index + 1) * 2 * HALF]
                sums[target] = sums[target] + part if target in sums else part
        for (shift, y), part in sums.items():
            for parity in range(2):
                total_ref[x - shift, y, parity] += part[:, parity * LANES : (parity + 1) * LANES]

    over_columns(size_x, column)


def inside_track(cells, low):
    at = lax.axis_index("lateral")
    inside = at > 0 if low else at < lax.axis_size("lateral") - 1
    return jnp.where(inside, cells, jnp.zeros_like(cells))


def add_sides(one_ref, two_ref, rows, total):
    size_x, size_y = total.shape[:2]

    def both(low_ref, high_ref):
        def column(x, shifts):
            for cells, y, step in (
                (inside_track(low_ref[x], True), 0, 0),
                (inside_track(high_ref[x], False), size_y - 1, 2),
            ):
                add_from(total, rows, cells, [(x - shift, y, (shift + 1) * 3 + step) for shift in shifts])

        over_columns(size_x, column)

    odd = lax.axis_index("depth") % 2
    pl.when(odd == 0)(lambda: both(one_ref, two_ref))
    pl.when(odd == 1)(lambda: both(two_ref, one_ref))


def give_faces(low, high, one_ref, two_ref, x):
    even = lax.axis_index("depth") % 2 == 0
    for z in range(2):
        one_ref[x, z] = jnp.where(even, high[z], low[z])
        two_ref[x, z] = jnp.where(even, low[z], high[z])


def give_all_faces(cells_ref, ends_ref, one_ref, two_ref):
    size_x, size_y = cells_ref.shape[:2]

    for x in range(1, size_x - 1):
        give_faces(cells_ref.at[x, 0], cells_ref.at[x, size_y - 1], one_ref, two_ref, x)
    for end in range(2):
        ends = tip(ends_ref, end)
        give_faces(ends.at[0], ends.at[size_y - 1], one_ref, two_ref, end * (size_x - 1))


def round_kernel(start_ref, round_ref, one_ref, two_ref, held, arrived):
    size_x, size_y = start_ref.shape[:2]
    copies = [pltpu.make_async_copy(start_ref.at[x], held.at[x], arrived.at[x]) for x in range(size_x)]
    for copy in copies:
        copy.start()
    for x, copy in enumerate(copies):
        copy.wait()
        cells = [[held[x, y, z].astype(BF16) for z in range(2)] for y in range(size_y)]
        for y, column in enumerate(cells):
            for z in range(2):
                round_ref[x, y, z] = column[z]
        give_faces(cells[0], cells[-1], one_ref, two_ref, x)


def round_start(start):
    size_x, _, layers, width, loads = start.shape
    face = jax.ShapeDtypeStruct((size_x, layers, width, loads), BF16)
    return pl.pallas_call(
        round_kernel,
        in_specs=[pl.BlockSpec(memory_space=pltpu.HBM)],
        out_specs=[VMEM] * 3,
        out_shape=[jax.ShapeDtypeStruct(start.shape, BF16), face, face],
        scratch_shapes=[pltpu.VMEM(start.shape, F32), pltpu.SemaphoreType.DMA((size_x,))],
        compiler_params=pltpu.CompilerParams(vmem_limit_bytes=LIMIT),
        name="round_start",
    )(in_hbm(start))


def add_ends(given_refs, rows, total, size_x):
    size_y = total.shape[1]
    odd = lax.axis_index("depth") % 2
    at, count = lax.axis_index("track"), lax.axis_size("track")
    for near in range(-1, size_y + 1):
        ys = [y for y in range(size_y) if abs(near - y) <= 1]
        corner = near in (-1, size_y)
        place = (odd if near < 0 else 1 - odd) if corner else near
        for end, inside in ((0, at > 0), (1, at < count - 1)):
            cells = given_refs[2 * corner + end][place]
            cells = jnp.where(inside, cells, jnp.zeros_like(cells))
            if corner:
                cells = inside_track(cells, near < 0)
            targets = [(end * (size_x - 1), y, 6 * end + near - y + 1) for y in ys]
            add_from(total, rows, cells, targets, slot=lambda x, end=end: end)


def add_coarse_ends(one_ref, two_ref, rows, total):
    size_x, size_y = total.shape[:2]
    even = lax.axis_index("depth") % 2 == 0
    at = lax.axis_index(("track", "lateral"))
    count = lax.axis_size(("track", "lateral"))
    for near in range(size_y):
        ys = [y for y in range(size_y) if abs(near - y) <= 1]
        one, two = one_ref[near], two_ref[near]
        for end, cells, inside in ((0, jnp.where(even, one, two), at > 0), (1, jnp.where(even, two, one), at < count - 1)):
            cells = jnp.where(inside, cells, jnp.zeros_like(cells))
            add_from(total, rows, cells, [(end * (size_x - 1), y, 6 * end + near - y + 1) for y in ys])


def over_inside(size_x, body):
    for x in range(1, size_x - 1):
        body(x)


def smooth_columns(rows, total, places, smoothers, rhs, old, scratch):
    first = [scratch.at[index, 0] for index in range(len(places))]
    second = [scratch.at[index, 1] for index in range(len(places))]
    applied = natural(rows, total, places, first)
    residuals = [[ref[z] - part[z] for z in range(2)] for ref, part in zip(rhs, applied)]
    lefts = [mask_layers(smoother, rows.kind()) for smoother in smoothers]
    changes = smoothed(rows, lefts, residuals, total, places, second)
    return [[ref[z] + DAMPING * part[z] for z in range(2)] for ref, part in zip(old, changes)]


def keep_ends(total, end_total_ref):
    for end in range(2):
        end_total_ref[end] = tip(total, end)[...]


def smooth_inside_kernel(
    one_ref, two_ref, ops_ref, smoother_ref, given_ref, rhs_ref, old_ref, end_total_ref, new_ref, round_ref, total, scratch
):
    size_x, size_y = total.shape[:2]
    rows = Fine(ops_ref, size_y)
    total[...] = given_ref[...]
    add_sides(one_ref, two_ref, rows, total)
    keep_ends(total, end_total_ref)

    def body(x):
        ys = range(size_y)
        values = smooth_columns(
            rows, total, [(x, y) for y in ys], [smoother_ref[x * size_y + y] for y in ys],
            [rhs_ref.at[x, y] for y in ys], [old_ref.at[x, y] for y in ys], scratch,
        )
        for y in ys:
            for z in range(2):
                new_ref[x, y, z] = values[y][z]
                round_ref[x, y, z] = values[y][z].astype(BF16)

    over_inside(size_x, body)


def smooth_ends_kernel(
    before_ref, after_ref, corner_before_ref, corner_after_ref, ops_ref, smoother_ref, given_ref, rhs_ref, old_ref, cells_ref,
    new_ref, round_ref, one_ref, two_ref, total, scratch,
):
    size_x, size_y = cells_ref.shape[:2]
    rows = Fine(ops_ref, size_y)
    total[...] = given_ref[...]
    add_ends([before_ref, after_ref, corner_before_ref, corner_after_ref], rows, total, size_x)

    places = [(end, y) for end in range(2) for y in range(size_y)]
    row = lambda end: end * (size_x - 1)
    values = smooth_columns(
        rows, total, places, [smoother_ref[row(end) * size_y + y] for end, y in places],
        [rhs_ref.at[row(end), y] for end, y in places], [tip(old_ref, end).at[y] for end, y in places], scratch,
    )
    for (end, y), value in zip(places, values):
        for z in range(2):
            new_ref[end, y, z] = value[z]
            round_ref[end, y, z] = value[z].astype(BF16)
    give_all_faces(cells_ref, round_ref, one_ref, two_ref)


def restrict_columns(rows, total, places, transfers, rhs, group_ref, xs, coarse_ref, scratch):
    size_x = coarse_ref.shape[0]
    first = [scratch.at[index, 0] for index in range(len(places))]
    applied = natural(rows, total, places, first)
    for index, place in enumerate(places):
        for z in range(2):
            scratch[index, 1, z] = rhs[index][z] - applied[index][z]
    for index, place in enumerate(places):
        for z in range(2):
            for parity in range(2):
                taken = scratch[index, 1, z, pl.ds(parity, HALF, stride=2), :]
                total[(*place, parity, pl.ds(z, HALF, stride=2), slice(None))] = taken
    given = []
    for place, transfer in zip(places, transfers):
        left = mask_layers(transfer, rows.kind())
        right = jnp.concatenate([total[(*place, 0)], total[(*place, 1)]], axis=1).astype(BF16)
        given.append(lax.dot_general(left, right, (((0,), (0,)), ((), ())), preferred_element_type=F32))
    for (_, y), x, both in zip(places, xs, given):
        for z in range(2):
            target = group_ref[y, z, x] - lax.axis_index("track") * size_x
            own = both[z * LANES : (z + 1) * LANES]
            coarse_ref[target, y // 2, z] += own[:64, :LANES] + own[64:, LANES:]


def restrict_inside_kernel(
    group_ref, one_ref, two_ref, ops_ref, transfer_ref, given_ref, rhs_ref, end_total_ref, coarse_ref, total, scratch
):
    size_x, size_y = total.shape[:2]
    rows = Fine(ops_ref, size_y)
    total[...] = given_ref[...]
    coarse_ref[...] = jnp.zeros_like(coarse_ref)
    add_sides(one_ref, two_ref, rows, total)
    keep_ends(total, end_total_ref)

    def body(x):
        ys = range(size_y)
        restrict_columns(
            rows, total, [(x, y) for y in ys], [transfer_ref[x * size_y + y] for y in ys],
            [rhs_ref.at[x, y] for y in ys], group_ref, [x] * size_y, coarse_ref, scratch,
        )

    over_inside(size_x, body)


def restrict_ends_kernel(
    group_ref, before_ref, after_ref, corner_before_ref, corner_after_ref, ops_ref, transfer_ref, given_ref, rhs_ref,
    part_ref, *refs
):
    pieces, (coarse_ref, total, scratch) = refs[:-3], refs[-3:]
    size_x, size_y = rhs_ref.shape[:2]
    rows = Fine(ops_ref, size_y)
    total[...] = given_ref[...]
    coarse_ref[...] = part_ref[...]
    add_ends([before_ref, after_ref, corner_before_ref, corner_after_ref], rows, total, size_x)

    places = [(end, y) for end in range(2) for y in range(size_y)]
    xs = [end * (size_x - 1) for end, _ in places]
    restrict_columns(
        rows, total, places, [transfer_ref[x * size_y + y] for x, (_, y) in zip(xs, places)],
        [rhs_ref.at[x, y] for x, (_, y) in zip(xs, places)], group_ref, xs, coarse_ref, scratch,
    )
    for step, piece in enumerate(pieces):
        first = lax.bitwise_xor(lax.axis_index("lateral"), step) * piece.shape[0]
        for x in range(piece.shape[0]):
            piece[x] = coarse_ref[first + x].astype(BF16)


def placed(pieces):
    found = []
    for step, piece in enumerate(pieces):
        first = lax.bitwise_xor(lax.axis_index("lateral"), step) * piece.shape[1]
        found += [(x, first + y, piece.at[x, y]) for x in range(piece.shape[0]) for y in range(piece.shape[1])]
    return found


def first_kernel(own_ref, other_ref, *refs):
    pieces, (coarse_ref, first_ref, round_ref, one_ref, two_ref, total, scratch) = refs[:-7], refs[-7:]
    rows = Coarse(own_ref, other_ref, coarse_ref.shape[1])
    columns = placed(pieces[::-1])
    cells = [[piece[z] for z in range(2)] for _, _, piece in columns]
    lefts = [mask_layers(rows.smoother(x, y), rows.kind()) for x, y, _ in columns]
    places = [(index,) for index in range(len(columns))]
    changes = smoothed(rows, lefts, cells, total, places, [scratch.at[index] for index in range(len(columns))])
    for (x, y, _), cell, change in zip(columns, cells, changes):
        for z in range(2):
            value = DAMPING * change[z]
            coarse_ref[x, y, z] = cell[z]
            first_ref[x, y, z] = value
            round_ref[x, y, z] = value.astype(BF16)
    for y in range(one_ref.shape[0]):
        give_faces(round_ref.at[0, y], round_ref.at[round_ref.shape[0] - 1, y], one_ref, two_ref, y)


def second_kernel(one_ref, two_ref, own_ref, other_ref, given_ref, coarse_ref, first_ref, *refs):
    pieces, (total, scratch) = refs[:-2], refs[-2:]
    rows = Coarse(own_ref, other_ref, total.shape[1])
    total[...] = given_ref[...]
    add_coarse_ends(one_ref, two_ref, rows, total)
    columns = placed(pieces)
    values = smooth_columns(
        rows, total, [(x, y) for x, y, _ in columns], [rows.smoother(x, y) for x, y, _ in columns],
        [[coarse_ref[x, y, z].astype(F32) for z in range(2)] for x, y, _ in columns],
        [first_ref.at[x, y] for x, y, _ in columns], scratch,
    )
    for (_, _, piece), value in zip(columns, values):
        for z in range(2):
            piece[z] = value[z].astype(BF16)


def prolong_kernel(group_ref, transfer_ref, iterate_ref, ends_ref, *refs):
    pieces, (out_ref, correction, total, scratch, made, sent) = refs[:-6], refs[-6:]
    size_x, size_y = out_ref.shape[:2]
    for step, piece in enumerate(pieces[::-1]):
        first = lax.bitwise_xor(lax.axis_index("lateral"), step) * piece.shape[0]
        for x in range(piece.shape[0]):
            correction[first + x] = piece[x]
    rows = Fine(None, size_y)

    def send(x):
        return pltpu.make_async_copy(made.at[x], out_ref.at[x], sent.at[x])

    def added(x, iterate):
        ys = range(size_y)
        source = lambda y, z: group_ref[y, z, x] - lax.axis_index("track") * size_x
        cells = [[correction[source(y, z), y // 2, z] for z in range(2)] for y in ys]
        lefts = [mask_layers(transfer_ref[x * size_y + y], rows.kind()) for y in ys]
        changes = smoothed(rows, lefts, cells, total, [(y,) for y in ys], [scratch.at[y, 0] for y in ys])
        for y in ys:
            for z in range(2):
                made[x, y, z] = iterate[y, z] + changes[y][z]
        send(x).start()

    for end in range(2):
        added(end * (size_x - 1), tip(ends_ref, end))
    over_inside(size_x, lambda x: added(x, iterate_ref.at[x]))
    for x in range(size_x):
        send(x).wait()


SMEM = pl.BlockSpec(memory_space=pltpu.SMEM)
VMEM = pl.BlockSpec(memory_space=pltpu.VMEM)


def call(kernel, name, scalars, operands, out_shape, scratch=(), out_space=pltpu.VMEM):
    return pl.pallas_call(
        kernel,
        in_specs=[SMEM] * len(scalars) + [VMEM] * len(operands),
        out_specs=jax.tree.map(lambda _: pl.BlockSpec(memory_space=out_space), out_shape),
        out_shape=out_shape,
        scratch_shapes=list(scratch),
        compiler_params=pltpu.CompilerParams(vmem_limit_bytes=LIMIT),
        name=name,
    )(*scalars, *operands)


def swap_round(one, two, axes):
    count, depth = lax.axis_size(axes), lax.axis_size("depth")
    ring = [i * depth for i in range(count)] + [i * depth + 1 for i in reversed(range(count))]
    onward = list(zip(ring, ring[1:] + ring[:1]))
    back = [(b, a) for a, b in onward]
    return lax.ppermute(one, (*axes, "depth"), onward), lax.ppermute(two, (*axes, "depth"), back)


def swap_sides(one, two):
    return swap_round(one, two, ("lateral",))


def swap_ends(last, first):
    count = lax.axis_size("track")
    before = lax.ppermute(last, "track", [(i, (i + 1) % count) for i in range(count)])
    after = lax.ppermute(first, "track", [((i + 1) % count, i) for i in range(count)])
    return before, after


def swap_corners(one, two):
    return swap_ends(jnp.concatenate([one[-1:], two[-1:]], axis=0), jnp.concatenate([one[:1], two[:1]], axis=0))


def swap_pieces(pieces):
    count = len(pieces)
    moved = [lax.ppermute(pieces[step], "lateral", [(i, i ^ step) for i in range(count)]) for step in range(1, count)]
    return moved[::-1] + [pieces[0]]


def per_device(
    rhs,
    start,
    fine_blocks,
    fine_cols,
    fine_mass,
    fine_smoother,
    transfer,
    aggregate,
    coarse_blocks,
    coarse_cols,
    coarse_mass,
    coarse_smoother,
):
    size_x, size_y, size_z, width, loads = rhs.shape
    count = lax.axis_size("lateral")
    groups = in_hbm(aggregate.transpose(1, 2, 0))
    part_x, all_y = coarse_blocks.shape[:2]
    coarse_y = size_y // 2

    paired = lambda a: a.reshape(size_x, size_y, size_z, HALF, LANES).transpose(0, 1, 3, 2, 4).reshape(-1, 2 * HALF, LANES)
    smoothers, transfers = paired(fine_smoother), paired(transfer)
    field = (size_x, size_y, size_z, width, loads)
    coarse_field = (size_x, coarse_y, size_z, width, loads)
    solve_field = (part_x, all_y, size_z, width, loads)
    sums = lambda shape: shape[:2] + (2, 2 * HALF, LANES)
    full = jax.ShapeDtypeStruct
    two_ends = lambda shape: (2,) + shape[1:]
    scratch = pltpu.VMEM((2 * size_y, 2, 2, width, loads), F32)
    whole, ends = pltpu.VMEM(sums(field), F32), pltpu.VMEM(two_ends(sums(field)), F32)
    face = full((size_x, size_z, width, loads), BF16)

    def inner_of(cells, tips, ops, grid):
        shape = full(sums(cells.shape), F32)
        return call(functools.partial(inner_kernel, grid=grid), "inner", [], [cells, tips, *ops], shape)

    rounded, one, two = round_start(start)
    tips, old, old_tips = rounded, start, start
    fine_cols, one, two = lax.optimization_barrier((fine_cols, one, two))
    one, two = swap_sides(one, two)
    fine_ops = sort_fine(fine_blocks, fine_cols, fine_mass)
    for sweep in range(SWEEPS + 1):
        inner = inner_of(rounded, tips, [fine_ops], Fine)
        inner, tips = lax.optimization_barrier((inner, tips))
        near = swap_ends(tips[-1], tips[0])
        if sweep == 1:
            coarse_cols, inner = lax.optimization_barrier((coarse_cols, inner))
            own_ops = sort_coarse(coarse_blocks, coarse_cols, coarse_mass, coarse_smoother)
            inner, one, two, own_ops = lax.optimization_barrier((inner, one, two, own_ops))
            other_ops = lax.ppermute(own_ops, "depth", [(0, 1), (1, 0)])
        else:
            inner, one, two = lax.optimization_barrier((inner, one, two))
        around = [*near, *swap_corners(one, two)]
        if sweep == SWEEPS:
            break
        end_total, new, rounded = call(
            smooth_inside_kernel, "smooth_inside", [], [one, two, fine_ops, smoothers, inner, rhs, old],
            [full(two_ends(sums(field)), F32), full(field, F32), full(field, BF16)], [whole, scratch],
        )
        new_tips, tips, one, two = call(
            smooth_ends_kernel, "smooth_ends", [], [*around, fine_ops, smoothers, end_total, rhs, old_tips, rounded],
            [full(two_ends(field), F32), full(two_ends(field), BF16), face, face], [ends, scratch],
        )
        old, old_tips = new, new_tips
        one, two = swap_sides(one, two)
    end_total, coarse_part = call(
        restrict_inside_kernel, "restrict_inside", [groups], [one, two, fine_ops, transfers, inner, rhs],
        [full(two_ends(sums(field)), F32), full(coarse_field, F32)], [whole, scratch],
    )
    piece = full((part_x,) + coarse_field[1:], BF16)
    pieces = call(
        restrict_ends_kernel, "restrict_ends", [groups],
        [*around, fine_ops, transfers, end_total, rhs, coarse_part], [piece] * count,
        [pltpu.VMEM(coarse_field, F32), ends, scratch],
    )
    line = pltpu.VMEM((part_x * all_y, 2, 2, width, loads), F32)
    coarse_ops = [own_ops, other_ops]
    row = full(solve_field[1:], BF16)
    coarse_res, first, rounded, one, two = call(
        first_kernel, "first", [], coarse_ops + swap_pieces(pieces),
        [full(solve_field, BF16), full(solve_field, F32), full(solve_field, BF16), row, row],
        [
            pltpu.VMEM((part_x * all_y, 2, 2 * HALF, LANES), F32),
            pltpu.VMEM((part_x * all_y, 2, width, loads), F32),
        ],
    )
    one, two = swap_round(one, two, ("track", "lateral"))
    inner = inner_of(rounded, rounded, coarse_ops, Coarse)
    pieces = call(
        second_kernel, "second", [], [one, two, *coarse_ops, inner, coarse_res, first], [piece] * count,
        [pltpu.VMEM(sums(solve_field), F32), line],
    )
    return call(
        prolong_kernel, "prolong", [groups], [transfers, old, old_tips] + swap_pieces(pieces), full(field, F32),
        [
            pltpu.VMEM(coarse_field, BF16), pltpu.VMEM((size_y, 2, 2 * HALF, LANES), F32), scratch,
            pltpu.VMEM(field, F32), pltpu.SemaphoreType.DMA((size_x,)),
        ],
        out_space=pltpu.HBM,
    )


def solution(mesh):
    in_specs = (
        P("track", "lateral", None, None, "depth"),
        P("track", "lateral", None, None, "depth"),
        P("track", "lateral", None, None, None),
        P("track", "lateral", None, None),
        P("track", "lateral", None, None),
        P("track", "lateral", None, None),
        P("track", "lateral", None, None),
        P("track", "lateral", None),
        P(("track", "lateral"), None, "depth", None, None),
        P(("track", "lateral"), None, "depth", None),
        P(("track", "lateral"), None, "depth", None),
        P(("track", "lateral"), None, "depth", None),
    )
    out_specs = P("track", "lateral", None, None, "depth")
    return jax.shard_map(
        per_device, mesh=mesh, in_specs=in_specs, out_specs=out_specs, check_vma=False
    )
```

```python
import functools

import jax
import jax.numpy as jnp
from jax import lax
from jax.experimental import pallas as pl
from jax.experimental.pallas import tpu as pltpu
from jax.sharding import PartitionSpec as P

SWEEPS = 2
DAMPING = 0.8
HALF = 32
LANES = 128
WIDE = 256
STEPS = 9
BF16 = jnp.bfloat16
F32 = jnp.float32
LIMIT = 8 * 1024 * 1024


def listed_at(cols_ref, slots, index, groups):
    for group in range(groups):
        codes = [cols_ref[index * groups + group, slot] for slot in range(27)]
        for slot, code in enumerate(codes):
            slots[group, code] = slot


def diagonal(mass, rows, groups):
    row = lax.broadcasted_iota(jnp.int32, (rows, LANES), 0)
    lane = lax.broadcasted_iota(jnp.int32, (rows, LANES), 1)
    spread = jnp.zeros((rows, LANES), F32)
    for group in range(groups):
        spread = jnp.where(row % groups == group, mass[group : group + 1], spread)
    return jnp.where(lane % 64 == 2 * (row // groups) + lane // 64, spread, 0.0)


def fine_sort_kernel(cols_ref, mass_ref, blocks_ref, out_ref, slots, held, arrived):
    second = lax.broadcasted_iota(jnp.int32, (2 * HALF, LANES), 0) % 2 == 1
    columns, parts = out_ref.shape[0], arrived.shape[0]
    each = columns // parts
    copies = [
        pltpu.make_async_copy(blocks_ref.at[pl.ds(part * each, each)], held.at[pl.ds(part * each, each)], arrived.at[part])
        for part in range(parts)
    ]
    for copy in copies:
        copy.start()
    for index in range(columns):
        listed_at(cols_ref, slots.at[index], index, 2)
    for index in range(columns):
        if index % each == 0:
            copies[index // each].wait()
        for step in range(STEPS):
            for side in range(2):
                upper = held[index, slots[index, 0, 3 * step + side + 1]]
                lower = held[index, slots[index, 1, 3 * step + side]]
                span = slice(side * LANES, (side + 1) * LANES)
                out_ref[index, step * 2 * HALF : (step + 1) * 2 * HALF, span] = jnp.where(second, lower, upper)
        mass = mass_ref[index].astype(F32)
        mass = diagonal(jnp.concatenate([mass, mass], axis=1), 2 * HALF, 2)
        for side in range(2):
            span = slice(side * LANES, (side + 1) * LANES)
            out_ref[index, STEPS * 2 * HALF :, span] = jnp.where(second == (side == 1), mass, 0.0).astype(BF16)


def coarse_sort_kernel(cols_ref, mass_ref, smoother_ref, blocks_ref, out_ref, slots, scratch):
    groups = blocks_ref.shape[2] // HALF
    rows = groups * HALF
    kind = lax.broadcasted_iota(jnp.int32, (rows, LANES), 0) % groups

    def hand_out(values, first, span):
        scratch[...] = values
        for y in range(groups):
            out_ref[y, first : first + HALF, span] = scratch[pl.ds(y, HALF, stride=groups), :].astype(BF16)

    listed_at(cols_ref, slots, pl.program_id(0), groups)
    for step in range(STEPS):
        for side in range(2):
            code = 3 * step + side + 1 - lax.axis_index("depth")
            values = blocks_ref[0, slots[0, code]]
            for group in range(1, groups):
                values = jnp.where(kind == group, blocks_ref[0, slots[group, code]], values)
            hand_out(values.astype(F32), step * HALF, slice(side * LANES, (side + 1) * LANES))
    hand_out(smoother_ref[0].astype(F32), STEPS * HALF, slice(0, LANES))
    mass = mass_ref[0].astype(F32)
    mass = diagonal(jnp.concatenate([mass, mass], axis=1), rows, groups)
    hand_out(mass, STEPS * HALF, slice(LANES, WIDE))


def in_hbm(array):
    return pltpu.with_memory_space_constraint(array, pltpu.HBM)


def sort_fine(blocks, cols, mass):
    size_x, size_y, layers = blocks.shape[:3]
    columns = size_x * size_y
    paired = blocks.reshape(size_x, size_y, layers, 27, HALF, LANES).transpose(0, 1, 3, 4, 2, 5)
    rows = (STEPS + 1) * 2 * HALF
    shape = (columns, 27, layers * HALF, LANES)
    return pl.pallas_call(
        fine_sort_kernel,
        in_specs=[SMEM, VMEM, pl.BlockSpec(memory_space=pltpu.HBM)],
        out_specs=VMEM,
        out_shape=jax.ShapeDtypeStruct((columns, rows, WIDE), BF16),
        scratch_shapes=[
            pltpu.SMEM((columns, 2, 27), jnp.int32), pltpu.VMEM(shape, BF16), pltpu.SemaphoreType.DMA((columns // 2,)),
        ],
        compiler_params=pltpu.CompilerParams(vmem_limit_bytes=2 * LIMIT),
        name="sort_fine",
    )(in_hbm(cols.reshape(columns * layers, 27)), in_hbm(mass.reshape(columns, layers, 64)), in_hbm(paired.reshape(shape)))


def sort_coarse(blocks, cols, mass, smoother):
    size_x, size_y = blocks.shape[:2]
    paired = blocks.reshape(size_x, size_y, 27, HALF, LANES).transpose(0, 2, 3, 1, 4)
    smoothers = smoother.reshape(size_x, size_y, HALF, LANES).transpose(0, 2, 1, 3)
    rows = (STEPS + 1) * HALF
    return pl.pallas_call(
        coarse_sort_kernel,
        grid=(size_x,),
        in_specs=[
            SMEM,
            pl.BlockSpec((1, size_y, 64), lambda i: (i, 0, 0)),
            pl.BlockSpec((1, size_y * HALF, LANES), lambda i: (i, 0, 0)),
            pl.BlockSpec((1, 27, size_y * HALF, LANES), lambda i: (i, 0, 0, 0)),
        ],
        out_specs=pl.BlockSpec((size_y, rows, WIDE), lambda i: (i, 0, 0)),
        out_shape=jax.ShapeDtypeStruct((size_x * size_y, rows, WIDE), BF16),
        scratch_shapes=[pltpu.SMEM((size_y, 27), jnp.int32), pltpu.VMEM((size_y * HALF, LANES), F32)],
        compiler_params=pltpu.CompilerParams(vmem_limit_bytes=LIMIT),
        name="sort_coarse",
    )(
        in_hbm(cols.reshape(size_x * size_y, 27)),
        in_hbm(mass.reshape(size_x, size_y, 64)),
        in_hbm(smoothers.reshape(size_x, size_y * HALF, LANES)),
        in_hbm(paired.reshape(size_x, 27, size_y * HALF, LANES)),
    )


def two_sided(block):
    none = jnp.zeros_like(block)
    return jnp.concatenate(
        [jnp.concatenate([block, none], axis=1), jnp.concatenate([none, block], axis=1)], axis=0
    )


def mask_layers(block, kind):
    none = jnp.zeros_like(block)
    return jnp.concatenate([jnp.where(kind == 0, block, none), jnp.where(kind == 1, block, none)], axis=1)


class Fine:
    def __init__(self, ops_ref, size_y):
        self.ops_ref, self.size_y = ops_ref, size_y

    def kind(self):
        return lax.broadcasted_iota(jnp.int32, (2 * HALF, LANES), 0) % 2

    def step(self, x, y, step):
        return self.ops_ref[x * self.size_y + y, step * 2 * HALF : (step + 1) * 2 * HALF, :]

    def mass(self, x, y):
        return self.step(x, y, STEPS)

    def half(self, total, place, z, parity):
        return total[(*place, parity, pl.ds(z, HALF, stride=2), slice(None))]


class Coarse:
    def __init__(self, own_ref, other_ref, size_y):
        self.own_ref, self.other_ref, self.size_y = own_ref, other_ref, size_y

    def kind(self):
        row = lax.broadcasted_iota(jnp.int32, (2 * HALF, LANES), 0)
        return lax.bitwise_xor(row // HALF, lax.axis_index("depth"))

    def step(self, x, y, step):
        place, span = x * self.size_y + y, slice(step * HALF, (step + 1) * HALF)
        return jnp.concatenate([self.own_ref[place, span, :], self.other_ref[place, span, :]], axis=0)

    def smoother(self, x, y):
        return self.step(x, y, STEPS)[:, :LANES]

    def mass(self, x, y):
        return mask_layers(self.step(x, y, STEPS)[:, LANES:], self.kind())

    def half(self, total, place, z, parity):
        first = pl.multiple_of(lax.bitwise_xor(jnp.int32(z), lax.axis_index("depth")) * HALF, HALF)
        return total[(*place, parity, pl.ds(first, HALF), slice(None))]


def both_layers(cells):
    return jnp.concatenate([two_sided(cells[0]), two_sided(cells[1])], axis=0)


def tip(ref, end):
    return ref.at[end * (ref.shape[0] - 1)]


def add_from(total_ref, rows, cells, targets, slot=lambda x: x):
    left = [rows.step(*target) for target in targets]
    given = jnp.dot(jnp.concatenate(left, axis=0), both_layers(cells), preferred_element_type=F32)
    parts = [given[index * 2 * HALF : (index + 1) * 2 * HALF] for index in range(len(left))]
    for (x, y, _), part in zip(targets, parts):
        for parity in range(2):
            total_ref[slot(x), y, parity] += part[:, parity * LANES : (parity + 1) * LANES]


def natural(rows, total, places, scratches):
    for place, scratch in zip(places, scratches):
        for z in range(2):
            for parity in range(2):
                scratch[z, pl.ds(parity, HALF, stride=2), :] = rows.half(total, place, z, parity)
    return [[scratch[z] for z in range(2)] for scratch in scratches]


def smoothed(rows, lefts, columns, total, places, scratches):
    given = [
        jnp.dot(left, both_layers([cell.astype(BF16) for cell in cells]), preferred_element_type=F32)
        for left, cells in zip(lefts, columns)
    ]
    for part, place in zip(given, places):
        for parity in range(2):
            total[(*place, parity)] = part[:, parity * LANES : (parity + 1) * LANES]
    return natural(rows, total, places, scratches)


def over_columns(size_x, column):
    if size_x == 1:
        column(0, (0,))
        return
    column(0, (-1, 0))
    for x in range(1, size_x - 1):
        column(x, (-1, 0, 1))
    column(size_x - 1, (0, 1))


def inner_kernel(cells_ref, ends_ref, *refs, grid):
    *ops, total_ref = refs
    size_x, size_y = cells_ref.shape[:2]
    rows = grid(*ops, size_y)
    total_ref[...] = jnp.zeros_like(total_ref)

    def column(x, shifts):
        row = tip(ends_ref, min(x, 1)) if x in (0, size_x - 1) else cells_ref.at[x]
        sums = {}
        for near in range(size_y):
            targets = [(shift, y) for shift in shifts for y in range(size_y) if abs(near - y) <= 1]
            left = [rows.step(x - shift, y, (shift + 1) * 3 + near - y + 1) for shift, y in targets]
            left.append(rows.mass(x, near))
            given = jnp.dot(jnp.concatenate(left, axis=0), both_layers(row[near]), preferred_element_type=F32)
            for index, target in enumerate(targets + [(0, near)]):
                part = given[index * 2 * HALF : (index + 1) * 2 * HALF]
                sums[target] = sums[target] + part if target in sums else part
        for (shift, y), part in sums.items():
            for parity in range(2):
                total_ref[x - shift, y, parity] += part[:, parity * LANES : (parity + 1) * LANES]

    over_columns(size_x, column)


def inside_track(cells, low):
    at = lax.axis_index("lateral")
    inside = at > 0 if low else at < lax.axis_size("lateral") - 1
    return jnp.where(inside, cells, jnp.zeros_like(cells))


def add_sides(one_ref, two_ref, rows, total):
    size_x, size_y = total.shape[:2]

    def both(low_ref, high_ref):
        def column(x, shifts):
            for cells, y, step in (
                (inside_track(low_ref[x], True), 0, 0),
                (inside_track(high_ref[x], False), size_y - 1, 2),
            ):
                add_from(total, rows, cells, [(x - shift, y, (shift + 1) * 3 + step) for shift in shifts])

        over_columns(size_x, column)

    odd = lax.axis_index("depth") % 2
    pl.when(odd == 0)(lambda: both(one_ref, two_ref))
    pl.when(odd == 1)(lambda: both(two_ref, one_ref))


def give_faces(low, high, one_ref, two_ref, x):
    even = lax.axis_index("depth") % 2 == 0
    for z in range(2):
        one_ref[x, z] = jnp.where(even, high[z], low[z])
        two_ref[x, z] = jnp.where(even, low[z], high[z])


def give_all_faces(cells_ref, ends_ref, one_ref, two_ref):
    size_x, size_y = cells_ref.shape[:2]

    for x in range(1, size_x - 1):
        give_faces(cells_ref.at[x, 0], cells_ref.at[x, size_y - 1], one_ref, two_ref, x)
    for end in range(2):
        ends = tip(ends_ref, end)
        give_faces(ends.at[0], ends.at[size_y - 1], one_ref, two_ref, end * (size_x - 1))


def round_kernel(start_ref, round_ref, one_ref, two_ref, held, arrived):
    size_x, size_y = start_ref.shape[:2]
    copies = [pltpu.make_async_copy(start_ref.at[x], held.at[x], arrived.at[x]) for x in range(size_x)]
    for copy in copies:
        copy.start()
    for x, copy in enumerate(copies):
        copy.wait()
        cells = [[held[x, y, z].astype(BF16) for z in range(2)] for y in range(size_y)]
        for y, column in enumerate(cells):
            for z in range(2):
                round_ref[x, y, z] = column[z]
        give_faces(cells[0], cells[-1], one_ref, two_ref, x)


def round_start(start):
    size_x, _, layers, width, loads = start.shape
    face = jax.ShapeDtypeStruct((size_x, layers, width, loads), BF16)
    return pl.pallas_call(
        round_kernel,
        in_specs=[pl.BlockSpec(memory_space=pltpu.HBM)],
        out_specs=[VMEM] * 3,
        out_shape=[jax.ShapeDtypeStruct(start.shape, BF16), face, face],
        scratch_shapes=[pltpu.VMEM(start.shape, F32), pltpu.SemaphoreType.DMA((size_x,))],
        compiler_params=pltpu.CompilerParams(vmem_limit_bytes=LIMIT),
        name="round_start",
    )(in_hbm(start))


def add_ends(given_refs, rows, total, size_x):
    size_y = total.shape[1]
    odd = lax.axis_index("depth") % 2
    at, count = lax.axis_index("track"), lax.axis_size("track")
    for near in range(-1, size_y + 1):
        ys = [y for y in range(size_y) if abs(near - y) <= 1]
        corner = near in (-1, size_y)
        place = (odd if near < 0 else 1 - odd) if corner else near
        for end, inside in ((0, at > 0), (1, at < count - 1)):
            cells = given_refs[2 * corner + end][place]
            if not corner:
                cells = jnp.where(odd == end, given_refs[0][place], given_refs[1][place])
            cells = jnp.where(inside, cells, jnp.zeros_like(cells))
            if corner:
                cells = inside_track(cells, near < 0)
            targets = [(end * (size_x - 1), y, 6 * end + near - y + 1) for y in ys]
            add_from(total, rows, cells, targets, slot=lambda x, end=end: end)


def add_coarse_ends(one_ref, two_ref, rows, total):
    size_x, size_y = total.shape[:2]
    even = lax.axis_index("depth") % 2 == 0
    at = lax.axis_index(("track", "lateral"))
    count = lax.axis_size(("track", "lateral"))
    for near in range(size_y):
        ys = [y for y in range(size_y) if abs(near - y) <= 1]
        one, two = one_ref[near], two_ref[near]
        for end, cells, inside in ((0, jnp.where(even, one, two), at > 0), (1, jnp.where(even, two, one), at < count - 1)):
            cells = jnp.where(inside, cells, jnp.zeros_like(cells))
            add_from(total, rows, cells, [(end * (size_x - 1), y, 6 * end + near - y + 1) for y in ys])


def over_inside(size_x, body):
    for x in range(1, size_x - 1):
        body(x)


def smooth_columns(rows, total, places, smoothers, rhs, old, scratch):
    first = [scratch.at[index, 0] for index in range(len(places))]
    second = [scratch.at[index, 1] for index in range(len(places))]
    applied = natural(rows, total, places, first)
    residuals = [[ref[z] - part[z] for z in range(2)] for ref, part in zip(rhs, applied)]
    lefts = [mask_layers(smoother, rows.kind()) for smoother in smoothers]
    changes = smoothed(rows, lefts, residuals, total, places, second)
    return [[ref[z] + DAMPING * part[z] for z in range(2)] for ref, part in zip(old, changes)]


def keep_ends(total, end_total_ref):
    for end in range(2):
        end_total_ref[end] = tip(total, end)[...]


def smooth_inside_kernel(
    one_ref, two_ref, ops_ref, smoother_ref, given_ref, rhs_ref, old_ref, end_total_ref, new_ref, round_ref, total, scratch
):
    size_x, size_y = total.shape[:2]
    rows = Fine(ops_ref, size_y)
    total[...] = given_ref[...]
    add_sides(one_ref, two_ref, rows, total)
    keep_ends(total, end_total_ref)

    def body(x):
        ys = range(size_y)
        values = smooth_columns(
            rows, total, [(x, y) for y in ys], [smoother_ref[x * size_y + y] for y in ys],
            [rhs_ref.at[x, y] for y in ys], [old_ref.at[x, y] for y in ys], scratch,
        )
        for y in ys:
            for z in range(2):
                new_ref[x, y, z] = values[y][z]
                round_ref[x, y, z] = values[y][z].astype(BF16)

    over_inside(size_x, body)


def smooth_ends_kernel(
    before_ref, after_ref, corner_before_ref, corner_after_ref, ops_ref, smoother_ref, given_ref, rhs_ref, old_ref, cells_ref,
    new_ref, round_ref, one_ref, two_ref, total, scratch,
):
    size_x, size_y = cells_ref.shape[:2]
    rows = Fine(ops_ref, size_y)
    total[...] = given_ref[...]
    add_ends([before_ref, after_ref, corner_before_ref, corner_after_ref], rows, total, size_x)

    places = [(end, y) for end in range(2) for y in range(size_y)]
    row = lambda end: end * (size_x - 1)
    values = smooth_columns(
        rows, total, places, [smoother_ref[row(end) * size_y + y] for end, y in places],
        [rhs_ref.at[row(end), y] for end, y in places], [tip(old_ref, end).at[y] for end, y in places], scratch,
    )
    for (end, y), value in zip(places, values):
        for z in range(2):
            new_ref[end, y, z] = value[z]
            round_ref[end, y, z] = value[z].astype(BF16)
    give_all_faces(cells_ref, round_ref, one_ref, two_ref)


def restrict_columns(rows, total, places, transfers, rhs, group_ref, xs, coarse_ref, scratch):
    size_x = coarse_ref.shape[0]
    first = [scratch.at[index, 0] for index in range(len(places))]
    applied = natural(rows, total, places, first)
    for index, place in enumerate(places):
        for z in range(2):
            scratch[index, 1, z] = rhs[index][z] - applied[index][z]
    for index, place in enumerate(places):
        for z in range(2):
            for parity in range(2):
                taken = scratch[index, 1, z, pl.ds(parity, HALF, stride=2), :]
                total[(*place, parity, pl.ds(z, HALF, stride=2), slice(None))] = taken
    given = []
    for place, transfer in zip(places, transfers):
        left = mask_layers(transfer, rows.kind())
        right = jnp.concatenate([total[(*place, 0)], total[(*place, 1)]], axis=1).astype(BF16)
        given.append(lax.dot_general(left, right, (((0,), (0,)), ((), ())), preferred_element_type=F32))
    for (_, y), x, both in zip(places, xs, given):
        for z in range(2):
            target = group_ref[y, z, x] - lax.axis_index("track") * size_x
            own = both[z * LANES : (z + 1) * LANES]
            coarse_ref[target, y // 2, z] += own[:64, :LANES] + own[64:, LANES:]


def restrict_inside_kernel(
    group_ref, one_ref, two_ref, ops_ref, transfer_ref, given_ref, rhs_ref, end_total_ref, coarse_ref, total, scratch
):
    size_x, size_y = total.shape[:2]
    rows = Fine(ops_ref, size_y)
    total[...] = given_ref[...]
    coarse_ref[...] = jnp.zeros_like(coarse_ref)
    add_sides(one_ref, two_ref, rows, total)
    keep_ends(total, end_total_ref)

    def body(x):
        ys = range(size_y)
        restrict_columns(
            rows, total, [(x, y) for y in ys], [transfer_ref[x * size_y + y] for y in ys],
            [rhs_ref.at[x, y] for y in ys], group_ref, [x] * size_y, coarse_ref, scratch,
        )

    over_inside(size_x, body)


def restrict_ends_kernel(
    group_ref, before_ref, after_ref, corner_before_ref, corner_after_ref, ops_ref, transfer_ref, given_ref, rhs_ref,
    part_ref, *refs
):
    pieces, (coarse_ref, total, scratch) = refs[:-3], refs[-3:]
    size_x, size_y = rhs_ref.shape[:2]
    rows = Fine(ops_ref, size_y)
    total[...] = given_ref[...]
    coarse_ref[...] = part_ref[...]
    add_ends([before_ref, after_ref, corner_before_ref, corner_after_ref], rows, total, size_x)

    places = [(end, y) for end in range(2) for y in range(size_y)]
    xs = [end * (size_x - 1) for end, _ in places]
    restrict_columns(
        rows, total, places, [transfer_ref[x * size_y + y] for x, (_, y) in zip(xs, places)],
        [rhs_ref.at[x, y] for x, (_, y) in zip(xs, places)], group_ref, xs, coarse_ref, scratch,
    )
    for step, piece in enumerate(pieces):
        first = lax.bitwise_xor(lax.axis_index("lateral"), step) * piece.shape[0]
        for x in range(piece.shape[0]):
            piece[x] = coarse_ref[first + x].astype(BF16)


def placed(pieces):
    found = []
    for step, piece in enumerate(pieces):
        first = lax.bitwise_xor(lax.axis_index("lateral"), step) * piece.shape[1]
        found += [(x, first + y, piece.at[x, y]) for x in range(piece.shape[0]) for y in range(piece.shape[1])]
    return found


def first_kernel(own_ref, other_ref, *refs):
    pieces, (coarse_ref, first_ref, round_ref, one_ref, two_ref, total, scratch) = refs[:-7], refs[-7:]
    rows = Coarse(own_ref, other_ref, coarse_ref.shape[1])
    columns = placed(pieces[::-1])
    cells = [[piece[z] for z in range(2)] for _, _, piece in columns]
    lefts = [mask_layers(rows.smoother(x, y), rows.kind()) for x, y, _ in columns]
    places = [(index,) for index in range(len(columns))]
    changes = smoothed(rows, lefts, cells, total, places, [scratch.at[index] for index in range(len(columns))])
    for (x, y, _), cell, change in zip(columns, cells, changes):
        for z in range(2):
            value = DAMPING * change[z]
            coarse_ref[x, y, z] = cell[z]
            first_ref[x, y, z] = value
            round_ref[x, y, z] = value.astype(BF16)
    for y in range(one_ref.shape[0]):
        give_faces(round_ref.at[0, y], round_ref.at[round_ref.shape[0] - 1, y], one_ref, two_ref, y)


def second_kernel(one_ref, two_ref, own_ref, other_ref, given_ref, coarse_ref, first_ref, *refs):
    pieces, (total, scratch) = refs[:-2], refs[-2:]
    rows = Coarse(own_ref, other_ref, total.shape[1])
    total[...] = given_ref[...]
    add_coarse_ends(one_ref, two_ref, rows, total)
    columns = placed(pieces)
    values = smooth_columns(
        rows, total, [(x, y) for x, y, _ in columns], [rows.smoother(x, y) for x, y, _ in columns],
        [[coarse_ref[x, y, z].astype(F32) for z in range(2)] for x, y, _ in columns],
        [first_ref.at[x, y] for x, y, _ in columns], scratch,
    )
    for (_, _, piece), value in zip(columns, values):
        for z in range(2):
            piece[z] = value[z].astype(BF16)


def prolong_kernel(group_ref, transfer_ref, iterate_ref, ends_ref, *refs):
    pieces, (out_ref, correction, total, scratch, made, sent) = refs[:-6], refs[-6:]
    size_x, size_y = out_ref.shape[:2]
    for step, piece in enumerate(pieces[::-1]):
        first = lax.bitwise_xor(lax.axis_index("lateral"), step) * piece.shape[0]
        for x in range(piece.shape[0]):
            correction[first + x] = piece[x]
    rows = Fine(None, size_y)

    def send(x):
        return pltpu.make_async_copy(made.at[x], out_ref.at[x], sent.at[x])

    def added(x, iterate):
        ys = range(size_y)
        source = lambda y, z: group_ref[y, z, x] - lax.axis_index("track") * size_x
        cells = [[correction[source(y, z), y // 2, z] for z in range(2)] for y in ys]
        lefts = [mask_layers(transfer_ref[x * size_y + y], rows.kind()) for y in ys]
        changes = smoothed(rows, lefts, cells, total, [(y,) for y in ys], [scratch.at[y, 0] for y in ys])
        for y in ys:
            for z in range(2):
                made[x, y, z] = iterate[y, z] + changes[y][z]
        send(x).start()

    for end in range(2):
        added(end * (size_x - 1), tip(ends_ref, end))
    over_inside(size_x, lambda x: added(x, iterate_ref.at[x]))
    for x in range(size_x):
        send(x).wait()


SMEM = pl.BlockSpec(memory_space=pltpu.SMEM)
VMEM = pl.BlockSpec(memory_space=pltpu.VMEM)


def call(kernel, name, scalars, operands, out_shape, scratch=(), out_space=pltpu.VMEM):
    return pl.pallas_call(
        kernel,
        in_specs=[SMEM] * len(scalars) + [VMEM] * len(operands),
        out_specs=jax.tree.map(lambda _: pl.BlockSpec(memory_space=out_space), out_shape),
        out_shape=out_shape,
        scratch_shapes=list(scratch),
        compiler_params=pltpu.CompilerParams(vmem_limit_bytes=LIMIT),
        name=name,
    )(*scalars, *operands)


def swap_round(one, two, axes):
    count, depth = lax.axis_size(axes), lax.axis_size("depth")
    ring = [i * depth for i in range(count)] + [i * depth + 1 for i in reversed(range(count))]
    onward = list(zip(ring, ring[1:] + ring[:1]))
    back = [(b, a) for a, b in onward]
    return lax.ppermute(one, (*axes, "depth"), onward), lax.ppermute(two, (*axes, "depth"), back)


def swap_sides(one, two):
    return swap_round(one, two, ("lateral",))


def swap_ends(last, first):
    count = lax.axis_size("track")
    before = lax.ppermute(last, "track", [(i, (i + 1) % count) for i in range(count)])
    after = lax.ppermute(first, "track", [((i + 1) % count, i) for i in range(count)])
    return before, after


def swap_tips(last, first):
    even = lax.axis_index("depth") % 2 == 0
    return swap_round(jnp.where(even, last, first), jnp.where(even, first, last), ("track",))


def swap_corners(one, two):
    return swap_ends(jnp.concatenate([one[-1:], two[-1:]], axis=0), jnp.concatenate([one[:1], two[:1]], axis=0))


def swap_pieces(pieces):
    count = len(pieces)
    moved = [lax.ppermute(pieces[step], "lateral", [(i, i ^ step) for i in range(count)]) for step in range(1, count)]
    return moved[::-1] + [pieces[0]]


def per_device(
    rhs,
    start,
    fine_blocks,
    fine_cols,
    fine_mass,
    fine_smoother,
    transfer,
    aggregate,
    coarse_blocks,
    coarse_cols,
    coarse_mass,
    coarse_smoother,
):
    size_x, size_y, size_z, width, loads = rhs.shape
    count = lax.axis_size("lateral")
    groups = in_hbm(aggregate.transpose(1, 2, 0))
    part_x, all_y = coarse_blocks.shape[:2]
    coarse_y = size_y // 2

    paired = lambda a: a.reshape(size_x, size_y, size_z, HALF, LANES).transpose(0, 1, 3, 2, 4).reshape(-1, 2 * HALF, LANES)
    smoothers, transfers = paired(fine_smoother), paired(transfer)
    field = (size_x, size_y, size_z, width, loads)
    coarse_field = (size_x, coarse_y, size_z, width, loads)
    solve_field = (part_x, all_y, size_z, width, loads)
    sums = lambda shape: shape[:2] + (2, 2 * HALF, LANES)
    full = jax.ShapeDtypeStruct
    two_ends = lambda shape: (2,) + shape[1:]
    scratch = pltpu.VMEM((2 * size_y, 2, 2, width, loads), F32)
    whole, ends = pltpu.VMEM(sums(field), F32), pltpu.VMEM(two_ends(sums(field)), F32)
    face = full((size_x, size_z, width, loads), BF16)

    def inner_of(cells, tips, ops, grid):
        shape = full(sums(cells.shape), F32)
        return call(functools.partial(inner_kernel, grid=grid), "inner", [], [cells, tips, *ops], shape)

    rounded, one, two = round_start(start)
    tips, old, old_tips = rounded, start, start
    fine_cols, one, two = lax.optimization_barrier((fine_cols, one, two))
    one, two = swap_sides(one, two)
    fine_ops = sort_fine(fine_blocks, fine_cols, fine_mass)
    for sweep in range(SWEEPS + 1):
        inner = inner_of(rounded, tips, [fine_ops], Fine)
        inner, tips = lax.optimization_barrier((inner, tips))
        near = swap_tips(tips[-1], tips[0])
        if sweep == 1:
            coarse_cols, inner = lax.optimization_barrier((coarse_cols, inner))
            own_ops = sort_coarse(coarse_blocks, coarse_cols, coarse_mass, coarse_smoother)
            inner, one, two, own_ops = lax.optimization_barrier((inner, one, two, own_ops))
            other_ops = lax.ppermute(own_ops, "depth", [(0, 1), (1, 0)])
        else:
            inner, one, two = lax.optimization_barrier((inner, one, two))
        around = [*near, *swap_corners(one, two)]
        if sweep == SWEEPS:
            break
        end_total, new, rounded = call(
            smooth_inside_kernel, "smooth_inside", [], [one, two, fine_ops, smoothers, inner, rhs, old],
            [full(two_ends(sums(field)), F32), full(field, F32), full(field, BF16)], [whole, scratch],
        )
        new_tips, tips, one, two = call(
            smooth_ends_kernel, "smooth_ends", [], [*around, fine_ops, smoothers, end_total, rhs, old_tips, rounded],
            [full(two_ends(field), F32), full(two_ends(field), BF16), face, face], [ends, scratch],
        )
        old, old_tips = new, new_tips
        one, two = swap_sides(one, two)
    end_total, coarse_part = call(
        restrict_inside_kernel, "restrict_inside", [groups], [one, two, fine_ops, transfers, inner, rhs],
        [full(two_ends(sums(field)), F32), full(coarse_field, F32)], [whole, scratch],
    )
    piece = full((part_x,) + coarse_field[1:], BF16)
    pieces = call(
        restrict_ends_kernel, "restrict_ends", [groups],
        [*around, fine_ops, transfers, end_total, rhs, coarse_part], [piece] * count,
        [pltpu.VMEM(coarse_field, F32), ends, scratch],
    )
    line = pltpu.VMEM((part_x * all_y, 2, 2, width, loads), F32)
    coarse_ops = [own_ops, other_ops]
    row = full(solve_field[1:], BF16)
    coarse_res, first, rounded, one, two = call(
        first_kernel, "first", [], coarse_ops + swap_pieces(pieces),
        [full(solve_field, BF16), full(solve_field, F32), full(solve_field, BF16), row, row],
        [
            pltpu.VMEM((part_x * all_y, 2, 2 * HALF, LANES), F32),
            pltpu.VMEM((part_x * all_y, 2, width, loads), F32),
        ],
    )
    one, two = swap_round(one, two, ("track", "lateral"))
    inner = inner_of(rounded, rounded, coarse_ops, Coarse)
    pieces = call(
        second_kernel, "second", [], [one, two, *coarse_ops, inner, coarse_res, first], [piece] * count,
        [pltpu.VMEM(sums(solve_field), F32), line],
    )
    return call(
        prolong_kernel, "prolong", [groups], [transfers, old, old_tips] + swap_pieces(pieces), full(field, F32),
        [
            pltpu.VMEM(coarse_field, BF16), pltpu.VMEM((size_y, 2, 2 * HALF, LANES), F32), scratch,
            pltpu.VMEM(field, F32), pltpu.SemaphoreType.DMA((size_x,)),
        ],
        out_space=pltpu.HBM,
    )


def solution(mesh):
    in_specs = (
        P("track", "lateral", None, None, "depth"),
        P("track", "lateral", None, None, "depth"),
        P("track", "lateral", None, None, None),
        P("track", "lateral", None, None),
        P("track", "lateral", None, None),
        P("track", "lateral", None, None),
        P("track", "lateral", None, None),
        P("track", "lateral", None),
        P(("track", "lateral"), None, "depth", None, None),
        P(("track", "lateral"), None, "depth", None),
        P(("track", "lateral"), None, "depth", None),
        P(("track", "lateral"), None, "depth", None),
    )
    out_specs = P("track", "lateral", None, None, "depth")
    return jax.shard_map(
        per_device, mesh=mesh, in_specs=in_specs, out_specs=out_specs, check_vma=False
    )
```
